32 devices in a mesh: sub: 8 (over z, x), grp: 4 (over y, core).
Axes of the slice: x: 2, y: 2, z: 4, core: 2. Of those that a mesh axis runs over, the one named last changes fastest.
Arguments:
- rhs: float32 [4, 32, 256, 256], P('grp', 'sub')
- counts: int32 [4, 32], P('grp', 'sub'), may hold values from 64 to 256, as said below
- solve_panel: bfloat16 [4, 32, 512, 512], P('grp', 'sub'), as said below
- dirichlet_panel: bfloat16 [4, 32, 512, 512], P('grp', 'sub'), as said below
- coupling: float32 [4, 32, 32, 512], P('grp', 'sub'), may hold values from -0.25 to 0.25
- corner_map: int32 [4, 32, 32], P('grp', 'sub'), may hold values from 0 to 1023
- coarse_inverse: float32 [8, 1024, 1024], P('sub', 'grp'), as said below
Outputs:
- multipliers: float32 [4, 32, 256, 256], P('grp', 'sub')
- residual: float32 [4, 32, 256, 256], P('grp', 'sub')
The draws below stay inside these ranges and needn't reach their ends.
Inputs may be any that keep to these rules, and one draw needn't show every extreme that they name: `counts`: some pair has all 256 unknowns constrained. `solve_panel`: each panel is symmetric positive definite. `dirichlet_panel`: each panel is symmetric positive definite. `coarse_inverse`: each slab's matrix is symmetric positive definite.
All inputs are finite; a program needn't handle non-finite values.
Results may differ from the reference program's by a relative error of at most 0.0003.
Values sent between devices are 32-bit elements; how exact they have to be, the bound alone decides.
No kernel may reach another device: no remote copies, remote signals or barrier semaphores. Data moves between devices by JAX's collectives and lax.ppermute only.
A program may use at most 128 MiB of HBM per device.

```python
import math
import jax
import jax.numpy as jnp
from jax import lax

P_SIZE = 512
H = 256
NC = 32
R = 256
ITERS = 3
CHAIN = 32
SECTORS = 4
SLABS = 8
NCO = 1024


def gram_block(key, order):
    key_mix, key_scale = jax.random.split(key)
    mixing = jax.random.randint(key_mix, (order, order), -3, 4).astype(jnp.float32)
    gram = jnp.dot(mixing, mixing.T, precision=lax.Precision.HIGHEST) * (0.25 / order)
    scales = jnp.exp(jax.random.uniform(key_scale, (order,), jnp.float32, 0.0, math.log(1.7)))
    outer = scales[:, None] * scales[None, :]
    eye = jnp.eye(order, dtype=jnp.float32)
    return (gram + 0.5 * eye) * outer


def panel_stack(key):

    def one_sector(index):
        keys = jax.random.split(jax.random.fold_in(key, index), CHAIN)
        blocks = jax.vmap(lambda single: gram_block(single, P_SIZE))(keys)
        return blocks.astype(jnp.bfloat16)
    return lax.map(one_sector, jnp.arange(SECTORS))


def draw_solve_panel(key, part):
    return panel_stack(jax.random.fold_in(key, 11))


def draw_dirichlet_panel(key, part):
    return panel_stack(jax.random.fold_in(key, 23))


def draw_coarse_inverse(key, part):
    base = jax.random.fold_in(key, 37)
    return lax.map(lambda index: gram_block(jax.random.fold_in(base, index), NCO), jnp.arange(SLABS))


def draw_counts(key, part):
    values = jax.random.randint(jax.random.fold_in(key, 41), (SECTORS, CHAIN), H // 4, H + 1)
    return values.at[0, 0].set(H).astype(jnp.int32)


def draw_rhs(key, part):
    key_main = jax.random.fold_in(jax.random.fold_in(key, 53), 0)
    rising = 3.0 ** (jnp.arange(CHAIN, dtype=jnp.float32) / max(CHAIN - 1, 1))
    rising = rising[None, :, None, None]
    base = jax.random.normal(key_main, (SECTORS, CHAIN, R, H), jnp.float32)
    return jnp.clip(base, -6.0, 6.0) * rising


def plant(values, stream_key, smallest, largest):
    longest = values.shape.index(max(values.shape))
    spots = []
    for shift in (0, 1):
        where = [jax.random.randint(jax.random.fold_in(stream_key, axis), (), 0, length) for axis, length in enumerate(values.shape)]
        where[longest] = (where[longest] + shift) % values.shape[longest]
        spots.append(tuple(where))
    return values.at[spots[0]].set(smallest).at[spots[1]].set(largest)


def steps_of(own_key, dims, shards, smallest, top_value):
    gain, own = 1.0, jax.random.fold_in(own_key, 6)
    for axis_at, shards_of in shards:
        draws = jnp.exp(jax.random.uniform(jax.random.fold_in(own, axis_at), (shards_of,), jnp.float32, smallest / len(shards), top_value / len(shards)))
        gain = gain * jnp.repeat(draws, dims[axis_at] // shards_of).reshape([-1 if axis == axis_at else 1 for axis in range(len(dims))])
    return gain


def normal_values(rng, extent, deviation, most, shards=(), kind=jnp.bfloat16):
    values = deviation * jax.random.normal(rng, extent, jnp.float32)
    if shards:
        values = values * steps_of(rng, extent, shards, -0.22, 0.18)
    return jnp.clip(values, -most, most).astype(kind)


def setup_inputs(seed: int = 0) -> dict:
    splits = jax.random.split(jax.random.key(seed), 8)
    rhs = draw_rhs(jax.random.fold_in(splits[7], 71), 0)
    counts = draw_counts(jax.random.fold_in(splits[7], 71), 0)
    solve_panel = draw_solve_panel(jax.random.fold_in(splits[7], 71), 0)
    dirichlet_panel = draw_dirichlet_panel(jax.random.fold_in(splits[7], 71), 0)
    coupling = normal_values(splits[4], (SECTORS, CHAIN, NC, P_SIZE), P_SIZE ** -0.5, 0.25, ((0, 4), (1, 8)), jnp.float32)
    corner_map = plant(jax.random.randint(splits[5], (SECTORS, CHAIN, NC), 0, NCO), jax.random.fold_in(splits[5], 1), 0, NCO - 1).astype(jnp.int32)
    coarse_inverse = draw_coarse_inverse(jax.random.fold_in(splits[7], 71), 0)
    return dict(rhs=rhs, counts=counts, solve_panel=solve_panel, dirichlet_panel=dirichlet_panel, coupling=coupling, corner_map=corner_map, coarse_inverse=coarse_inverse)


HIGH = lax.Precision.HIGHEST


def spread_faces(values):
    prior = jnp.concatenate([jnp.zeros_like(values[:, :1]), values[:, :-1]], axis=1)
    return jnp.concatenate([-prior, values], axis=3)


def face_jump(result, live_mask):
    width = result.shape[3] // 2
    following = jnp.concatenate([result[:, 1:, :, :width], jnp.zeros_like(result[:, :1, :, :width])], axis=1)
    return live_mask * (result[..., width:] - following)


def panel_apply(panel, face_vals):
    def one_sector(pair):
        block, vals = pair
        return jnp.einsum("crp,cqp->crq", vals, block.astype(jnp.float32), precision=HIGH)
    return lax.map(one_sector, (panel, face_vals))


def coarse_apply(face_vals, coupling, corner_map, coarse_inverse):
    sectors, chain, corners = corner_map.shape
    slabs, size = coarse_inverse.shape[0], coarse_inverse.shape[1]
    loads = face_vals.shape[2]
    corner_vals = jnp.einsum("gcrp,gckp->gcrk", face_vals, coupling, precision=HIGH)
    onehot = (corner_map[..., None] == jnp.arange(size, dtype=jnp.int32)).astype(jnp.float32)
    onehot = onehot.reshape(sectors, slabs, chain // slabs, corners, size)
    corner_vals = corner_vals.reshape(sectors, slabs, chain // slabs, loads, corners)
    totals = jnp.einsum("gaskn,gasrk->anr", onehot, corner_vals, precision=HIGH)
    solved = jnp.einsum("amn,anr->amr", coarse_inverse, totals, precision=HIGH)
    back = jnp.einsum("gaskn,anr->gasrk", onehot, solved, precision=HIGH)
    back = back.reshape(sectors, chain, loads, corners)
    return jnp.einsum("gcrk,gckp->gcrp", back, coupling, precision=HIGH)


def reference(rhs, counts, solve_panel, dirichlet_panel, coupling, corner_map, coarse_inverse):
    sectors, chain, loads, width = rhs.shape
    positions = jnp.arange(width, dtype=jnp.int32)
    not_last = (jnp.arange(chain, dtype=jnp.int32) != chain - 1)
    live = (positions[None, None, :] < counts[:, :, None]) & not_last[None, :, None]
    live_mask = live.astype(jnp.float32)[:, :, None, :]

    def apply_dual(values):
        face_vals = spread_faces(values)
        result = panel_apply(solve_panel, face_vals) + coarse_apply(face_vals, coupling, corner_map, coarse_inverse)
        return face_jump(result, live_mask)

    def precondition(values):
        return 0.25 * face_jump(panel_apply(dirichlet_panel, spread_faces(values)), live_mask)

    def inner(first, second):
        return jnp.sum(first * second, axis=(0, 1, 3))

    def expand(scalars):
        return scalars[None, None, :, None]

    multipliers = jnp.zeros_like(rhs)
    residual = live_mask * rhs
    precond = precondition(residual)
    direction = precond
    rz_now = inner(residual, precond)
    for step in range(ITERS):
        image = apply_dual(direction)
        alpha = rz_now / inner(direction, image)
        multipliers = multipliers + expand(alpha) * direction
        residual = residual - expand(alpha) * image
        if step + 1 < ITERS:
            precond = precondition(residual)
            rz_next = inner(residual, precond)
            direction = precond + expand(rz_next / rz_now) * direction
            rz_now = rz_next
    return multipliers, residual
```

```python
import jax
import jax.numpy as jnp
from jax import lax
from jax.sharding import PartitionSpec as P

ITERS = 3


HIGH = lax.Precision.HIGH


def split(values):
    high = lax.reduce_precision(values, exponent_bits=8, mantissa_bits=7)
    return high.astype(jnp.bfloat16), (values - high).astype(jnp.bfloat16)


def neighbour_pairs(size, first):
    pairs = [(i, i + 1) for i in range(first, size - 1, 2)]
    return [route for a, b in pairs for route in ((a, b), (b, a))]


def swap_with_neighbours(to_next, to_prev, even):
    size = lax.axis_size("sub")
    near = lax.ppermute(jnp.where(even, to_next, to_prev), "sub", neighbour_pairs(size, 0))
    far = lax.ppermute(jnp.where(even, to_prev, to_next), "sub", neighbour_pairs(size, 1))
    return jnp.where(even, far, near), jnp.where(even, near, far)


def sum_all(rows):
    size = lax.axis_size("sub") * lax.axis_size("grp")
    copies = jnp.broadcast_to(rows[None], (size,) + rows.shape)
    return jnp.sum(lax.all_to_all(copies, ("sub", "grp"), 0, 0), axis=0)


def spread_faces(edges):
    return jnp.concatenate([-edges[:-1], edges[1:]], axis=2)


def panel_apply(panel, face_vals):
    high, low = split(face_vals)
    dims = (((2,), (2,)), ((0,), (0,)))
    return lax.dot_general(high, panel, dims, preferred_element_type=jnp.float32) + lax.dot_general(
        low, panel, dims, preferred_element_type=jnp.float32
    )


def face_jump(result, live, even):
    width = result.shape[2] // 2
    from_prev, from_next = swap_with_neighbours(result[-1, :, width:], result[0, :, :width], even)
    right = jnp.concatenate([from_prev[None], result[:, :, width:]], axis=0)
    left = jnp.concatenate([result[:, :, :width], from_next[None]], axis=0)
    return live * (right - left)


def coarse_block(corner_map, coarse_inverse):
    rows, size = coarse_inverse.shape
    own = corner_map.size
    grp, group = lax.axis_index("grp"), lax.axis_size("grp")
    everyone = lax.all_gather(corner_map.reshape(own), "grp", tiled=True)
    columns = (everyone[None, :] == jnp.arange(size, dtype=jnp.int32)[:, None]).astype(jnp.float32)
    picked = jnp.dot(coarse_inverse, columns, precision=HIGH)
    owned = jnp.arange(rows, dtype=jnp.int32) + grp * rows

    def rows_for(member):
        wanted = lax.dynamic_slice_in_dim(everyone, member * own, own)
        chosen = (wanted[:, None] == owned[None, :]).astype(jnp.float32)
        return jnp.dot(chosen, picked, precision=HIGH)

    block = rows_for(grp)
    for distance in range(1, group):
        routes = [(i, i ^ distance) for i in range(group)]
        block = block + lax.ppermute(rows_for(grp ^ distance), "grp", routes)
    return block


def inner(first, second):
    return jnp.sum(first * second, axis=(0, 2))


def expand(scalars):
    return scalars[None, :, None]


def local(rhs, counts, solve_panel, dirichlet_panel, coupling, corner_map, coarse_inverse):
    local_subs, loads, width = rhs.shape[1:]
    corners = coupling.shape[2]
    place = lax.axis_index("sub")
    even = place % 2 == 0
    last_device = place == lax.axis_size("sub") - 1
    slots = jnp.arange(local_subs, dtype=jnp.int32)
    positions = jnp.arange(width, dtype=jnp.int32)
    not_last = jnp.logical_not(last_device & (slots == local_subs - 1))
    live = ((positions[None, :] < counts[0][:, None]) & not_last[:, None]).astype(jnp.float32)
    residual = live[:, None, :] * rhs[0]

    size = lax.axis_size("sub")
    tail = jnp.concatenate([residual[-1], jnp.broadcast_to(live[-1:], (8, width))], axis=0)
    head = lax.ppermute(tail, "sub", [(i, i + 1) for i in range(size - 1)])
    residual = jnp.concatenate([head[None, :loads], residual], axis=0)
    live = jnp.concatenate([head[loads : loads + 1], live], axis=0)[:, None, :]

    block = coarse_block(corner_map[0], coarse_inverse[0])

    def precondition(edges):
        return face_jump(panel_apply(dirichlet_panel[0], spread_faces(edges)), 0.25 * live, even)

    def apply_dual(edges):
        faces = spread_faces(edges)
        corner_vals = jnp.einsum("skp,srp->skr", coupling[0], faces, precision=HIGH)
        everyone = lax.all_gather(
            corner_vals.reshape(local_subs * corners, loads), "grp", tiled=True
        )
        back = jnp.dot(block, everyone, precision=HIGH).reshape(local_subs, corners, loads)
        result = panel_apply(solve_panel[0], faces) + jnp.einsum(
            "skr,skp->srp", back, coupling[0], precision=HIGH
        )
        return face_jump(result, live, even)

    multipliers = jnp.zeros_like(rhs[0])
    precond = precondition(residual)
    image = apply_dual(precond)
    for step in range(ITERS):
        sums = sum_all(
            jnp.stack([inner(residual[1:], precond[1:]), inner(image[1:], precond[1:])])
        )
        if step + 1 < ITERS:
            next_precond = precondition(image)
            next_image = apply_dual(next_precond)
        rz_now, curvature = sums[0], sums[1]
        if step == 0:
            alpha = rz_now / curvature
            direction, direction_image = precond, image
            step_precond, step_image = next_precond, next_image
        else:
            beta = rz_now / rz_before
            alpha = rz_now / (curvature - beta * rz_now / alpha)
            direction = precond + expand(beta) * direction
            direction_image = image + expand(beta) * direction_image
            if step + 1 < ITERS:
                step_precond = next_precond + expand(beta) * step_precond
                step_image = next_image + expand(beta) * step_image
        multipliers = multipliers + expand(alpha) * direction[1:]
        residual = residual - expand(alpha) * direction_image
        if step + 1 < ITERS:
            precond = precond - expand(alpha) * step_precond
            image = image - expand(alpha) * step_image
        rz_before = rz_now
    return (multipliers[None], residual[1:][None])


def solution(mesh):
    return jax.shard_map(
        local,
        mesh=mesh,
        in_specs=(
            P("grp", "sub", None, None),
            P("grp", "sub"),
            P("grp", "sub", None, None),
            P("grp", "sub", None, None),
            P("grp", "sub", None, None),
            P("grp", "sub", None),
            P("sub", "grp", None),
        ),
        out_specs=(P("grp", "sub", None, None), P("grp", "sub", None, None)),
        check_vma=False,
    )
```

```python
import functools

import jax
import jax.numpy as jnp
from jax import lax
from jax.experimental import pallas as pl
from jax.experimental.pallas import tpu as pltpu
from jax.sharding import PartitionSpec as P

ITERS = 3


HIGH = lax.Precision.HIGH
VMEM_LIMIT = 32 * 1024 * 1024


def split(values):
    high = values.astype(jnp.bfloat16)
    return high, (values - high.astype(jnp.float32)).astype(jnp.bfloat16)


def split_outside(values):
    high = lax.reduce_precision(values, exponent_bits=8, mantissa_bits=7)
    return high.astype(jnp.bfloat16), (values - high).astype(jnp.bfloat16)


def mul(first, second):
    return jnp.dot(first, second, preferred_element_type=jnp.float32)


def mul_rows(first, second):
    dims = (((1,), (1,)), ((), ()))
    return lax.dot_general(first, second, dims, preferred_element_type=jnp.float32)


def call(kernel, out_shapes, *operands):
    scalars = 1
    return pl.pallas_call(
        kernel,
        out_shape=[jax.ShapeDtypeStruct(shape, jnp.float32) for shape in out_shapes],
        in_specs=[pl.BlockSpec(memory_space=pltpu.SMEM)] * scalars
        + [pl.BlockSpec(memory_space=pltpu.VMEM)] * (len(operands) - scalars),
        out_specs=[pl.BlockSpec(memory_space=pltpu.VMEM)] * len(out_shapes),
        compiler_params=pltpu.CompilerParams(vmem_limit_bytes=VMEM_LIMIT),
    )(*operands)


def jump_edges(even, result, near, far, live):
    subs, width = result.shape[0], result.shape[2] // 2
    for edge in range(subs + 1):
        if edge == 0:
            right = jnp.where(even, far[...], near[...])
        else:
            right = result[edge - 1, :, width:]
        if edge == subs:
            left = jnp.where(even, near[...], far[...])
        else:
            left = result[edge, :, :width]
        yield edge, live[edge] * (right - left)


def send_faces(even, result, near_out, far_out):
    subs, width = result.shape[0], result.shape[2] // 2
    to_next, to_prev = result[subs - 1, :, width:], result[0, :, :width]
    near_out[...] = jnp.where(even, to_next, to_prev)
    far_out[...] = jnp.where(even, to_prev, to_next)


def panel_products(edges, panel, result, extra=None):
    parts = [split(edges[edge]) for edge in range(edges.shape[0])]
    for sub in range(panel.shape[0]):
        high = jnp.concatenate([-parts[sub][0], parts[sub + 1][0]], axis=1)
        low = jnp.concatenate([-parts[sub][1], parts[sub + 1][1]], axis=1)
        total = mul(high, panel[sub]) + mul(low, panel[sub])
        if extra is not None:
            total = total + extra(sub)
        result[sub] = total


def column(row, width):
    lanes = jnp.broadcast_to(row, (128, row.shape[1])).T
    return jnp.concatenate([lanes] * (width // 128), axis=1)


def row_sums(values):
    ones = jnp.ones((8, values.shape[1]), jnp.bfloat16)
    high, rest = split(values)
    middle, low = split(values - high.astype(jnp.float32))
    return (mul_rows(ones, high) + mul_rows(ones, middle) + mul_rows(ones, low))[:1]


def step_scalars(step, sums, before):
    totals = jnp.sum(sums[...], axis=0)
    rz_now, curvature = totals[:1], totals[1:2]
    if step == 0:
        return rz_now, rz_now / curvature, None
    beta = rz_now / before[0:1]
    return rz_now, rz_now / (curvature - beta * rz_now / before[1:2]), beta


def first_kernel(even_ref, edges, panel, result, near_out, far_out):
    panel_products(edges, panel, result)
    send_faces(even_ref[0] == 1, result, near_out, far_out)


def corner_kernel(even_ref, result, near, far, live, coupling, edges, corners):
    even = even_ref[0] == 1
    width = result.shape[2] // 2
    subs, rows = coupling.shape[0], coupling.shape[1] // 2
    for edge, value in jump_edges(even, result, near, far, live):
        edges[edge] = value
    parts = [split(edges[edge]) for edge in range(subs + 1)]
    for sub in range(subs):
        high = jnp.concatenate([-parts[sub][0], parts[sub + 1][0]], axis=1)
        low = jnp.concatenate([-parts[sub][1], parts[sub + 1][1]], axis=1)
        both = mul_rows(coupling[sub], high)
        corners[sub * rows : (sub + 1) * rows, :] = (
            both[:rows] + both[rows:] + mul_rows(coupling[sub, :rows], low)
        )


def dual_kernel(
    even_ref, edges, residual, panel, everyone, block, lift, result, near_out, far_out, sums
):
    even = even_ref[0] == 1
    subs, width = panel.shape[0], edges.shape[2]
    rows = block.shape[0] // 2
    high, low = split(everyone[...])
    both = mul(block[...], high)
    back = (both[:rows] + both[rows:] + mul(block[:rows], low)).T
    back_high, back_low = split(back)
    lifted = jnp.concatenate([back_high, back_low, back_high], axis=1)
    panel_products(edges, panel, result, lambda sub: mul(lifted, lift[sub]))
    send_faces(even, result, near_out, far_out)
    product = residual[1] * edges[1]
    curvature = result[0, :, width:] * edges[1] - result[0, :, :width] * edges[0]
    for sub in range(1, subs):
        product = product + residual[sub + 1] * edges[sub + 1]
        curvature = curvature + (
            result[sub, :, width:] * edges[sub + 1] - result[sub, :, :width] * edges[sub]
        )
    sums[...] = jnp.concatenate([row_sums(product), row_sums(curvature)], axis=0)


def update_kernel(step, even_ref, result, near, far, live, sums, before, image_old, residual,
                  panel, image_new, residual_new, result_new, near_out, far_out, scalars):
    even = even_ref[0] == 1
    width = near.shape[1]
    rz_now, alpha, beta = step_scalars(step, sums, before)
    scalars[...] = jnp.concatenate([rz_now, alpha], axis=0)
    alpha_column = column(alpha, width)
    beta_column = None if beta is None else column(beta, width)
    for edge, value in jump_edges(even, result, near, far, live):
        if beta is not None:
            value = value + beta_column * image_old[edge]
        image_new[edge] = value
        residual_new[edge] = residual[edge] - alpha_column * value
    panel_products(residual_new, panel, result_new)
    send_faces(even, result_new, near_out, far_out)


def last_kernel(step, even_ref, result, near, far, live, sums, before, older, image_old, residual,
                first, second, third, multipliers, residual_new):
    even = even_ref[0] == 1
    width = near.shape[1]
    rz_now, alpha, beta = step_scalars(step, sums, before)
    beta_before = before[0:1] / older[0:1]
    on_second = before[1:2] + alpha * beta
    on_first = older[1:2] + on_second * beta_before
    alpha_column, beta_column = column(alpha, width), column(beta, width)
    second_column, first_column = column(on_second, width), column(on_first, width)
    for edge, value in jump_edges(even, result, near, far, live):
        if edge > 0:
            value = value + beta_column * image_old[edge]
            residual_new[edge - 1] = residual[edge] - alpha_column * value
            multipliers[edge - 1] = (
                first_column * first[edge]
                + second_column * second[edge]
                + alpha_column * third[edge]
            )


def neighbour_pairs(size, first):
    pairs = [(i, i + 1) for i in range(first, size - 1, 2)]
    return [route for a, b in pairs for route in ((a, b), (b, a))]


def swap(near, far):
    size = lax.axis_size("sub")
    return (
        lax.ppermute(near, "sub", neighbour_pairs(size, 0)),
        lax.ppermute(far, "sub", neighbour_pairs(size, 1)),
    )


def from_all(rows):
    size = lax.axis_size("sub") * lax.axis_size("grp")
    copies = jnp.broadcast_to(rows[None], (size,) + rows.shape)
    return lax.all_to_all(copies, ("sub", "grp"), 0, 0)


def coarse_block(corner_map, coarse_inverse):
    rows, size = coarse_inverse.shape
    own = corner_map.size
    grp, group = lax.axis_index("grp"), lax.axis_size("grp")
    everyone = lax.all_gather(corner_map.reshape(own), "grp", tiled=True)
    columns = (everyone[None, :] == jnp.arange(size, dtype=jnp.int32)[:, None]).astype(jnp.float32)
    picked = jnp.dot(coarse_inverse, columns, precision=HIGH)
    owned = jnp.arange(rows, dtype=jnp.int32) + grp * rows

    def rows_for(member):
        wanted = lax.dynamic_slice_in_dim(everyone, member * own, own)
        chosen = (wanted[:, None] == owned[None, :]).astype(jnp.float32)
        return jnp.dot(chosen, picked, precision=HIGH)

    block = rows_for(grp)
    for distance in range(1, group):
        routes = [(i, i ^ distance) for i in range(group)]
        block = block + lax.ppermute(rows_for(grp ^ distance), "grp", routes)
    return block


def local(rhs, counts, solve_panel, dirichlet_panel, coupling, corner_map, coarse_inverse):
    subs, loads, width = rhs.shape[1:]
    corners = coupling.shape[2]
    solve, dirichlet, couple = solve_panel[0], dirichlet_panel[0], coupling[0]
    place, size = lax.axis_index("sub"), lax.axis_size("sub")
    even = (1 - place % 2).astype(jnp.int32).reshape(1)
    slots = jnp.arange(subs, dtype=jnp.int32)
    positions = jnp.arange(width, dtype=jnp.int32)
    not_last = jnp.logical_not((place == size - 1) & (slots == subs - 1))
    live = ((positions[None, :] < counts[0][:, None]) & not_last[:, None]).astype(jnp.float32)
    residual = live[:, None, :] * rhs[0]

    tail = jnp.concatenate([residual[-1], jnp.broadcast_to(live[-1:], (8, width))], axis=0)
    head = lax.ppermute(tail, "sub", [(i, i + 1) for i in range(size - 1)])
    residual = jnp.concatenate([head[None, :loads], residual], axis=0)
    live = jnp.concatenate([head[loads : loads + 1], live], axis=0)[:, None, :]

    block = jnp.concatenate(split_outside(coarse_block(corner_map[0], coarse_inverse[0])), axis=0)
    high, low = split_outside(couple)
    stacked = jnp.concatenate([high, low], axis=1)
    own = (slots[:, None] == slots[None, :])[:, :, None, None]

    def placed(part):
        wide = jnp.where(own, part[:, None], jnp.zeros((), part.dtype))
        return wide.reshape(subs, subs * corners, 2 * width)

    lift = jnp.concatenate([placed(high), placed(high), placed(low)], axis=1)

    edges_shape = (subs + 1, loads, width)
    result_shape = (subs, loads, 2 * width)
    face_shape = (loads, width)
    faces = [result_shape, face_shape, face_shape]

    result, near, far = call(first_kernel, faces, even, residual, dirichlet)
    scalars, images, preconds, image = [jnp.zeros((2, loads), jnp.float32)], [], [], None
    for step in range(ITERS):
        near, far = swap(near, far)
        edges, values = call(
            corner_kernel,
            [edges_shape, (subs * corners, loads)],
            even, result, near, far, 0.25 * live, stacked,
        )
        preconds.append(edges)
        everyone = lax.all_gather(values, "grp", tiled=True)
        result, near, far, sums = call(
            dual_kernel,
            faces + [(2, loads)],
            even, edges, residual, solve, everyone, block, lift,
        )
        sums = from_all(sums)
        near, far = swap(near, far)
        if step + 1 < ITERS:
            old = residual if image is None else image
            image, residual, result, near, far, now = call(
                functools.partial(update_kernel, step),
                [edges_shape, edges_shape] + faces + [(2, loads)],
                even, result, near, far, live, sums, scalars[-1], old, residual, dirichlet,
            )
            scalars.append(now)
    multipliers, residual = call(
        functools.partial(last_kernel, ITERS - 1),
        [(subs, loads, width)] * 2,
        even, result, near, far, live, sums, scalars[-1], scalars[-2], image, residual, *preconds,
    )
    return (multipliers[None], residual[None])


def solution(mesh):
    return jax.shard_map(
        local,
        mesh=mesh,
        in_specs=(
            P("grp", "sub", None, None),
            P("grp", "sub"),
            P("grp", "sub", None, None),
            P("grp", "sub", None, None),
            P("grp", "sub", None, None),
            P("grp", "sub", None),
            P("sub", "grp", None),
        ),
        out_specs=(P("grp", "sub", None, None), P("grp", "sub", None, None)),
        check_vma=False,
    )
```

```python
import functools

import jax
import jax.numpy as jnp
from jax import lax
from jax.experimental import pallas as pl
from jax.experimental.pallas import tpu as pltpu
from jax.sharding import PartitionSpec as P

ITERS = 3


HIGH = lax.Precision.HIGH
VMEM_LIMIT = 8 * 1024 * 1024


def split(values):
    high = values.astype(jnp.bfloat16)
    return high, (values - high.astype(jnp.float32)).astype(jnp.bfloat16)


def split_outside(values):
    high = lax.reduce_precision(values, exponent_bits=8, mantissa_bits=7)
    return high.astype(jnp.bfloat16), (values - high).astype(jnp.bfloat16)


def mul(first, second):
    return jnp.dot(first, second, preferred_element_type=jnp.float32)


def mul_rows(first, second):
    dims = (((1,), (1,)), ((), ()))
    return lax.dot_general(first, second, dims, preferred_element_type=jnp.float32)


def call(kernel, out_shapes, *operands, scalars=1):
    return pl.pallas_call(
        kernel,
        out_shape=[jax.ShapeDtypeStruct(shape, jnp.float32) for shape in out_shapes],
        in_specs=[pl.BlockSpec(memory_space=pltpu.SMEM)] * scalars
        + [pl.BlockSpec(memory_space=pltpu.VMEM)] * (len(operands) - scalars),
        out_specs=[pl.BlockSpec(memory_space=pltpu.VMEM)] * len(out_shapes),
        compiler_params=pltpu.CompilerParams(vmem_limit_bytes=VMEM_LIMIT),
    )(*operands)


def jump_edges(even, result, near, far, live):
    subs, width = result.shape[0], result.shape[2] // 2
    for edge in range(subs + 1):
        if edge == 0:
            right = jnp.where(even, far[...], near[...])
        else:
            right = result[edge - 1, :, width:]
        if edge == subs:
            left = jnp.where(even, near[...], far[...])
        else:
            left = result[edge, :, :width]
        yield edge, live[edge] * (right - left)


def send_faces(even, result, near_out, far_out):
    subs, width = result.shape[0], result.shape[2] // 2
    to_next, to_prev = result[subs - 1, :, width:], result[0, :, :width]
    near_out[...] = jnp.where(even, to_next, to_prev)
    far_out[...] = jnp.where(even, to_prev, to_next)


def panel_products(edges, panel, result, extra=None):
    parts = [split(edges[edge]) for edge in range(edges.shape[0])]
    for sub in range(panel.shape[0]):
        high = jnp.concatenate([-parts[sub][0], parts[sub + 1][0]], axis=1)
        low = jnp.concatenate([-parts[sub][1], parts[sub + 1][1]], axis=1)
        total = mul(high, panel[sub]) + mul(low, panel[sub])
        if extra is not None:
            total = total + extra(sub)
        result[sub] = total


def column(row, width):
    lanes = jnp.broadcast_to(row, (128, row.shape[1])).T
    return jnp.concatenate([lanes] * (width // 128), axis=1)


def row_sums(values):
    ones = jnp.ones((8, values.shape[1]), jnp.bfloat16)
    high, rest = split(values)
    middle, low = split(values - high.astype(jnp.float32))
    return (mul_rows(ones, high) + mul_rows(ones, middle) + mul_rows(ones, low))[:1]


def step_scalars(step, sums, before):
    totals = jnp.sum(sums[...], axis=0)
    rz_now, curvature = totals[:1], totals[1:2]
    if step == 0:
        return rz_now, rz_now / curvature, None
    beta = rz_now / before[0:1]
    return rz_now, rz_now / (curvature - beta * rz_now / before[1:2]), beta


def first_kernel(even_ref, counts, rhs, head, panel, edges, live, result, near_out, far_out):
    subs, loads, width = rhs.shape
    positions = lax.broadcasted_iota(jnp.int32, (1, width), 1)
    live[0] = head[loads : loads + 1]
    edges[0] = head[:loads]
    for sub in range(subs):
        mask = (positions < counts[sub]).astype(jnp.float32)
        live[sub + 1] = mask
        edges[sub + 1] = mask * rhs[sub]
    panel_products(edges, panel, result)
    send_faces(even_ref[0] == 1, result, near_out, far_out)


def pick_kernel(grp_ref, everyone, coarse, picked):
    group, own = everyone.shape[0], everyone.shape[2]
    rows, size = coarse.shape
    grp = grp_ref[0]
    high, rest = split(coarse[...])
    middle, low = split(coarse[...] - high.astype(jnp.float32))
    unknowns = lax.broadcasted_iota(jnp.int32, (size, own), 0)
    columns = []
    for member in range(group):
        chosen = (unknowns == everyone[member]).astype(jnp.bfloat16)
        columns.append(mul(high, chosen) + mul(middle, chosen) + mul(low, chosen))
    high, rest = split(jnp.concatenate(columns, axis=1))
    low = rest
    owned = lax.broadcasted_iota(jnp.int32, (rows, own), 0) + grp * rows
    dims = (((0,), (0,)), ((), ()))
    for distance in range(group):
        chosen = (owned == everyone[grp ^ distance]).astype(jnp.bfloat16)
        picked[distance] = lax.dot_general(
            chosen, high, dims, preferred_element_type=jnp.float32
        ) + lax.dot_general(chosen, low, dims, preferred_element_type=jnp.float32)


def corner_kernel(even_ref, result, near, far, live, coupling, edges, corners):
    even = even_ref[0] == 1
    width = result.shape[2] // 2
    subs, rows = coupling.shape[0], coupling.shape[1] // 2
    for edge, value in jump_edges(even, result, near, far, live):
        edges[edge] = 0.25 * value
    parts = [split(edges[edge]) for edge in range(subs + 1)]
    for sub in range(subs):
        high = jnp.concatenate([-parts[sub][0], parts[sub + 1][0]], axis=1)
        low = jnp.concatenate([-parts[sub][1], parts[sub + 1][1]], axis=1)
        both = mul_rows(coupling[sub], high)
        corners[sub * rows : (sub + 1) * rows, :] = (
            both[:rows] + both[rows:] + mul_rows(coupling[sub, :rows], low)
        )


def dual_kernel(
    even_ref, edges, residual, panel, everyone, block, lift, result, near_out, far_out, sums
):
    even = even_ref[0] == 1
    subs, width = panel.shape[0], edges.shape[2]
    rows = block.shape[0] // 2
    high, low = split(everyone[...])
    both = mul(block[...], high)
    back = (both[:rows] + both[rows:] + mul(block[:rows], low)).T
    back_high, back_low = split(back)
    lifted = jnp.concatenate([back_high, back_low, back_high], axis=1)
    panel_products(edges, panel, result, lambda sub: mul(lifted, lift[sub]))
    send_faces(even, result, near_out, far_out)
    product = residual[1] * edges[1]
    curvature = result[0, :, width:] * edges[1] - result[0, :, :width] * edges[0]
    for sub in range(1, subs):
        product = product + residual[sub + 1] * edges[sub + 1]
        curvature = curvature + (
            result[sub, :, width:] * edges[sub + 1] - result[sub, :, :width] * edges[sub]
        )
    sums[...] = jnp.concatenate([row_sums(product), row_sums(curvature)], axis=0)


def update_kernel(step, even_ref, result, near, far, live, sums, before, image_old, residual,
                  panel, image_new, residual_new, result_new, near_out, far_out, scalars):
    even = even_ref[0] == 1
    width = near.shape[1]
    rz_now, alpha, beta = step_scalars(step, sums, before)
    scalars[...] = jnp.concatenate([rz_now, alpha], axis=0)
    alpha_column = column(alpha, width)
    beta_column = None if beta is None else column(beta, width)
    for edge, value in jump_edges(even, result, near, far, live):
        if beta is not None:
            value = value + beta_column * image_old[edge]
        image_new[edge] = value
        residual_new[edge] = residual[edge] - alpha_column * value
    panel_products(residual_new, panel, result_new)
    send_faces(even, result_new, near_out, far_out)


def last_kernel(step, even_ref, result, near, far, live, sums, before, older, image_old, residual,
                first, second, third, multipliers, residual_new):
    even = even_ref[0] == 1
    width = near.shape[1]
    rz_now, alpha, beta = step_scalars(step, sums, before)
    beta_before = before[0:1] / older[0:1]
    on_second = before[1:2] + alpha * beta
    on_first = older[1:2] + on_second * beta_before
    alpha_column, beta_column = column(alpha, width), column(beta, width)
    second_column, first_column = column(on_second, width), column(on_first, width)
    for edge, value in jump_edges(even, result, near, far, live):
        if edge > 0:
            value = value + beta_column * image_old[edge]
            residual_new[edge - 1] = residual[edge] - alpha_column * value
            multipliers[edge - 1] = (
                first_column * first[edge]
                + second_column * second[edge]
                + alpha_column * third[edge]
            )


def neighbour_pairs(size, first):
    pairs = [(i, i + 1) for i in range(first, size - 1, 2)]
    return [route for a, b in pairs for route in ((a, b), (b, a))]


def swap(near, far):
    size = lax.axis_size("sub")
    return (
        lax.ppermute(near, "sub", neighbour_pairs(size, 0)),
        lax.ppermute(far, "sub", neighbour_pairs(size, 1)),
    )


def from_all(rows):
    size = lax.axis_size("sub") * lax.axis_size("grp")
    copies = jnp.broadcast_to(rows[None], (size,) + rows.shape)
    return lax.all_to_all(copies, ("sub", "grp"), 0, 0)


def coarse_block(everyone, coarse_inverse):
    group, own = everyone.shape[0], everyone.shape[2]
    grp = lax.axis_index("grp").reshape(1)
    (picked,) = call(pick_kernel, [(group, own, group * own)], grp, everyone, coarse_inverse)
    block = picked[0]
    for distance in range(1, group):
        routes = [(i, i ^ distance) for i in range(group)]
        block = block + lax.ppermute(picked[distance], "grp", routes)
    return block


def local(rhs, counts, solve_panel, dirichlet_panel, coupling, corner_map, coarse_inverse):
    subs, loads, width = rhs.shape[1:]
    corners = coupling.shape[2]
    solve, dirichlet, couple = solve_panel[0], dirichlet_panel[0], coupling[0]
    place, size = lax.axis_index("sub"), lax.axis_size("sub")
    even = (1 - place % 2).astype(jnp.int32).reshape(1)
    slots = jnp.arange(subs, dtype=jnp.int32)
    live_counts = jnp.where((place == size - 1) & (slots == subs - 1), 0, counts[0])
    positions = jnp.arange(width, dtype=jnp.int32)
    last_live = (positions < live_counts[-1]).astype(jnp.float32)
    tail = jnp.concatenate(
        [last_live * rhs[0, -1], jnp.broadcast_to(last_live, (8, width))], axis=0
    )
    tail, corner_map = lax.optimization_barrier((tail, corner_map))
    head = lax.ppermute(tail, "sub", [(i, i + 1) for i in range(size - 1)])
    everyone = lax.all_gather(corner_map.reshape(1, subs * corners), "grp")

    edges_shape = (subs + 1, loads, width)
    result_shape = (subs, loads, 2 * width)
    face_shape = (loads, width)
    faces = [result_shape, face_shape, face_shape]

    residual, live, result, near, far = call(
        first_kernel,
        [edges_shape, (subs + 1, 1, width)] + faces,
        even, live_counts, rhs[0], head, dirichlet, scalars=2,
    )
    result, everyone, couple = lax.optimization_barrier((result, everyone, couple))
    block = jnp.concatenate(split_outside(coarse_block(everyone, coarse_inverse[0])), axis=0)
    high, low = split_outside(couple)
    stacked = jnp.concatenate([high, low], axis=1)
    own = (slots[:, None] == slots[None, :])[:, :, None, None]

    def placed(part):
        wide = jnp.where(own, part[:, None], jnp.zeros((), part.dtype))
        return wide.reshape(subs, subs * corners, 2 * width)

    lift = jnp.concatenate([placed(high), placed(high), placed(low)], axis=1)

    scalars, preconds, image = [jnp.zeros((2, loads), jnp.float32)], [], None
    for step in range(ITERS):
        near, far = swap(near, far)
        edges, values = call(
            corner_kernel,
            [edges_shape, (subs * corners, loads)],
            even, result, near, far, live, stacked,
        )
        preconds.append(edges)
        everyone = lax.all_gather(values, "grp", tiled=True)
        result, near, far, sums = call(
            dual_kernel,
            faces + [(2, loads)],
            even, edges, residual, solve, everyone, block, lift,
        )
        sums = from_all(sums)
        near, far = swap(near, far)
        if step + 1 < ITERS:
            old = residual if image is None else image
            image, residual, result, near, far, now = call(
                functools.partial(update_kernel, step),
                [edges_shape, edges_shape] + faces + [(2, loads)],
                even, result, near, far, live, sums, scalars[-1], old, residual, dirichlet,
            )
            scalars.append(now)
    multipliers, residual = call(
        functools.partial(last_kernel, ITERS - 1),
        [(subs, loads, width)] * 2,
        even, result, near, far, live, sums, scalars[-1], scalars[-2], image, residual, *preconds,
    )
    return (multipliers[None], residual[None])


def solution(mesh):
    return jax.shard_map(
        local,
        mesh=mesh,
        in_specs=(
            P("grp", "sub", None, None),
            P("grp", "sub"),
            P("grp", "sub", None, None),
            P("grp", "sub", None, None),
            P("grp", "sub", None, None),
            P("grp", "sub", None),
            P("sub", "grp", None),
        ),
        out_specs=(P("grp", "sub", None, None), P("grp", "sub", None, None)),
        check_vma=False,
    )
```

```python
import functools

import jax
import jax.numpy as jnp
from jax import lax
from jax.experimental import pallas as pl
from jax.experimental.pallas import tpu as pltpu
from jax.sharding import PartitionSpec as P

ITERS = 3


VMEM_LIMIT = 8 * 1024 * 1024
TAIL_LIMIT = 62 * 1024 * 1024


def split(values):
    high = values.astype(jnp.bfloat16)
    return high, (values - high.astype(jnp.float32)).astype(jnp.bfloat16)


def split_outside(values):
    high = lax.reduce_precision(values, exponent_bits=8, mantissa_bits=7)
    return high.astype(jnp.bfloat16), (values - high).astype(jnp.bfloat16)


def mul(first, second):
    return jnp.dot(first, second, preferred_element_type=jnp.float32)


def mul_rows(first, second):
    dims = (((1,), (1,)), ((), ()))
    return lax.dot_general(first, second, dims, preferred_element_type=jnp.float32)


def call(kernel, out_shapes, *operands, scalars=1):
    return pl.pallas_call(
        kernel,
        out_shape=[jax.ShapeDtypeStruct(shape, jnp.float32) for shape in out_shapes],
        in_specs=[pl.BlockSpec(memory_space=pltpu.SMEM)] * scalars
        + [pl.BlockSpec(memory_space=pltpu.VMEM)] * (len(operands) - scalars),
        out_specs=[pl.BlockSpec(memory_space=pltpu.VMEM)] * len(out_shapes),
        compiler_params=pltpu.CompilerParams(vmem_limit_bytes=VMEM_LIMIT),
    )(*operands)


class Joined:
    def __init__(self, first, rest):
        self.first, self.rest = first, rest

    def __getitem__(self, place):
        return self.first[...] if place == 0 else self.rest[place - 1]

    def __setitem__(self, place, value):
        if place == 0:
            self.first[...] = value
        else:
            self.rest[place - 1] = value


def jump_edge(even, result, near, far, live, edge, subs):
    width = near.shape[1]
    if edge == 0:
        right = jnp.where(even, far[...], near[...])
    else:
        right = result[edge - 1][:, width:]
    if edge == subs:
        left = jnp.where(even, near[...], far[...])
    else:
        left = result[edge][:, :width]
    return live[edge] * (right - left)


def send_faces(even, first, last, near_out, far_out):
    width = first.shape[1] // 2
    to_next, to_prev = last[:, width:], first[:, :width]
    near_out[...] = jnp.where(even, to_next, to_prev)
    far_out[...] = jnp.where(even, to_prev, to_next)


def panel_products(parts, panel, result, extra=None):
    subs = panel.shape[0]
    for sub in range(subs):
        high = jnp.concatenate([-parts[sub][0], parts[sub + 1][0]], axis=1)
        low = jnp.concatenate([-parts[sub][1], parts[sub + 1][1]], axis=1)
        total = mul(high, panel[sub]) + mul(low, panel[sub])
        if extra is not None:
            total = total + extra(sub)
        result[sub] = total


def column(row, width):
    lanes = jnp.broadcast_to(row, (128, row.shape[1])).T
    return jnp.concatenate([lanes] * (width // 128), axis=1)


def row_sums(values):
    ones = jnp.ones((8, values.shape[1]), jnp.bfloat16)
    high, rest = split(values)
    middle, low = split(values - high.astype(jnp.float32))
    return (mul_rows(ones, high) + mul_rows(ones, middle) + mul_rows(ones, low))[:1]


def step_scalars(step, sums, before):
    totals = jnp.sum(sums[...], axis=0)
    rz_now, curvature = totals[:1], totals[1:2]
    if step == 0:
        return rz_now, rz_now / curvature, None
    beta = rz_now / before[0:1]
    return rz_now, rz_now / (curvature - beta * rz_now / before[1:2]), beta


def tail_kernel(places, counts, rhs, tail, face, done):
    loads, width = rhs.shape[2:]
    copy = pltpu.make_async_copy(rhs.at[0, rhs.shape[1] - 1], face, done)
    copy.start()
    last = jnp.where(places[2] == 1, 0, counts[0, counts.shape[1] - 1])
    mask = (lax.broadcasted_iota(jnp.int32, (8, width), 1) < last).astype(jnp.float32)
    tail[loads:] = mask
    copy.wait()
    tail[:loads] = mask[:1] * face[...]


def early_kernel(places, counts, rhs, panel, live, own, partial, rest):
    subs, loads, width = own.shape
    positions = lax.broadcasted_iota(jnp.int32, (1, width), 1)
    parts = [None]
    for sub in range(subs):
        count = counts[0, sub]
        if sub == subs - 1:
            count = jnp.where(places[2] == 1, 0, count)
        mask = (positions < count).astype(jnp.float32)
        live[sub] = mask
        own[sub] = mask * rhs[0, sub]
        parts.append(split(own[sub]))
    partial[...] = mul(parts[1][0], panel[0, width:]) + mul(parts[1][1], panel[0, width:])
    for sub in range(1, subs):
        high = jnp.concatenate([-parts[sub][0], parts[sub + 1][0]], axis=1)
        low = jnp.concatenate([-parts[sub][1], parts[sub + 1][1]], axis=1)
        rest[sub - 1] = mul(high, panel[sub]) + mul(low, panel[sub])


def head_kernel(places, head, partial, rest, panel, live, edge, first, near_out, far_out):
    loads, width = edge.shape
    live[...] = head[loads : loads + 1]
    edge[...] = head[:loads]
    high, low = split(head[:loads])
    first[...] = partial[...] - mul(high, panel[0, :width]) - mul(low, panel[0, :width])
    last = rest[rest.shape[0] - 1]
    send_faces(places[0] == 1, first[...], last, near_out, far_out)


def pick_kernel(places, everyone, coarse, picked):
    group, own = everyone.shape[0], everyone.shape[2]
    rows, size = coarse.shape
    grp = places[1]
    high, low = split(coarse[...])
    unknowns = lax.broadcasted_iota(jnp.int32, (size, own), 0)
    columns = []
    for member in range(group):
        chosen = (unknowns == everyone[grp ^ member]).astype(jnp.bfloat16)
        columns.append(mul(high, chosen) + mul(low, chosen))
    high, low = split(jnp.concatenate(columns, axis=1))
    owned = lax.broadcasted_iota(jnp.int32, (rows, own), 0) + grp * rows
    dims = (((0,), (0,)), ((), ()))
    for distance in range(group):
        chosen = (owned == everyone[distance]).astype(jnp.bfloat16)
        picked[distance] = lax.dot_general(
            chosen, high, dims, preferred_element_type=jnp.float32
        ) + lax.dot_general(chosen, low, dims, preferred_element_type=jnp.float32)


def corner_kernel(places, first, rest, near, far, live_first, live_rest, coupling,
                  edge, own, corners):
    even = places[0] == 1
    subs, rows = coupling.shape[0], coupling.shape[1] // 2
    result, live, edges = Joined(first, rest), Joined(live_first, live_rest), Joined(edge, own)
    parts = []
    for place in range(subs + 1):
        edges[place] = 0.25 * jump_edge(even, result, near, far, live, place, subs)
        parts.append(split(edges[place]))
    for sub in range(subs):
        high = jnp.concatenate([-parts[sub][0], parts[sub + 1][0]], axis=1)
        low = jnp.concatenate([-parts[sub][1], parts[sub + 1][1]], axis=1)
        both = mul_rows(coupling[sub], high)
        corners[sub * rows : (sub + 1) * rows, :] = (
            both[:rows] + both[rows:] + mul_rows(coupling[sub, :rows], low)
        )


def dual_kernel(places, edge, own, residual, panel, everyone, block, lift,
                first, rest, near_out, far_out, sums):
    even = places[0] == 1
    subs, width = panel.shape[0], edge.shape[1]
    edges, result = Joined(edge, own), Joined(first, rest)
    rows = block.shape[0] // 2
    high, low = split(everyone[...])
    both = mul(block[...], high)
    back = (both[:rows] + both[rows:] + mul(block[:rows], low)).T
    back_high, back_low = split(back)
    lifted = jnp.concatenate([back_high, back_low, back_high], axis=1)
    parts = [split(edges[place]) for place in range(subs + 1)]
    panel_products(parts, panel, result, lambda sub: mul(lifted, lift[sub]))
    send_faces(even, result[0], result[subs - 1], near_out, far_out)
    product = curvature = 0.0
    for sub in range(subs):
        product = product + residual[sub] * edges[sub + 1]
        curvature = curvature + (
            result[sub][:, width:] * edges[sub + 1] - result[sub][:, :width] * edges[sub]
        )
    sums[...] = jnp.concatenate([row_sums(product), row_sums(curvature)], axis=0)


def update_kernel(step, places, first, rest, near, far, live_first, live_rest, sums, before,
                  old_edge, old_own, residual_edge, residual_own, panel,
                  image_edge, image_own, new_edge, new_own,
                  first_new, rest_new, near_out, far_out, scalars):
    even = places[0] == 1
    subs, width = panel.shape[0], near.shape[1]
    result, live = Joined(first, rest), Joined(live_first, live_rest)
    image_old, residual = Joined(old_edge, old_own), Joined(residual_edge, residual_own)
    image, residual_new = Joined(image_edge, image_own), Joined(new_edge, new_own)
    result_new = Joined(first_new, rest_new)
    rz_now, alpha, beta = step_scalars(step, sums, before)
    scalars[...] = jnp.concatenate([rz_now, alpha], axis=0)
    alpha_column = column(alpha, width)
    beta_column = None if beta is None else column(beta, width)
    parts = []
    for place in range(subs + 1):
        value = jump_edge(even, result, near, far, live, place, subs)
        if beta is not None:
            value = value + beta_column * image_old[place]
        image[place] = value
        residual_new[place] = residual[place] - alpha_column * value
        parts.append(split(residual_new[place]))
    panel_products(parts, panel, result_new)
    send_faces(even, result_new[0], result_new[subs - 1], near_out, far_out)


def last_kernel(step, places, first, rest, following, live, sums, before, older, image_old,
                residual, first_z, second_z, third_z, multipliers, residual_new):
    subs, width = residual.shape[0], following.shape[1]
    result = Joined(first, rest)
    rz_now, alpha, beta = step_scalars(step, sums, before)
    beta_before = before[0:1] / older[0:1]
    on_second = before[1:2] + alpha * beta
    on_first = older[1:2] + on_second * beta_before
    alpha_column, beta_column = column(alpha, width), column(beta, width)
    second_column, first_column = column(on_second, width), column(on_first, width)
    for sub in range(subs):
        left = following[...] if sub == subs - 1 else result[sub + 1][:, :width]
        image = live[sub] * (result[sub][:, width:] - left) + beta_column * image_old[sub]
        residual_new[sub] = residual[sub] - alpha_column * image
        multipliers[sub] = (
            first_column * first_z[sub]
            + second_column * second_z[sub]
            + alpha_column * third_z[sub]
        )


def neighbour_pairs(size, first):
    pairs = [(i, i + 1) for i in range(first, size - 1, 2)]
    return [route for a, b in pairs for route in ((a, b), (b, a))]


def swap(near, far):
    size = lax.axis_size("sub")
    return (
        lax.ppermute(near, "sub", neighbour_pairs(size, 0)),
        lax.ppermute(far, "sub", neighbour_pairs(size, 1)),
    )


def from_all(rows):
    size = lax.axis_size("sub") * lax.axis_size("grp")
    copies = jnp.broadcast_to(rows[None], (size,) + rows.shape)
    return lax.all_to_all(copies, ("sub", "grp"), 0, 0)


def from_group(values):
    group = lax.axis_size("grp")
    received = [values]
    for distance in range(1, group):
        routes = [(i, i ^ distance) for i in range(group)]
        received.append(lax.ppermute(values, "grp", routes))
    return jnp.stack(received)


def swap_blocks(picked):
    group = lax.axis_size("grp")
    block = picked[0]
    for distance in range(1, group):
        routes = [(i, i ^ distance) for i in range(group)]
        block = block + lax.ppermute(picked[distance], "grp", routes)
    return block


def make_tail(places, counts, rhs):
    loads, width = rhs.shape[2:]
    return pl.pallas_call(
        tail_kernel,
        out_shape=jax.ShapeDtypeStruct((loads + 8, width), jnp.float32),
        in_specs=[
            pl.BlockSpec(memory_space=pltpu.SMEM),
            pl.BlockSpec(memory_space=pltpu.SMEM),
            pl.BlockSpec(memory_space=pltpu.HBM),
        ],
        out_specs=pl.BlockSpec(memory_space=pltpu.VMEM),
        scratch_shapes=[pltpu.VMEM((loads, width), jnp.float32), pltpu.SemaphoreType.DMA],
        compiler_params=pltpu.CompilerParams(vmem_limit_bytes=TAIL_LIMIT),
    )(places, counts, rhs)


def local(rhs, counts, solve_panel, dirichlet_panel, coupling, corner_map, coarse_inverse):
    subs, loads, width = rhs.shape[1:]
    corners = coupling.shape[2]
    solve, dirichlet, couple = solve_panel[0], dirichlet_panel[0], coupling[0]
    place, size = lax.axis_index("sub"), lax.axis_size("sub")
    places = jnp.stack([1 - place % 2, lax.axis_index("grp"), place == size - 1]).astype(jnp.int32)

    face_shape, own_shape = (loads, width), (subs, loads, width)
    first_shape, rest_shape = (loads, 2 * width), (subs - 1, loads, 2 * width)
    edges_shapes = [face_shape, own_shape]
    result_shapes = [first_shape, rest_shape, face_shape, face_shape]

    tail = make_tail(places, counts, rhs)
    tail, places, corner_map = lax.optimization_barrier((tail, places, corner_map))
    head = lax.ppermute(tail, "sub", [(i, i + 1) for i in range(size - 1)])
    everyone = from_group(corner_map.reshape(1, subs * corners))
    live_own, residual_own, partial, rest = call(
        early_kernel,
        [(subs, 1, width), own_shape, first_shape, rest_shape],
        places, counts, rhs, dirichlet, scalars=2,
    )
    group = everyone.shape[0]
    (picked,) = call(
        pick_kernel, [(group, subs * corners, group * subs * corners)],
        places, everyone, coarse_inverse[0],
    )
    head, picked, rest = lax.optimization_barrier((head, picked, rest))
    live_edge, residual_edge, first, near, far = call(
        head_kernel,
        [(1, width), face_shape, first_shape, face_shape, face_shape],
        places, head, partial, rest, dirichlet,
    )
    first, couple = lax.optimization_barrier((first, couple))
    block = jnp.concatenate(split_outside(swap_blocks(picked)), axis=0)
    high, low = split_outside(couple)
    stacked = jnp.concatenate([high, low], axis=1)
    slots = jnp.arange(subs, dtype=jnp.int32)
    own = (slots[:, None] == slots[None, :])[:, :, None, None]

    def placed(part):
        wide = jnp.where(own, part[:, None], jnp.zeros((), part.dtype))
        return wide.reshape(subs, subs * corners, 2 * width)

    lift = jnp.concatenate([placed(high), placed(high), placed(low)], axis=1)

    scalars, preconds = [jnp.zeros((2, loads), jnp.float32)], []
    image = residual = (residual_edge, residual_own)
    live = (live_edge, live_own)
    for step in range(ITERS):
        near, far = swap(near, far)
        edge, own, values = call(
            corner_kernel,
            edges_shapes + [(subs * corners, loads)],
            places, first, rest, near, far, *live, stacked,
        )
        preconds.append(own)
        everyone = lax.all_gather(values, "grp", tiled=True)
        first, rest, near, far, sums = call(
            dual_kernel,
            result_shapes + [(2, loads)],
            places, edge, own, residual[1], solve, everyone, block, lift,
        )
        sums = from_all(sums)
        if step + 1 < ITERS:
            near, far = swap(near, far)
            *new, first, rest, near, far, now = call(
                functools.partial(update_kernel, step),
                edges_shapes + edges_shapes + result_shapes + [(2, loads)],
                places, first, rest, near, far, *live, sums, scalars[-1],
                *image, *residual, dirichlet,
            )
            image, residual = new[:2], new[2:]
            scalars.append(now)
    following = lax.ppermute(first[:, :width], "sub", [(i + 1, i) for i in range(size - 1)])
    multipliers, residual = call(
        functools.partial(last_kernel, ITERS - 1),
        [own_shape] * 2,
        places, first, rest, following, live[1], sums, scalars[-1], scalars[-2],
        image[1], residual[1], *preconds,
    )
    return (multipliers[None], residual[None])


def solution(mesh):
    return jax.shard_map(
        local,
        mesh=mesh,
        in_specs=(
            P("grp", "sub", None, None),
            P("grp", "sub"),
            P("grp", "sub", None, None),
            P("grp", "sub", None, None),
            P("grp", "sub", None, None),
            P("grp", "sub", None),
            P("sub", "grp", None),
        ),
        out_specs=(P("grp", "sub", None, None), P("grp", "sub", None, None)),
        check_vma=False,
    )
```

```python
import functools

import jax
import jax.numpy as jnp
from jax import lax
from jax.experimental import pallas as pl
from jax.experimental.pallas import tpu as pltpu
from jax.sharding import PartitionSpec as P

ITERS = 3


VMEM_LIMIT = 8 * 1024 * 1024
TAIL_LIMIT = 62 * 1024 * 1024


def split(values):
    high = values.astype(jnp.bfloat16)
    return high, (values - high.astype(jnp.float32)).astype(jnp.bfloat16)


def split_outside(values):
    high = lax.reduce_precision(values, exponent_bits=8, mantissa_bits=7)
    return high.astype(jnp.bfloat16), (values - high).astype(jnp.bfloat16)


def mul(first, second):
    return jnp.dot(first, second, preferred_element_type=jnp.float32)


def mul_rows(first, second):
    dims = (((1,), (1,)), ((), ()))
    return lax.dot_general(first, second, dims, preferred_element_type=jnp.float32)


def call(kernel, out_shapes, *operands):
    return pl.pallas_call(
        kernel,
        out_shape=[jax.ShapeDtypeStruct(shape, jnp.float32) for shape in out_shapes],
        in_specs=[pl.BlockSpec(memory_space=pltpu.VMEM)] * len(operands),
        out_specs=[pl.BlockSpec(memory_space=pltpu.VMEM)] * len(out_shapes),
        compiler_params=pltpu.CompilerParams(vmem_limit_bytes=VMEM_LIMIT),
    )(*operands)


class Joined:
    def __init__(self, first, rest):
        self.first, self.rest = first, rest

    def __getitem__(self, place):
        return self.first[...] if place == 0 else self.rest[place - 1]

    def __setitem__(self, place, value):
        if place == 0:
            self.first[...] = value
        else:
            self.rest[place - 1] = value


def jump_edge(even, result, near, far, live, edge, subs):
    width = near.shape[1]
    if edge == 0:
        right = jnp.where(even, far[...], near[...])
    else:
        right = result[edge - 1][:, width:]
    if edge == subs:
        left = jnp.where(even, near[...], far[...])
    else:
        left = result[edge][:, :width]
    return live[edge] * (right - left)


def send_faces(even, first, last, near_out, far_out):
    width = first.shape[1] // 2
    to_next, to_prev = last[:, width:], first[:, :width]
    near_out[...] = jnp.where(even, to_next, to_prev)
    far_out[...] = jnp.where(even, to_prev, to_next)


def panel_products(parts, panel, result, extra=None):
    subs = panel.shape[0]
    for sub in range(subs):
        high = jnp.concatenate([-parts[sub][0], parts[sub + 1][0]], axis=1)
        low = jnp.concatenate([-parts[sub][1], parts[sub + 1][1]], axis=1)
        total = mul(high, panel[sub]) + mul(low, panel[sub])
        if extra is not None:
            total = total + extra(sub)
        result[sub] = total


def column(row, width):
    lanes = jnp.broadcast_to(row, (128, row.shape[1])).T
    return jnp.concatenate([lanes] * (width // 128), axis=1)


def row_sums(values):
    ones = jnp.ones((8, values.shape[1]), jnp.bfloat16)
    high, rest = split(values)
    middle, low = split(values - high.astype(jnp.float32))
    return (mul_rows(ones, high) + mul_rows(ones, middle) + mul_rows(ones, low))[:1]


def step_scalars(step, sums, before):
    totals = jnp.sum(sums[...], axis=0)
    rz_now, curvature = totals[:1], totals[1:2]
    if step == 0:
        return rz_now, rz_now / curvature, None
    beta = rz_now / before[0:1]
    return rz_now, rz_now / (curvature - beta * rz_now / before[1:2]), beta


def even_place():
    return lax.rem(lax.axis_index("sub"), 2) == 0


def live_rows(counts, sub, rows, width):
    last = lax.axis_index("sub") == lax.axis_size("sub") - 1
    count = jnp.broadcast_to(counts[:, sub : sub + 1], (rows, width))
    if sub == counts.shape[1] - 1:
        count = jnp.where(last, 0, count)
    return (lax.broadcasted_iota(jnp.int32, (rows, width), 1) < count).astype(jnp.float32)


def tail_kernel(counts_ref, rhs, tail, counts, face, counts_done, face_done):
    loads, width = rhs.shape[2:]
    counts_copy = pltpu.make_async_copy(counts_ref, counts, counts_done)
    face_copy = pltpu.make_async_copy(rhs.at[0, rhs.shape[1] - 1], face, face_done)
    counts_copy.start()
    face_copy.start()
    counts_copy.wait()
    mask = live_rows(counts, counts.shape[1] - 1, 8, width)
    tail[loads:] = mask
    face_copy.wait()
    tail[:loads] = mask[:1] * face[...]


def early_kernel(counts, rhs, panel, live, own, partial, rest):
    subs, loads, width = own.shape
    parts = [None]
    for sub in range(subs):
        mask = live_rows(counts, sub, 1, width)
        live[sub] = mask
        own[sub] = mask * rhs[sub]
        parts.append(split(own[sub]))
    partial[...] = mul(parts[1][0], panel[0, width:]) + mul(parts[1][1], panel[0, width:])
    for sub in range(1, subs):
        high = jnp.concatenate([-parts[sub][0], parts[sub + 1][0]], axis=1)
        low = jnp.concatenate([-parts[sub][1], parts[sub + 1][1]], axis=1)
        rest[sub - 1] = mul(high, panel[sub]) + mul(low, panel[sub])


def head_kernel(head, partial, rest, panel, live, edge, first, near_out, far_out):
    loads, width = edge.shape
    live[...] = head[loads : loads + 1]
    edge[...] = head[:loads]
    high, low = split(head[:loads])
    first[...] = partial[...] - mul(high, panel[0, :width]) - mul(low, panel[0, :width])
    last = rest[rest.shape[0] - 1]
    send_faces(even_place(), first[...], last, near_out, far_out)


def pick_kernel(everyone, coarse, picked):
    group, own = everyone.shape[0], everyone.shape[2]
    rows, size = coarse.shape
    grp = lax.axis_index("grp")
    high, low = split(coarse[...])
    unknowns = lax.broadcasted_iota(jnp.int32, (size, own), 0)
    columns = []
    for member in range(group):
        chosen = (unknowns == everyone[grp ^ member]).astype(jnp.bfloat16)
        columns.append(mul(high, chosen) + mul(low, chosen))
    high, low = split(jnp.concatenate(columns, axis=1))
    owned = lax.broadcasted_iota(jnp.int32, (rows, own), 0) + grp * rows
    dims = (((0,), (0,)), ((), ()))
    for distance in range(group):
        chosen = (owned == everyone[distance]).astype(jnp.bfloat16)
        picked[distance] = lax.dot_general(
            chosen, high, dims, preferred_element_type=jnp.float32
        ) + lax.dot_general(chosen, low, dims, preferred_element_type=jnp.float32)


def corner_kernel(first, rest, near, far, live_first, live_rest, coupling,
                  edge, own, corners):
    even = even_place()
    subs, rows = coupling.shape[0], coupling.shape[1] // 2
    result, live, edges = Joined(first, rest), Joined(live_first, live_rest), Joined(edge, own)
    parts = []
    for place in range(subs + 1):
        edges[place] = 0.25 * jump_edge(even, result, near, far, live, place, subs)
        parts.append(split(edges[place]))
    for sub in range(subs):
        high = jnp.concatenate([-parts[sub][0], parts[sub + 1][0]], axis=1)
        low = jnp.concatenate([-parts[sub][1], parts[sub + 1][1]], axis=1)
        both = mul_rows(coupling[sub], high)
        corners[sub * rows : (sub + 1) * rows, :] = (
            both[:rows] + both[rows:] + mul_rows(coupling[sub, :rows], low)
        )


def dual_kernel(edge, own, residual, panel, everyone, block, lift,
                first, rest, near_out, far_out, sums):
    even = even_place()
    subs, width = panel.shape[0], edge.shape[1]
    edges, result = Joined(edge, own), Joined(first, rest)
    rows = block.shape[0] // 2
    high, low = split(everyone[...])
    both = mul(block[...], high)
    back = (both[:rows] + both[rows:] + mul(block[:rows], low)).T
    back_high, back_low = split(back)
    lifted = jnp.concatenate([back_high, back_low, back_high], axis=1)
    parts = [split(edges[place]) for place in range(subs + 1)]
    panel_products(parts, panel, result, lambda sub: mul(lifted, lift[sub]))
    send_faces(even, result[0], result[subs - 1], near_out, far_out)
    product = curvature = 0.0
    for sub in range(subs):
        product = product + residual[sub] * edges[sub + 1]
        curvature = curvature + (
            result[sub][:, width:] * edges[sub + 1] - result[sub][:, :width] * edges[sub]
        )
    sums[...] = jnp.concatenate([row_sums(product), row_sums(curvature)], axis=0)


def update_kernel(step, first, rest, near, far, live_first, live_rest, sums, before,
                  old_edge, old_own, residual_edge, residual_own, panel,
                  image_edge, image_own, new_edge, new_own,
                  first_new, rest_new, near_out, far_out, scalars):
    even = even_place()
    subs, width = panel.shape[0], near.shape[1]
    result, live = Joined(first, rest), Joined(live_first, live_rest)
    image_old, residual = Joined(old_edge, old_own), Joined(residual_edge, residual_own)
    image, residual_new = Joined(image_edge, image_own), Joined(new_edge, new_own)
    result_new = Joined(first_new, rest_new)
    rz_now, alpha, beta = step_scalars(step, sums, before)
    scalars[...] = jnp.concatenate([rz_now, alpha], axis=0)
    alpha_column = column(alpha, width)
    beta_column = None if beta is None else column(beta, width)
    parts = []
    for place in range(subs + 1):
        value = jump_edge(even, result, near, far, live, place, subs)
        if beta is not None:
            value = value + beta_column * image_old[place]
        image[place] = value
        residual_new[place] = residual[place] - alpha_column * value
        parts.append(split(residual_new[place]))
    panel_products(parts, panel, result_new)
    send_faces(even, result_new[0], result_new[subs - 1], near_out, far_out)


def last_kernel(step, first, rest, following, live, sums, before, older, image_old,
                residual, first_z, second_z, third_z, multipliers, residual_new):
    subs, width = residual.shape[0], following.shape[1]
    result = Joined(first, rest)
    rz_now, alpha, beta = step_scalars(step, sums, before)
    beta_before = before[0:1] / older[0:1]
    on_second = before[1:2] + alpha * beta
    on_first = older[1:2] + on_second * beta_before
    alpha_column, beta_column = column(alpha, width), column(beta, width)
    second_column, first_column = column(on_second, width), column(on_first, width)
    for sub in range(subs):
        left = following[...] if sub == subs - 1 else result[sub + 1][:, :width]
        image = live[sub] * (result[sub][:, width:] - left) + beta_column * image_old[sub]
        residual_new[sub] = residual[sub] - alpha_column * image
        multipliers[sub] = (
            first_column * first_z[sub]
            + second_column * second_z[sub]
            + alpha_column * third_z[sub]
        )


def neighbour_pairs(size, first):
    pairs = [(i, i + 1) for i in range(first, size - 1, 2)]
    return [route for a, b in pairs for route in ((a, b), (b, a))]


def swap(near, far):
    size = lax.axis_size("sub")
    return (
        lax.ppermute(near, "sub", neighbour_pairs(size, 0)),
        lax.ppermute(far, "sub", neighbour_pairs(size, 1)),
    )


def from_all(rows):
    size = lax.axis_size("sub") * lax.axis_size("grp")
    copies = jnp.broadcast_to(rows[None], (size,) + rows.shape)
    return lax.all_to_all(copies, ("sub", "grp"), 0, 0)


def from_group(values):
    group = lax.axis_size("grp")
    received = [values]
    for distance in range(1, group):
        routes = [(i, i ^ distance) for i in range(group)]
        received.append(lax.ppermute(values, "grp", routes))
    return jnp.stack(received)


def swap_blocks(picked):
    group = lax.axis_size("grp")
    block = picked[0]
    for distance in range(1, group):
        routes = [(i, i ^ distance) for i in range(group)]
        block = block + lax.ppermute(picked[distance], "grp", routes)
    return block


def make_tail(counts, rhs):
    loads, width = rhs.shape[2:]
    return pl.pallas_call(
        tail_kernel,
        out_shape=jax.ShapeDtypeStruct((loads + 8, width), jnp.float32),
        in_specs=[
            pl.BlockSpec(memory_space=pltpu.HBM),
            pl.BlockSpec(memory_space=pltpu.HBM),
        ],
        out_specs=pl.BlockSpec(memory_space=pltpu.VMEM),
        scratch_shapes=[
            pltpu.VMEM(counts.shape, counts.dtype),
            pltpu.VMEM((loads, width), jnp.float32),
            pltpu.SemaphoreType.DMA,
            pltpu.SemaphoreType.DMA,
        ],
        compiler_params=pltpu.CompilerParams(vmem_limit_bytes=TAIL_LIMIT),
    )(counts, rhs)


def local(rhs, counts, solve_panel, dirichlet_panel, coupling, corner_map, coarse_inverse):
    subs, loads, width = rhs.shape[1:]
    corners = coupling.shape[2]
    solve, dirichlet, couple = solve_panel[0], dirichlet_panel[0], coupling[0]
    size = lax.axis_size("sub")

    face_shape, own_shape = (loads, width), (subs, loads, width)
    first_shape, rest_shape = (loads, 2 * width), (subs - 1, loads, 2 * width)
    edges_shapes = [face_shape, own_shape]
    result_shapes = [first_shape, rest_shape, face_shape, face_shape]

    tail = make_tail(counts, rhs)
    tail, counts, corner_map = lax.optimization_barrier((tail, counts, corner_map))
    head = lax.ppermute(tail, "sub", [(i, i + 1) for i in range(size - 1)])
    everyone = from_group(corner_map.reshape(1, subs * corners))
    live_own, residual_own, partial, rest = call(
        early_kernel,
        [(subs, 1, width), own_shape, first_shape, rest_shape],
        counts, rhs[0], dirichlet,
    )
    group = everyone.shape[0]
    (picked,) = call(
        pick_kernel, [(group, subs * corners, group * subs * corners)],
        everyone, coarse_inverse[0],
    )
    head, picked, rest = lax.optimization_barrier((head, picked, rest))
    live_edge, residual_edge, first, near, far = call(
        head_kernel,
        [(1, width), face_shape, first_shape, face_shape, face_shape],
        head, partial, rest, dirichlet,
    )
    first, couple = lax.optimization_barrier((first, couple))
    block = jnp.concatenate(split_outside(swap_blocks(picked)), axis=0)
    high, low = split_outside(couple)
    stacked = jnp.concatenate([high, low], axis=1)
    slots = jnp.arange(subs, dtype=jnp.int32)
    own = (slots[:, None] == slots[None, :])[:, :, None, None]

    def placed(part):
        wide = jnp.where(own, part[:, None], jnp.zeros((), part.dtype))
        return wide.reshape(subs, subs * corners, 2 * width)

    lift = jnp.concatenate([placed(high), placed(high), placed(low)], axis=1)

    scalars, preconds = [jnp.zeros((2, loads), jnp.float32)], []
    image = residual = (residual_edge, residual_own)
    live = (live_edge, live_own)
    for step in range(ITERS):
        near, far = swap(near, far)
        edge, own, values = call(
            corner_kernel,
            edges_shapes + [(subs * corners, loads)],
            first, rest, near, far, *live, stacked,
        )
        preconds.append(own)
        everyone = lax.all_gather(values, "grp", tiled=True)
        first, rest, near, far, sums = call(
            dual_kernel,
            result_shapes + [(2, loads)],
            edge, own, residual[1], solve, everyone, block, lift,
        )
        sums = from_all(sums)
        if step + 1 < ITERS:
            near, far = swap(near, far)
            *new, first, rest, near, far, now = call(
                functools.partial(update_kernel, step),
                edges_shapes + edges_shapes + result_shapes + [(2, loads)],
                first, rest, near, far, *live, sums, scalars[-1],
                *image, *residual, dirichlet,
            )
            image, residual = new[:2], new[2:]
            scalars.append(now)
    following = lax.ppermute(first[:, :width], "sub", [(i + 1, i) for i in range(size - 1)])
    multipliers, residual = call(
        functools.partial(last_kernel, ITERS - 1),
        [own_shape] * 2,
        first, rest, following, live[1], sums, scalars[-1], scalars[-2],
        image[1], residual[1], *preconds,
    )
    return (multipliers[None], residual[None])


def solution(mesh):
    return jax.shard_map(
        local,
        mesh=mesh,
        in_specs=(
            P("grp", "sub", None, None),
            P("grp", "sub"),
            P("grp", "sub", None, None),
            P("grp", "sub", None, None),
            P("grp", "sub", None, None),
            P("grp", "sub", None),
            P("sub", "grp", None),
        ),
        out_specs=(P("grp", "sub", None, None), P("grp", "sub", None, None)),
        check_vma=False,
    )
```

```python
import functools

import jax
import jax.numpy as jnp
from jax import lax
from jax.experimental import pallas as pl
from jax.experimental.pallas import tpu as pltpu
from jax.sharding import PartitionSpec as P

ITERS = 3


VMEM_LIMIT = 8 * 1024 * 1024
TAIL_LIMIT = 62 * 1024 * 1024


def split(values):
    high = values.astype(jnp.bfloat16)
    return high, (values - high.astype(jnp.float32)).astype(jnp.bfloat16)


def split_outside(values):
    high = lax.reduce_precision(values, exponent_bits=8, mantissa_bits=7)
    return high.astype(jnp.bfloat16), (values - high).astype(jnp.bfloat16)


def mul(first, second):
    return jnp.dot(first, second, preferred_element_type=jnp.float32)


def mul_rows(first, second):
    dims = (((1,), (1,)), ((), ()))
    return lax.dot_general(first, second, dims, preferred_element_type=jnp.float32)


def call(kernel, out_shapes, *operands, kinds=None, scratch=()):
    kinds = kinds or [jnp.float32] * len(out_shapes)
    return pl.pallas_call(
        kernel,
        out_shape=[jax.ShapeDtypeStruct(*shape) for shape in zip(out_shapes, kinds)],
        in_specs=[pl.BlockSpec(memory_space=pltpu.VMEM)] * len(operands),
        out_specs=[pl.BlockSpec(memory_space=pltpu.VMEM)] * len(out_shapes),
        scratch_shapes=list(scratch),
        compiler_params=pltpu.CompilerParams(vmem_limit_bytes=VMEM_LIMIT),
    )(*operands)


class Joined:
    def __init__(self, first, rest):
        self.first, self.rest = first, rest

    def __getitem__(self, place):
        return self.first[...] if place == 0 else self.rest[place - 1]

    def __setitem__(self, place, value):
        if place == 0:
            self.first[...] = value
        else:
            self.rest[place - 1] = value


def jump_edge(even, result, near, far, live, edge, subs):
    width = near.shape[1]
    if edge == 0:
        right = jnp.where(even, far[...], near[...])
    else:
        right = result[edge - 1][:, width:]
    if edge == subs:
        left = jnp.where(even, near[...], far[...])
    else:
        left = result[edge][:, :width]
    return live[edge] * (right - left)


def send_faces(even, first, last, near_out, far_out):
    width = first.shape[1] // 2
    to_next, to_prev = last[:, width:], first[:, :width]
    near_out[...] = jnp.where(even, to_next, to_prev)
    far_out[...] = jnp.where(even, to_prev, to_next)


def panel_products(parts, panel, result, extra=None):
    subs = panel.shape[0]
    for sub in range(subs):
        high = jnp.concatenate([-parts[sub][0], parts[sub + 1][0]], axis=1)
        low = jnp.concatenate([-parts[sub][1], parts[sub + 1][1]], axis=1)
        total = mul(high, panel[sub]) + mul(low, panel[sub])
        if extra is not None:
            total = total + extra(sub)
        result[sub] = total


def column(row, width):
    lanes = jnp.broadcast_to(row, (128, row.shape[1])).T
    return jnp.concatenate([lanes] * (width // 128), axis=1)


def row_sums(values):
    half = values.shape[1] // 2
    return jnp.sum((values[:, :half] + values[:, half:]).T, axis=0, keepdims=True)


def step_scalars(step, sums, before):
    totals = jnp.sum(sums[...], axis=0)
    rz_now, curvature = totals[:1], totals[1:2]
    if step == 0:
        return rz_now, rz_now / curvature, None
    beta = rz_now / before[0:1]
    return rz_now, rz_now / (curvature - beta * rz_now / before[1:2]), beta


def even_place():
    return lax.rem(lax.axis_index("sub"), 2) == 0


def live_rows(counts, sub, rows, width):
    last = lax.axis_index("sub") == lax.axis_size("sub") - 1
    count = jnp.broadcast_to(counts[:, sub : sub + 1], (rows, width))
    if sub == counts.shape[1] - 1:
        count = jnp.where(last, 0, count)
    return (lax.broadcasted_iota(jnp.int32, (rows, width), 1) < count).astype(jnp.float32)


def tail_kernel(counts_ref, rhs, tail, counts, face, counts_done, face_done):
    loads, width = rhs.shape[2:]
    counts_copy = pltpu.make_async_copy(counts_ref, counts, counts_done)
    face_copy = pltpu.make_async_copy(rhs.at[0, rhs.shape[1] - 1], face, face_done)
    counts_copy.start()
    face_copy.start()
    counts_copy.wait()
    mask = live_rows(counts, counts.shape[1] - 1, 8, width)
    tail[loads:] = mask
    face_copy.wait()
    tail[:loads] = mask[:1] * face[...]


def early_kernel(counts, rhs, panel, live, own, partial, rest):
    subs, loads, width = own.shape
    parts = [None]
    for sub in range(subs):
        mask = live_rows(counts, sub, 1, width)
        live[sub] = mask
        own[sub] = mask * rhs[sub]
        parts.append(split(own[sub]))
    partial[...] = mul(parts[1][0], panel[0, width:]) + mul(parts[1][1], panel[0, width:])
    for sub in range(1, subs):
        high = jnp.concatenate([-parts[sub][0], parts[sub + 1][0]], axis=1)
        low = jnp.concatenate([-parts[sub][1], parts[sub + 1][1]], axis=1)
        rest[sub - 1] = mul(high, panel[sub]) + mul(low, panel[sub])


def head_kernel(head, partial, rest, panel, live, edge, first, near_out, far_out):
    loads, width = edge.shape
    live[...] = head[loads : loads + 1]
    edge[...] = head[:loads]
    high, low = split(head[:loads])
    first[...] = partial[...] - mul(high, panel[0, :width]) - mul(low, panel[0, :width])
    last = rest[rest.shape[0] - 1]
    send_faces(even_place(), first[...], last, near_out, far_out)


def setup_kernel(*refs):
    group = (len(refs) - 5) // 2
    maps, (coarse, coupling) = refs[:group], refs[group : group + 2]
    picked, (stacked, lift, everyone) = refs[group + 2 : -3], refs[-3:]
    subs, corners = maps[0].shape
    rows, size = coarse.shape
    own = subs * corners
    grp = lax.axis_index("grp")
    for sub in range(subs):
        high, low = split(coupling[sub])
        spare = jnp.zeros((lift.shape[1] - 3 * corners, high.shape[1]), jnp.bfloat16)
        stacked[sub] = jnp.concatenate([high, low], axis=0)
        lift[sub] = jnp.concatenate([high, high, low, spare], axis=0)
    for distance in range(group):
        unknowns = [maps[distance][sub : sub + 1, :] for sub in range(subs)]
        everyone[distance] = jnp.concatenate(unknowns, axis=1)
    high, low = split(coarse[...])
    unknowns = lax.broadcasted_iota(jnp.int32, (size, own), 0)
    columns = []
    for member in range(group):
        chosen = (unknowns == everyone[grp ^ member]).astype(jnp.bfloat16)
        columns.append(mul(high, chosen) + mul(low, chosen))
    high, low = split(jnp.concatenate(columns, axis=1))
    owned = lax.broadcasted_iota(jnp.int32, (rows, own), 0) + grp * rows
    dims = (((0,), (0,)), ((), ()))
    for distance in range(group):
        chosen = (owned == everyone[distance]).astype(jnp.bfloat16)
        picked[distance][...] = lax.dot_general(
            chosen, high, dims, preferred_element_type=jnp.float32
        ) + lax.dot_general(chosen, low, dims, preferred_element_type=jnp.float32)


def corner_kernel(first, rest, near, far, live_first, live_rest, coupling,
                  edge, own, corners):
    even = even_place()
    subs, rows = coupling.shape[0], coupling.shape[1] // 2
    result, live, edges = Joined(first, rest), Joined(live_first, live_rest), Joined(edge, own)
    parts = []
    for place in range(subs + 1):
        edges[place] = 0.25 * jump_edge(even, result, near, far, live, place, subs)
        parts.append(split(edges[place]))
    for sub in range(subs):
        high = jnp.concatenate([-parts[sub][0], parts[sub + 1][0]], axis=1)
        low = jnp.concatenate([-parts[sub][1], parts[sub + 1][1]], axis=1)
        both = mul_rows(coupling[sub], high)
        corners[sub * rows : (sub + 1) * rows, :] = (
            both[:rows] + both[rows:] + mul_rows(coupling[sub, :rows], low)
        )


def dual_kernel(edge, own, residual, panel, everyone, block, lift,
                first, rest, near_out, far_out, sums):
    even = even_place()
    subs, width = panel.shape[0], edge.shape[1]
    edges, result = Joined(edge, own), Joined(first, rest)
    rows = block.shape[0] // 2
    high, low = split(everyone[...])
    both = mul(block[...], high)
    back = both[:rows] + both[rows:] + mul(block[:rows], low)
    corners = rows // subs

    def lifted(sub):
        own = back[sub * corners : (sub + 1) * corners]
        own_high = own.astype(jnp.bfloat16).astype(jnp.float32)
        terms = [own_high, own - own_high, own_high]
        spare = jnp.zeros((lift.shape[1] - 3 * corners, own.shape[1]), jnp.float32)
        return mul(jnp.concatenate(terms + [spare], axis=0).T.astype(jnp.bfloat16), lift[sub])

    parts = [split(edges[place]) for place in range(subs + 1)]
    panel_products(parts, panel, result, lifted)
    send_faces(even, result[0], result[subs - 1], near_out, far_out)
    product = curvature = 0.0
    for sub in range(subs):
        product = product + residual[sub] * edges[sub + 1]
        curvature = curvature + (
            result[sub][:, width:] * edges[sub + 1] - result[sub][:, :width] * edges[sub]
        )
    sums[...] = jnp.concatenate([row_sums(product), row_sums(curvature)], axis=0)


def update_kernel(step, first, rest, near, far, live_first, live_rest, sums, before,
                  old_edge, old_own, residual_edge, residual_own, panel,
                  image_edge, image_own, new_edge, new_own,
                  first_new, rest_new, near_out, far_out, scalars):
    even = even_place()
    subs, width = panel.shape[0], near.shape[1]
    result, live = Joined(first, rest), Joined(live_first, live_rest)
    image_old, residual = Joined(old_edge, old_own), Joined(residual_edge, residual_own)
    image, residual_new = Joined(image_edge, image_own), Joined(new_edge, new_own)
    result_new = Joined(first_new, rest_new)
    rz_now, alpha, beta = step_scalars(step, sums, before)
    scalars[...] = jnp.concatenate([rz_now, alpha], axis=0)
    alpha_column = column(alpha, width)
    beta_column = None if beta is None else column(beta, width)
    parts = []
    for place in range(subs + 1):
        value = jump_edge(even, result, near, far, live, place, subs)
        if beta is not None:
            value = value + beta_column * image_old[place]
        image[place] = value
        residual_new[place] = residual[place] - alpha_column * value
        parts.append(split(residual_new[place]))
    panel_products(parts, panel, result_new)
    send_faces(even, result_new[0], result_new[subs - 1], near_out, far_out)


def last_kernel(step, first, rest, following, live, sums, before, older, image_old,
                residual, first_z, second_z, third_z, multipliers, residual_new):
    subs, width = residual.shape[0], following.shape[1]
    result = Joined(first, rest)
    rz_now, alpha, beta = step_scalars(step, sums, before)
    beta_before = before[0:1] / older[0:1]
    on_second = before[1:2] + alpha * beta
    on_first = older[1:2] + on_second * beta_before
    alpha_column, beta_column = column(alpha, width), column(beta, width)
    second_column, first_column = column(on_second, width), column(on_first, width)
    for sub in range(subs):
        left = following[...] if sub == subs - 1 else result[sub + 1][:, :width]
        image = live[sub] * (result[sub][:, width:] - left) + beta_column * image_old[sub]
        residual_new[sub] = residual[sub] - alpha_column * image
        multipliers[sub] = (
            first_column * first_z[sub]
            + second_column * second_z[sub]
            + alpha_column * third_z[sub]
        )


def neighbour_pairs(size, first):
    pairs = [(i, i + 1) for i in range(first, size - 1, 2)]
    return [route for a, b in pairs for route in ((a, b), (b, a))]


def swap(near, far):
    size = lax.axis_size("sub")
    return (
        lax.ppermute(near, "sub", neighbour_pairs(size, 0)),
        lax.ppermute(far, "sub", neighbour_pairs(size, 1)),
    )


def from_all(rows):
    size = lax.axis_size("sub") * lax.axis_size("grp")
    copies = jnp.broadcast_to(rows[None], (size,) + rows.shape)
    return lax.all_to_all(copies, ("sub", "grp"), 0, 0)


def from_group(values):
    group = lax.axis_size("grp")
    received = [values]
    for distance in range(1, group):
        routes = [(i, i ^ distance) for i in range(group)]
        received.append(lax.ppermute(values, "grp", routes))
    return received


def swap_blocks(picked):
    group = lax.axis_size("grp")
    block = picked[0]
    for distance in range(1, group):
        routes = [(i, i ^ distance) for i in range(group)]
        block = block + lax.ppermute(picked[distance], "grp", routes)
    return block


def make_tail(counts, rhs):
    loads, width = rhs.shape[2:]
    return pl.pallas_call(
        tail_kernel,
        out_shape=jax.ShapeDtypeStruct((loads + 8, width), jnp.float32),
        in_specs=[
            pl.BlockSpec(memory_space=pltpu.HBM),
            pl.BlockSpec(memory_space=pltpu.HBM),
        ],
        out_specs=pl.BlockSpec(memory_space=pltpu.VMEM),
        scratch_shapes=[
            pltpu.VMEM(counts.shape, counts.dtype),
            pltpu.VMEM((loads, width), jnp.float32),
            pltpu.SemaphoreType.DMA,
            pltpu.SemaphoreType.DMA,
        ],
        compiler_params=pltpu.CompilerParams(vmem_limit_bytes=TAIL_LIMIT),
    )(counts, rhs)


def local(rhs, counts, solve_panel, dirichlet_panel, coupling, corner_map, coarse_inverse):
    subs, loads, width = rhs.shape[1:]
    corners = coupling.shape[2]
    solve, dirichlet = solve_panel[0], dirichlet_panel[0]
    size = lax.axis_size("sub")

    face_shape, own_shape = (loads, width), (subs, loads, width)
    first_shape, rest_shape = (loads, 2 * width), (subs - 1, loads, 2 * width)
    edges_shapes = [face_shape, own_shape]
    result_shapes = [first_shape, rest_shape, face_shape, face_shape]

    tail = make_tail(counts, rhs)
    tail, counts, corner_map = lax.optimization_barrier((tail, counts, corner_map))
    head = lax.ppermute(tail, "sub", [(i, i + 1) for i in range(size - 1)])
    maps = from_group(corner_map[0])
    live_own, residual_own, partial, rest = call(
        early_kernel,
        [(subs, 1, width), own_shape, first_shape, rest_shape],
        counts, rhs[0], dirichlet,
    )
    group, own = len(maps), subs * corners
    *picked, stacked, lift = call(
        setup_kernel,
        [(own, group * own)] * group
        + [(subs, 2 * corners, 2 * width), (subs, 3 * corners + -3 * corners % 128, 2 * width)],
        *maps, coarse_inverse[0], coupling[0],
        kinds=[jnp.float32] * group + [jnp.bfloat16] * 2,
        scratch=[pltpu.VMEM((group, 1, own), jnp.int32)],
    )
    head, picked, rest = lax.optimization_barrier((head, picked, rest))
    live_edge, residual_edge, first, near, far = call(
        head_kernel,
        [(1, width), face_shape, first_shape, face_shape, face_shape],
        head, partial, rest, dirichlet,
    )
    block = jnp.concatenate(split_outside(swap_blocks(picked)), axis=0)

    scalars, preconds = [jnp.zeros((2, loads), jnp.float32)], []
    image = residual = (residual_edge, residual_own)
    live = (live_edge, live_own)
    for step in range(ITERS):
        near, far = swap(near, far)
        edge, own, values = call(
            corner_kernel,
            edges_shapes + [(subs * corners, loads)],
            first, rest, near, far, *live, stacked,
        )
        preconds.append(own)
        everyone = lax.all_gather(values, "grp", tiled=True)
        first, rest, near, far, sums = call(
            dual_kernel,
            result_shapes + [(2, loads)],
            edge, own, residual[1], solve, everyone, block, lift,
        )
        sums = from_all(sums)
        if step + 1 < ITERS:
            near, far = swap(near, far)
            *new, first, rest, near, far, now = call(
                functools.partial(update_kernel, step),
                edges_shapes + edges_shapes + result_shapes + [(2, loads)],
                first, rest, near, far, *live, sums, scalars[-1],
                *image, *residual, dirichlet,
            )
            image, residual = new[:2], new[2:]
            scalars.append(now)
    following = lax.ppermute(first[:, :width], "sub", [(i + 1, i) for i in range(size - 1)])
    multipliers, residual = call(
        functools.partial(last_kernel, ITERS - 1),
        [own_shape] * 2,
        first, rest, following, live[1], sums, scalars[-1], scalars[-2],
        image[1], residual[1], *preconds,
    )
    return (multipliers[None], residual[None])


def solution(mesh):
    return jax.shard_map(
        local,
        mesh=mesh,
        in_specs=(
            P("grp", "sub", None, None),
            P("grp", "sub"),
            P("grp", "sub", None, None),
            P("grp", "sub", None, None),
            P("grp", "sub", None, None),
            P("grp", "sub", None),
            P("sub", "grp", None),
        ),
        out_specs=(P("grp", "sub", None, None), P("grp", "sub", None, None)),
        check_vma=False,
    )
```

```python
import functools

import jax
import jax.numpy as jnp
from jax import lax
from jax.experimental import pallas as pl
from jax.experimental.pallas import tpu as pltpu
from jax.sharding import PartitionSpec as P

VMEM_LIMIT = 8 * 1024 * 1024
TAIL_LIMIT = 62 * 1024 * 1024


def split(values):
    high = values.astype(jnp.bfloat16)
    return high, (values - high.astype(jnp.float32)).astype(jnp.bfloat16)


def split_outside(values):
    high = lax.reduce_precision(values, exponent_bits=8, mantissa_bits=7)
    return high.astype(jnp.bfloat16), (values - high).astype(jnp.bfloat16)


def mul(first, second):
    return jnp.dot(first, second, preferred_element_type=jnp.float32)


def mul_rows(first, second):
    dims = (((1,), (1,)), ((), ()))
    return lax.dot_general(first, second, dims, preferred_element_type=jnp.float32)


def call(kernel, out_shapes, *operands, kinds=None, scratch=()):
    kinds = kinds or [jnp.float32] * len(out_shapes)
    return pl.pallas_call(
        kernel,
        out_shape=[jax.ShapeDtypeStruct(*shape) for shape in zip(out_shapes, kinds)],
        in_specs=[pl.BlockSpec(memory_space=pltpu.VMEM)] * len(operands),
        out_specs=[pl.BlockSpec(memory_space=pltpu.VMEM)] * len(out_shapes),
        scratch_shapes=list(scratch),
        compiler_params=pltpu.CompilerParams(vmem_limit_bytes=VMEM_LIMIT),
    )(*operands)


class Joined:
    def __init__(self, first, rest):
        self.first, self.rest = first, rest

    def __getitem__(self, place):
        return self.first[...] if place == 0 else self.rest[place - 1]

    def __setitem__(self, place, value):
        if place == 0:
            self.first[...] = value
        else:
            self.rest[place - 1] = value


def jump_edge(even, result, near, far, live, edge, subs):
    loads, width = result[0].shape[0], near.shape[1]
    if edge == 0:
        right = jnp.where(even, far[:loads], near[:loads])
    else:
        right = result[edge - 1][:, width:]
    if edge == subs:
        left = jnp.where(even, near[:loads], far[:loads])
    else:
        left = result[edge][:, :width]
    return live[edge] * (right - left)


def outer_rows(operator, edge):
    rows = operator.shape[0] // 2
    high, low = split(edge)
    both = mul_rows(operator[...], high)
    return both[:rows] + both[rows:] + mul_rows(operator[:rows], low)


def send(even, to_next, to_prev, near_out, far_out):
    near_out[...] = jnp.where(even, to_next, to_prev)
    far_out[...] = jnp.where(even, to_prev, to_next)


def send_faces(even, first, last, near_out, far_out):
    width = first.shape[1] // 2
    send(even, last[:, width:], first[:, :width], near_out, far_out)


def panel_products(parts, panel, result, extra=None):
    subs = panel.shape[0]
    for sub in range(subs):
        high = jnp.concatenate([-parts[sub][0], parts[sub + 1][0]], axis=1)
        low = jnp.concatenate([-parts[sub][1], parts[sub + 1][1]], axis=1)
        total = mul(high, panel[sub]) + mul(low, panel[sub])
        if extra is not None:
            total = total + extra(sub)
        result[sub] = total


def column(row, width):
    lanes = jnp.broadcast_to(row, (128, row.shape[1])).T
    return jnp.concatenate([lanes] * (width // 128), axis=1)


def row_sums(values):
    half = values.shape[1] // 2
    return jnp.sum((values[:, :half] + values[:, half:]).T, axis=0, keepdims=True)


def step_scalars(step, sums, before):
    totals = jnp.sum(sums[...], axis=0)
    rz_now, curvature = totals[:1], totals[1:2]
    if step == 0:
        return rz_now, rz_now / curvature, None
    beta = rz_now / before[0:1]
    return rz_now, rz_now / (curvature - beta * rz_now / before[1:2]), beta


def even_place():
    return lax.rem(lax.axis_index("sub"), 2) == 0


def live_rows(counts, sub, rows, width):
    last = lax.axis_index("sub") == lax.axis_size("sub") - 1
    count = jnp.broadcast_to(counts[:, sub : sub + 1], (rows, width))
    if sub == counts.shape[1] - 1:
        count = jnp.where(last, 0, count)
    return (lax.broadcasted_iota(jnp.int32, (rows, width), 1) < count).astype(jnp.float32)


def tail_kernel(counts_ref, rhs, tail, counts, face, counts_done, face_done):
    loads, width = rhs.shape[2:]
    counts_copy = pltpu.make_async_copy(counts_ref, counts, counts_done)
    face_copy = pltpu.make_async_copy(rhs.at[0, rhs.shape[1] - 1], face, face_done)
    counts_copy.start()
    face_copy.start()
    counts_copy.wait()
    mask = live_rows(counts, counts.shape[1] - 1, 8, width)
    tail[loads:] = mask
    face_copy.wait()
    tail[:loads] = mask[:1] * face[...]


def early_kernel(counts, rhs, panel, live, own, partial, rest):
    subs, loads, width = own.shape
    parts = [None]
    for sub in range(subs):
        mask = live_rows(counts, sub, 1, width)
        live[sub] = mask
        own[sub] = mask * rhs[sub]
        parts.append(split(own[sub]))
    partial[...] = mul(parts[1][0], panel[0, width:]) + mul(parts[1][1], panel[0, width:])
    for sub in range(1, subs):
        high = jnp.concatenate([-parts[sub][0], parts[sub + 1][0]], axis=1)
        low = jnp.concatenate([-parts[sub][1], parts[sub + 1][1]], axis=1)
        rest[sub - 1] = mul(high, panel[sub]) + mul(low, panel[sub])


def head_kernel(head, partial, rest, panel, live, edge, first, near_out, far_out):
    loads, width = edge.shape
    live[...] = head[loads : loads + 1]
    edge[...] = head[:loads]
    high, low = split(head[:loads])
    first[...] = partial[...] - mul(high, panel[0, :width]) - mul(low, panel[0, :width])
    last = rest[rest.shape[0] - 1]
    send_faces(even_place(), first[...], last, near_out, far_out)


def setup_kernel(*refs):
    group = (len(refs) - 7) // 2
    maps, (coarse, coupling) = refs[:group], refs[group : group + 2]
    picked, (stacked, lift, near_out, far_out, everyone) = refs[group + 2 : -5], refs[-5:]
    subs, corners = maps[0].shape
    rows, size = coarse.shape
    own = subs * corners
    grp = lax.axis_index("grp")
    for sub in range(subs):
        high, low = split(coupling[sub])
        spare = jnp.zeros((lift.shape[1] - 3 * corners, high.shape[1]), jnp.bfloat16)
        stacked[sub] = jnp.concatenate([high, low], axis=0)
        lift[sub] = jnp.concatenate([high, high, low, spare], axis=0)
    width = coupling.shape[2] // 2
    send(even_place(), coupling[subs - 1, :, width:], coupling[0, :, :width], near_out, far_out)
    for distance in range(group):
        unknowns = [maps[distance][sub : sub + 1, :] for sub in range(subs)]
        everyone[distance] = jnp.concatenate(unknowns, axis=1)
    high, low = split(coarse[...])
    unknowns = lax.broadcasted_iota(jnp.int32, (size, own), 0)
    columns = []
    for member in range(group):
        chosen = (unknowns == everyone[grp ^ member]).astype(jnp.bfloat16)
        columns.append(mul(high, chosen) + mul(low, chosen))
    high, low = split(jnp.concatenate(columns, axis=1))
    owned = lax.broadcasted_iota(jnp.int32, (rows, own), 0) + grp * rows
    dims = (((0,), (0,)), ((), ()))
    for distance in range(group):
        chosen = (owned == everyone[distance]).astype(jnp.bfloat16)
        picked[distance][...] = lax.dot_general(
            chosen, high, dims, preferred_element_type=jnp.float32
        ) + lax.dot_general(chosen, low, dims, preferred_element_type=jnp.float32)


def corner_kernel(first, rest, near, far, live_first, live_rest, coupling,
                  edge, own, corners):
    even = even_place()
    subs, rows = coupling.shape[0], coupling.shape[1] // 2
    result, live, edges = Joined(first, rest), Joined(live_first, live_rest), Joined(edge, own)
    parts = []
    for place in range(subs + 1):
        edges[place] = 0.25 * jump_edge(even, result, near, far, live, place, subs)
        parts.append(split(edges[place]))
    for sub in range(subs):
        high = jnp.concatenate([-parts[sub][0], parts[sub + 1][0]], axis=1)
        low = jnp.concatenate([-parts[sub][1], parts[sub + 1][1]], axis=1)
        both = mul_rows(coupling[sub], high)
        corners[sub * rows : (sub + 1) * rows, :] = (
            both[:rows] + both[rows:] + mul_rows(coupling[sub, :rows], low)
        )


def operators_kernel(coupling, live_edge, live_own, near, far, panel,
                     taken, ends, for_next, for_prev, given):
    even = even_place()
    subs, rows = coupling.shape[0], coupling.shape[1]
    width = coupling.shape[2] // 2
    live = Joined(live_edge, live_own)
    before = jnp.where(even, far[...], near[...])
    after = jnp.where(even, near[...], far[...])
    left = [coupling[sub, :, :width] * (0.25 * live[sub]) for sub in range(subs)]
    left.append(after * (0.25 * live[subs]))
    right = [before * (0.25 * live[0])]
    right += [coupling[sub, :, width:] * (0.25 * live[sub + 1]) for sub in range(subs)]
    none = jnp.zeros((rows, width), jnp.float32)
    inner, ahead, behind = [], [], []
    for sub in range(subs):
        factors = jnp.concatenate(
            [
                jnp.concatenate([left[sub], right[sub + 1]], axis=1),
                jnp.concatenate([none, left[sub + 1]], axis=1),
                jnp.concatenate([right[sub], none], axis=1),
            ],
            axis=0,
        )
        both = mul(jnp.concatenate(split(factors), axis=0), panel[sub])
        product = both[: 3 * rows] + both[3 * rows :]
        inner.append(product[:rows])
        ahead.append(product[rows : 2 * rows])
        behind.append(product[2 * rows :])
    total = subs * rows
    for sub in range(subs):
        blocks = [none] * (subs + 1)
        blocks[sub] = -inner[sub][:, :width]
        blocks[sub + 1] = inner[sub][:, width:]
        if sub > 0:
            blocks[sub - 1] = ahead[sub - 1][:, :width]
            blocks[sub] = blocks[sub] - ahead[sub - 1][:, width:]
        if sub + 1 < subs:
            blocks[sub + 1] = blocks[sub + 1] + behind[sub + 1][:, :width]
            blocks[sub + 2] = -behind[sub + 1][:, width:]
        if sub == 0:
            ends[0] = blocks[0]
            blocks[0] = none
        if sub == subs - 1:
            ends[1] = blocks[subs]
            blocks[subs] = none
        high, low = split(jnp.concatenate(blocks, axis=1))
        taken[sub * rows : (sub + 1) * rows, :] = high
        taken[total + sub * rows : total + (sub + 1) * rows, :] = low
    for_next[...] = jnp.concatenate(split(ahead[subs - 1][:, :width]), axis=0)
    for_prev[...] = jnp.concatenate(split(-behind[0][:, width:]), axis=0)
    given[0] = -ahead[subs - 1][:, width:]
    given[1] = behind[0][:, :width]


def early_corner_kernel(taken, ends, outside, edge, own, corners):
    subs, rows = own.shape[0], ends.shape[1]
    total = subs * rows
    edges = Joined(edge, own)
    parts = [split(edges[place]) for place in range(subs + 1)]
    high = jnp.concatenate([part[0] for part in parts], axis=1)
    low = jnp.concatenate([part[1] for part in parts], axis=1)
    both = mul_rows(taken[...], high)
    values = both[:total] + both[total:] + mul_rows(taken[:total], low)
    corners[...] = values
    for end, place in ((0, 0), (1, subs)):
        operator = jnp.concatenate(split(ends[end]), axis=0)
        row = end * (total - rows)
        corners[row : row + rows, :] = (
            values[row : row + rows]
            + outer_rows(operator, edges[place])
            + outside[end * rows : (end + 1) * rows, :]
        )


def dual_products(edges, residual, panel, everyone, block, lift, result, sums):
    subs, width = panel.shape[0], panel.shape[1] // 2
    rows = block.shape[0] // 2
    high, low = split(everyone[...])
    both = mul(block[...], high)
    back = both[:rows] + both[rows:] + mul(block[:rows], low)
    corners = rows // subs

    def lifted(sub):
        own = back[sub * corners : (sub + 1) * corners]
        own_high = own.astype(jnp.bfloat16).astype(jnp.float32)
        terms = [own_high, own - own_high, own_high]
        spare = jnp.zeros((lift.shape[1] - 3 * corners, own.shape[1]), jnp.float32)
        return mul(jnp.concatenate(terms + [spare], axis=0).T.astype(jnp.bfloat16), lift[sub])

    parts = [split(edges[place]) for place in range(subs + 1)]
    panel_products(parts, panel, result, lifted)
    product = curvature = 0.0
    for sub in range(subs):
        product = product + residual[sub] * edges[sub + 1]
        curvature = curvature + (
            result[sub][:, width:] * edges[sub + 1] - result[sub][:, :width] * edges[sub]
        )
    sums[...] = jnp.concatenate([row_sums(product), row_sums(curvature)], axis=0)


def send_dual(result, live_own, subs, for_next, for_prev, near_out, far_out, residual=None,
              given=None):
    even = even_place()
    width = near_out.shape[1]
    to_next, to_prev = [result[subs - 1][:, width:]], [result[0][:, :width]]
    if given is not None:
        to_next += [given[0], outer_rows(for_next, residual[subs - 2])]
        to_prev += [given[1], outer_rows(for_prev, residual[0])]
    upper = live_own[subs - 2] * (result[subs - 2][:, width:] - result[subs - 1][:, :width])
    lower = live_own[0] * (result[0][:, width:] - result[1][:, :width])
    to_next.append(outer_rows(for_next, upper))
    to_prev.append(outer_rows(for_prev, lower))
    row = 0
    for ahead, behind in zip(to_next, to_prev):
        rows = slice(row, row + ahead.shape[0])
        near_out[rows, :] = jnp.where(even, ahead, behind)
        far_out[rows, :] = jnp.where(even, behind, ahead)
        row += ahead.shape[0]


def first_dual_kernel(edge, own, residual, panel, everyone, block, lift, live_own,
                      for_next, for_prev, given, first, rest, near_out, far_out, sums):
    result = Joined(first, rest)
    dual_products(Joined(edge, own), residual, panel, everyone, block, lift, result, sums)
    send_dual(result, live_own, panel.shape[0], for_next, for_prev, near_out, far_out,
              residual, given)


def dual_kernel(last, *refs):
    first, rest, near, far, live_edge, live_own = refs[:6]
    residual, panel, everyone, block, lift = refs[6:11]
    even, subs = even_place(), panel.shape[0]
    before, live = Joined(first, rest), Joined(live_edge, live_own)
    edges = [
        0.25 * jump_edge(even, before, near, far, live, place, subs) for place in range(subs + 1)
    ]
    if last:
        own, first_new, rest_new, face, sums = refs[11:]
    else:
        for_next, for_prev, own, first_new, rest_new, near_out, far_out, sums = refs[11:]
    for sub in range(subs):
        own[sub] = edges[sub + 1]
    result = Joined(first_new, rest_new)
    dual_products(edges, residual, panel, everyone, block, lift, result, sums)
    if last:
        face[...] = result[0][:, : face.shape[1]]
    else:
        send_dual(result, live_own, subs, for_next, for_prev, near_out, far_out)


def received(even, near, far, start, rows):
    part = slice(start, start + rows)
    return jnp.concatenate(
        [jnp.where(even, far[part], near[part]), jnp.where(even, near[part], far[part])], axis=0
    )


def first_update_kernel(first, rest, near, far, live_first, live_rest, sums,
                        residual_edge, residual_own, panel, ends,
                        image_own, image_edge, new_edge, new_own, first_new, rest_new,
                        near_out, far_out, scalars, full_ends, outside_image, outside):
    even = even_place()
    loads, width = residual_edge.shape
    subs, rows = panel.shape[0], ends.shape[1]
    result, live = Joined(first, rest), Joined(live_first, live_rest)
    residual, image = Joined(residual_edge, residual_own), Joined(image_edge, image_own)
    residual_new, result_new = Joined(new_edge, new_own), Joined(first_new, rest_new)
    rz_now, alpha, _ = step_scalars(0, sums, None)
    scalars[...] = jnp.concatenate([rz_now, alpha], axis=0)
    operators = received(even, near, far, loads, rows)
    full_ends[0] = ends[0] + operators[:rows]
    full_ends[1] = ends[1] + operators[rows:]
    values = received(even, near, far, loads + 2 * rows, rows)
    outside_image[...] = values
    outside[...] = received(even, near, far, loads + rows, rows) - alpha * values
    alpha_column = column(alpha, width)
    parts = []
    for place in range(subs + 1):
        value = jump_edge(even, result, near, far, live, place, subs)
        image[place] = value
        residual_new[place] = residual[place] - alpha_column * value
        parts.append(split(residual_new[place]))
    panel_products(parts, panel, result_new)
    send_faces(even, result_new[0], result_new[subs - 1], near_out, far_out)


def update_kernel(first, rest, near, far, live_first, live_rest, sums, before,
                  old_edge, old_own, residual_edge, residual_own, panel,
                  outside_image_old, outside_old,
                  image_own, new_edge, new_own, first_new, rest_new,
                  near_out, far_out, scalars, outside):
    even = even_place()
    loads, width = residual_edge.shape
    subs, rows = panel.shape[0], outside.shape[0] // 2
    result, live = Joined(first, rest), Joined(live_first, live_rest)
    image_old, residual = Joined(old_edge, old_own), Joined(residual_edge, residual_own)
    residual_new, result_new = Joined(new_edge, new_own), Joined(first_new, rest_new)
    rz_now, alpha, beta = step_scalars(1, sums, before)
    scalars[...] = jnp.concatenate([rz_now, alpha], axis=0)
    values = received(even, near, far, loads, rows) + beta * outside_image_old[...]
    outside[...] = outside_old[...] - alpha * values
    alpha_column, beta_column = column(alpha, width), column(beta, width)
    parts = []
    for place in range(subs + 1):
        value = jump_edge(even, result, near, far, live, place, subs)
        value = value + beta_column * image_old[place]
        if place > 0:
            image_own[place - 1] = value
        residual_new[place] = residual[place] - alpha_column * value
        parts.append(split(residual_new[place]))
    panel_products(parts, panel, result_new)
    send_faces(even, result_new[0], result_new[subs - 1], near_out, far_out)


def last_kernel(first, rest, following, live, sums, before, older, image_old,
                residual, first_z, second_z, third_z, multipliers, residual_new):
    subs, width = residual.shape[0], following.shape[1]
    result = Joined(first, rest)
    rz_now, alpha, beta = step_scalars(2, sums, before)
    beta_before = before[0:1] / older[0:1]
    on_second = before[1:2] + alpha * beta
    on_first = older[1:2] + on_second * beta_before
    alpha_column, beta_column = column(alpha, width), column(beta, width)
    second_column, first_column = column(on_second, width), column(on_first, width)
    for sub in range(subs):
        left = following[...] if sub == subs - 1 else result[sub + 1][:, :width]
        image = live[sub] * (result[sub][:, width:] - left) + beta_column * image_old[sub]
        residual_new[sub] = residual[sub] - alpha_column * image
        multipliers[sub] = (
            first_column * first_z[sub]
            + second_column * second_z[sub]
            + alpha_column * third_z[sub]
        )


def neighbour_pairs(size, first):
    pairs = [(i, i + 1) for i in range(first, size - 1, 2)]
    return [route for a, b in pairs for route in ((a, b), (b, a))]


def swap(near, far):
    size = lax.axis_size("sub")
    return (
        lax.ppermute(near, "sub", neighbour_pairs(size, 0)),
        lax.ppermute(far, "sub", neighbour_pairs(size, 1)),
    )


def from_all(rows):
    size = lax.axis_size("sub") * lax.axis_size("grp")
    copies = jnp.broadcast_to(rows[None], (size,) + rows.shape)
    return lax.all_to_all(copies, ("sub", "grp"), 0, 0)


def from_group(values):
    group = lax.axis_size("grp")
    received = [values]
    for distance in range(1, group):
        routes = [(i, i ^ distance) for i in range(group)]
        received.append(lax.ppermute(values, "grp", routes))
    return received


def swap_blocks(picked):
    group = lax.axis_size("grp")
    block = picked[0]
    for distance in range(1, group):
        routes = [(i, i ^ distance) for i in range(group)]
        block = block + lax.ppermute(picked[distance], "grp", routes)
    return block


def make_tail(counts, rhs):
    loads, width = rhs.shape[2:]
    return pl.pallas_call(
        tail_kernel,
        out_shape=jax.ShapeDtypeStruct((loads + 8, width), jnp.float32),
        in_specs=[
            pl.BlockSpec(memory_space=pltpu.HBM),
            pl.BlockSpec(memory_space=pltpu.HBM),
        ],
        out_specs=pl.BlockSpec(memory_space=pltpu.VMEM),
        scratch_shapes=[
            pltpu.VMEM(counts.shape, counts.dtype),
            pltpu.VMEM((loads, width), jnp.float32),
            pltpu.SemaphoreType.DMA,
            pltpu.SemaphoreType.DMA,
        ],
        compiler_params=pltpu.CompilerParams(vmem_limit_bytes=TAIL_LIMIT),
    )(counts, rhs)


def local(rhs, counts, solve_panel, dirichlet_panel, coupling, corner_map, coarse_inverse):
    subs, loads, width = rhs.shape[1:]
    corners = coupling.shape[2]
    solve, dirichlet = solve_panel[0], dirichlet_panel[0]
    size = lax.axis_size("sub")

    face_shape, own_shape = (loads, width), (subs, loads, width)
    first_shape, rest_shape = (loads, 2 * width), (subs - 1, loads, 2 * width)
    edges_shapes = [face_shape, own_shape]
    result_shapes = [first_shape, rest_shape, face_shape, face_shape]

    tail = make_tail(counts, rhs)
    tail, counts, corner_map = lax.optimization_barrier((tail, counts, corner_map))
    head = lax.ppermute(tail, "sub", [(i, i + 1) for i in range(size - 1)])
    maps = from_group(corner_map[0])
    live_own, residual_own, partial, rest = call(
        early_kernel,
        [(subs, 1, width), own_shape, first_shape, rest_shape],
        counts, rhs[0], dirichlet,
    )
    group, own = len(maps), subs * corners
    pair = [(corners, width)] * 2
    *picked, stacked, lift, near_side, far_side = call(
        setup_kernel,
        [(own, group * own)] * group
        + [(subs, 2 * corners, 2 * width), (subs, 3 * corners + -3 * corners % 128, 2 * width)]
        + pair,
        *maps, coarse_inverse[0], coupling[0],
        kinds=[jnp.float32] * group + [jnp.bfloat16] * 2 + [jnp.float32] * 2,
        scratch=[pltpu.VMEM((group, 1, own), jnp.int32)],
    )
    head, picked, rest = lax.optimization_barrier((head, picked, rest))
    live_edge, residual_edge, first, near, far = call(
        head_kernel,
        [(1, width), face_shape, first_shape, face_shape, face_shape],
        head, partial, rest, dirichlet,
    )
    near, far, near_side, far_side = lax.optimization_barrier((near, far, near_side, far_side))
    near, far = swap(near, far)
    near_side, far_side = swap(near_side, far_side)
    block = jnp.concatenate(split_outside(swap_blocks(picked)), axis=0)
    live, residual = (live_edge, live_own), (residual_edge, residual_own)
    taken, ends, for_next, for_prev, given = call(
        operators_kernel,
        [(2 * own, (subs + 1) * width), (2,) + pair[0], (2 * corners, width),
         (2 * corners, width), (2,) + pair[0]],
        coupling[0], *live, near_side, far_side, dirichlet,
        kinds=[jnp.bfloat16, jnp.float32, jnp.bfloat16, jnp.bfloat16, jnp.float32],
    )

    scalars_shape, outside_shape = (2, loads), (2 * corners, loads)
    long_shape, longer_shape = (loads + corners, width), (loads + 3 * corners, width)
    edge, first_z, values = call(
        corner_kernel,
        edges_shapes + [(own, loads)],
        first, rest, near, far, *live, stacked,
    )
    everyone = lax.all_gather(values, "grp", tiled=True)
    first, rest, near, far, sums = call(
        first_dual_kernel,
        [first_shape, rest_shape, longer_shape, longer_shape, scalars_shape],
        edge, first_z, residual[1], solve, everyone, block, lift, live[1],
        for_next, for_prev, given,
    )
    sums = from_all(sums)
    near, far = swap(near, far)
    (image_own, image_edge, *residual, first, rest, near, far, scalars_first, ends, outside_image,
     outside) = call(
        first_update_kernel,
        [own_shape, face_shape] + edges_shapes + result_shapes
        + [scalars_shape, (2,) + pair[0], outside_shape, outside_shape],
        first, rest, near, far, *live, sums, *residual, dirichlet, ends,
    )

    near, far = swap(near, far)
    (values,) = call(early_corner_kernel, [(own, loads)], taken, ends, outside, *residual)
    everyone = lax.all_gather(values, "grp", tiled=True)
    second_z, first, rest, near, far, sums = call(
        functools.partial(dual_kernel, False),
        [own_shape, first_shape, rest_shape, long_shape, long_shape, scalars_shape],
        first, rest, near, far, *live, residual[1], solve, everyone, block, lift,
        for_next, for_prev,
    )
    sums = from_all(sums)
    near, far = swap(near, far)
    image_own, *residual, first, rest, near, far, scalars_second, outside = call(
        update_kernel,
        [own_shape] + edges_shapes + result_shapes + [scalars_shape, outside_shape],
        first, rest, near, far, *live, sums, scalars_first, image_edge, image_own, *residual,
        dirichlet, outside_image, outside,
    )

    near, far = swap(near, far)
    (values,) = call(early_corner_kernel, [(own, loads)], taken, ends, outside, *residual)
    everyone = lax.all_gather(values, "grp", tiled=True)
    third_z, first, rest, face, sums = call(
        functools.partial(dual_kernel, True),
        [own_shape, first_shape, rest_shape, face_shape, scalars_shape],
        first, rest, near, far, *live, residual[1], solve, everyone, block, lift,
    )
    sums = from_all(sums)
    following = lax.ppermute(face, "sub", [(i + 1, i) for i in range(size - 1)])
    multipliers, residual = call(
        last_kernel,
        [own_shape] * 2,
        first, rest, following, live[1], sums, scalars_second, scalars_first,
        image_own, residual[1], first_z, second_z, third_z,
    )
    return (multipliers[None], residual[None])


def solution(mesh):
    return jax.shard_map(
        local,
        mesh=mesh,
        in_specs=(
            P("grp", "sub", None, None),
            P("grp", "sub"),
            P("grp", "sub", None, None),
            P("grp", "sub", None, None),
            P("grp", "sub", None, None),
            P("grp", "sub", None),
            P("sub", "grp", None),
        ),
        out_specs=(P("grp", "sub", None, None), P("grp", "sub", None, None)),
        check_vma=False,
    )
```

```python
import functools

import jax
import jax.numpy as jnp
from jax import lax
from jax.experimental import pallas as pl
from jax.experimental.pallas import tpu as pltpu
from jax.sharding import PartitionSpec as P

VMEM_LIMIT = 8 * 1024 * 1024
TAIL_LIMIT = 62 * 1024 * 1024


def split(values):
    high = values.astype(jnp.bfloat16)
    return high, (values - high.astype(jnp.float32)).astype(jnp.bfloat16)


def split_outside(values):
    high = lax.reduce_precision(values, exponent_bits=8, mantissa_bits=7)
    return high.astype(jnp.bfloat16), (values - high).astype(jnp.bfloat16)


def mul(first, second):
    return jnp.dot(first, second, preferred_element_type=jnp.float32)


def mul_rows(first, second):
    dims = (((1,), (1,)), ((), ()))
    return lax.dot_general(first, second, dims, preferred_element_type=jnp.float32)


def call(kernel, out_shapes, *operands, kinds=None, scratch=()):
    kinds = kinds or [jnp.float32] * len(out_shapes)
    return pl.pallas_call(
        kernel,
        out_shape=[jax.ShapeDtypeStruct(*shape) for shape in zip(out_shapes, kinds)],
        in_specs=[pl.BlockSpec(memory_space=pltpu.VMEM)] * len(operands),
        out_specs=[pl.BlockSpec(memory_space=pltpu.VMEM)] * len(out_shapes),
        scratch_shapes=list(scratch),
        compiler_params=pltpu.CompilerParams(vmem_limit_bytes=VMEM_LIMIT),
    )(*operands)


class Joined:
    def __init__(self, first, rest):
        self.first, self.rest = first, rest

    def __getitem__(self, place):
        return self.first[...] if place == 0 else self.rest[place - 1]

    def __setitem__(self, place, value):
        if place == 0:
            self.first[...] = value
        else:
            self.rest[place - 1] = value


def jump_edge(even, result, near, far, live, edge, subs):
    loads, width = result[0].shape[0], near.shape[1]
    if edge == 0:
        right = jnp.where(even, far[:loads], near[:loads])
    else:
        right = result[edge - 1][:, width:]
    if edge == subs:
        left = jnp.where(even, near[:loads], far[:loads])
    else:
        left = result[edge][:, :width]
    return live[edge] * (right - left)


def outer_rows(operator, edge):
    rows = operator.shape[0] // 2
    high, low = split(edge)
    both = mul_rows(operator[...], high)
    return both[:rows] + both[rows:] + mul_rows(operator[:rows], low)


def send(even, to_next, to_prev, near_out, far_out):
    row = 0
    for ahead, behind in zip(to_next, to_prev):
        rows = slice(row, row + ahead.shape[0])
        near_out[rows, :] = jnp.where(even, ahead, behind)
        far_out[rows, :] = jnp.where(even, behind, ahead)
        row += ahead.shape[0]


def send_faces(even, first, last, near_out, far_out):
    width = first.shape[1] // 2
    send(even, [last[:, width:]], [first[:, :width]], near_out, far_out)


def panel_products(parts, panel, result, extra=None):
    subs = panel.shape[0]
    for sub in range(subs):
        high = jnp.concatenate([-parts[sub][0], parts[sub + 1][0]], axis=1)
        low = jnp.concatenate([-parts[sub][1], parts[sub + 1][1]], axis=1)
        total = mul(high, panel[sub]) + mul(low, panel[sub])
        if extra is not None:
            total = total + extra(sub)
        result[sub] = total


def column(row, width):
    lanes = jnp.broadcast_to(row, (128, row.shape[1])).T
    return jnp.concatenate([lanes] * (width // 128), axis=1)


def row_sums(values):
    half = values.shape[1] // 2
    return jnp.sum((values[:, :half] + values[:, half:]).T, axis=0, keepdims=True)


def step_scalars(step, sums, before):
    totals = jnp.sum(sums[...], axis=0)
    rz_now, curvature = totals[:1], totals[1:2]
    if step == 0:
        return rz_now, rz_now / curvature, None
    beta = rz_now / before[0:1]
    return rz_now, rz_now / (curvature - beta * rz_now / before[1:2]), beta


def even_place():
    return lax.rem(lax.axis_index("sub"), 2) == 0


def live_rows(counts, sub, rows, width):
    last = lax.axis_index("sub") == lax.axis_size("sub") - 1
    count = jnp.broadcast_to(counts[:, sub : sub + 1], (rows, width))
    if sub == counts.shape[1] - 1:
        count = jnp.where(last, 0, count)
    return (lax.broadcasted_iota(jnp.int32, (rows, width), 1) < count).astype(jnp.float32)


def tail_kernel(counts_ref, rhs, tail, counts, face, counts_done, face_done):
    loads, width = rhs.shape[2:]
    counts_copy = pltpu.make_async_copy(counts_ref, counts, counts_done)
    face_copy = pltpu.make_async_copy(rhs.at[0, rhs.shape[1] - 1], face, face_done)
    counts_copy.start()
    face_copy.start()
    counts_copy.wait()
    mask = live_rows(counts, counts.shape[1] - 1, 8, width)
    tail[loads:] = mask
    face_copy.wait()
    tail[:loads] = mask[:1] * face[...]


def early_kernel(counts, rhs, panel, live, own, partial, rest):
    subs, loads, width = own.shape
    parts = [None]
    for sub in range(subs):
        mask = live_rows(counts, sub, 1, width)
        live[sub] = mask
        own[sub] = mask * rhs[sub]
        parts.append(split(own[sub]))
    partial[...] = mul(parts[1][0], panel[0, width:]) + mul(parts[1][1], panel[0, width:])
    for sub in range(1, subs):
        high = jnp.concatenate([-parts[sub][0], parts[sub + 1][0]], axis=1)
        low = jnp.concatenate([-parts[sub][1], parts[sub + 1][1]], axis=1)
        rest[sub - 1] = mul(high, panel[sub]) + mul(low, panel[sub])


def head_kernel(head, partial, rest, panel, coupling, live, edge, first, near_out, far_out):
    loads, width = edge.shape
    live[...] = head[loads : loads + 1]
    edge[...] = head[:loads]
    high, low = split(head[:loads])
    first[...] = partial[...] - mul(high, panel[0, :width]) - mul(low, panel[0, :width])
    last = rest[rest.shape[0] - 1]
    to_next = [last[:, width:], coupling[coupling.shape[0] - 1, :, width:]]
    send(even_place(), to_next, [first[:, :width], coupling[0, :, :width]], near_out, far_out)


def setup_kernel(*refs):
    group = (len(refs) - 5) // 2
    maps, (coarse, coupling) = refs[:group], refs[group : group + 2]
    picked, (stacked, lift, everyone) = refs[group + 2 : -3], refs[-3:]
    subs, corners = maps[0].shape
    rows, size = coarse.shape
    own = subs * corners
    grp = lax.axis_index("grp")
    for sub in range(subs):
        high, low = split(coupling[sub])
        spare = jnp.zeros((lift.shape[1] - 3 * corners, high.shape[1]), jnp.bfloat16)
        stacked[sub] = jnp.concatenate([high, low], axis=0)
        lift[sub] = jnp.concatenate([high, high, low, spare], axis=0)
    for distance in range(group):
        unknowns = [maps[distance][sub : sub + 1, :] for sub in range(subs)]
        everyone[distance] = jnp.concatenate(unknowns, axis=1)
    high, low = split(coarse[...])
    unknowns = lax.broadcasted_iota(jnp.int32, (size, own), 0)
    columns = []
    for member in range(group):
        chosen = (unknowns == everyone[grp ^ member]).astype(jnp.bfloat16)
        columns.append(mul(high, chosen) + mul(low, chosen))
    high, low = split(jnp.concatenate(columns, axis=1))
    owned = lax.broadcasted_iota(jnp.int32, (rows, own), 0) + grp * rows
    dims = (((0,), (0,)), ((), ()))
    for distance in range(group):
        chosen = (owned == everyone[distance]).astype(jnp.bfloat16)
        picked[distance][...] = lax.dot_general(
            chosen, high, dims, preferred_element_type=jnp.float32
        ) + lax.dot_general(chosen, low, dims, preferred_element_type=jnp.float32)


def corner_kernel(first, rest, near, far, live_first, live_rest, coupling,
                  edge, own, corners):
    even = even_place()
    subs, rows = coupling.shape[0], coupling.shape[1] // 2
    result, live, edges = Joined(first, rest), Joined(live_first, live_rest), Joined(edge, own)
    parts = []
    for place in range(subs + 1):
        edges[place] = 0.25 * jump_edge(even, result, near, far, live, place, subs)
        parts.append(split(edges[place]))
    for sub in range(subs):
        high = jnp.concatenate([-parts[sub][0], parts[sub + 1][0]], axis=1)
        low = jnp.concatenate([-parts[sub][1], parts[sub + 1][1]], axis=1)
        both = mul_rows(coupling[sub], high)
        corners[sub * rows : (sub + 1) * rows, :] = (
            both[:rows] + both[rows:] + mul_rows(coupling[sub, :rows], low)
        )


def operators_kernel(coupling, live_edge, live_own, near, far, panel,
                     taken, ends, for_next, for_prev, given):
    even = even_place()
    subs, rows = coupling.shape[0], coupling.shape[1]
    width = coupling.shape[2] // 2
    live = Joined(live_edge, live_own)
    sides = received(even, near, far, near.shape[0] - rows, rows)
    before, after = sides[:rows], sides[rows:]
    left = [coupling[sub, :, :width] * (0.25 * live[sub]) for sub in range(subs)]
    left.append(after * (0.25 * live[subs]))
    right = [before * (0.25 * live[0])]
    right += [coupling[sub, :, width:] * (0.25 * live[sub + 1]) for sub in range(subs)]
    none = jnp.zeros((rows, width), jnp.float32)
    inner, ahead, behind = [], [], []
    for sub in range(subs):
        factors = jnp.concatenate(
            [
                jnp.concatenate([left[sub], right[sub + 1]], axis=1),
                jnp.concatenate([none, left[sub + 1]], axis=1),
                jnp.concatenate([right[sub], none], axis=1),
            ],
            axis=0,
        )
        both = mul(jnp.concatenate(split(factors), axis=0), panel[sub])
        product = both[: 3 * rows] + both[3 * rows :]
        inner.append(product[:rows])
        ahead.append(product[rows : 2 * rows])
        behind.append(product[2 * rows :])
    total = subs * rows
    for sub in range(subs):
        blocks = [none] * (subs + 1)
        blocks[sub] = -inner[sub][:, :width]
        blocks[sub + 1] = inner[sub][:, width:]
        if sub > 0:
            blocks[sub - 1] = ahead[sub - 1][:, :width]
            blocks[sub] = blocks[sub] - ahead[sub - 1][:, width:]
        if sub + 1 < subs:
            blocks[sub + 1] = blocks[sub + 1] + behind[sub + 1][:, :width]
            blocks[sub + 2] = -behind[sub + 1][:, width:]
        if sub == 0:
            ends[0] = blocks[0]
            blocks[0] = none
        if sub == subs - 1:
            ends[1] = blocks[subs]
            blocks[subs] = none
        high, low = split(jnp.concatenate(blocks, axis=1))
        taken[sub * rows : (sub + 1) * rows, :] = high
        taken[total + sub * rows : total + (sub + 1) * rows, :] = low
    for_next[...] = jnp.concatenate(split(ahead[subs - 1][:, :width]), axis=0)
    for_prev[...] = jnp.concatenate(split(-behind[0][:, width:]), axis=0)
    given[0] = -ahead[subs - 1][:, width:]
    given[1] = behind[0][:, :width]


def early_corner_kernel(taken, ends, outside, edge, own, corners):
    subs, rows = own.shape[0], ends.shape[1]
    total = subs * rows
    edges = Joined(edge, own)
    parts = [split(edges[place]) for place in range(subs + 1)]
    high = jnp.concatenate([part[0] for part in parts], axis=1)
    low = jnp.concatenate([part[1] for part in parts], axis=1)
    both = mul_rows(taken[...], high)
    values = both[:total] + both[total:] + mul_rows(taken[:total], low)
    corners[...] = values
    for end, place in ((0, 0), (1, subs)):
        operator = jnp.concatenate(split(ends[end]), axis=0)
        row = end * (total - rows)
        corners[row : row + rows, :] = (
            values[row : row + rows]
            + outer_rows(operator, edges[place])
            + outside[end * rows : (end + 1) * rows, :]
        )


def dual_products(edges, residual, panel, everyone, block, lift, result, sums):
    subs, width = panel.shape[0], panel.shape[1] // 2
    rows = block.shape[0] // 2
    high, low = split(everyone[...])
    both = mul(block[...], high)
    back = both[:rows] + both[rows:] + mul(block[:rows], low)
    corners = rows // subs

    def lifted(sub):
        own = back[sub * corners : (sub + 1) * corners]
        own_high = own.astype(jnp.bfloat16).astype(jnp.float32)
        terms = [own_high, own - own_high, own_high]
        spare = jnp.zeros((lift.shape[1] - 3 * corners, own.shape[1]), jnp.float32)
        return mul(jnp.concatenate(terms + [spare], axis=0).T.astype(jnp.bfloat16), lift[sub])

    parts = [split(edges[place]) for place in range(subs + 1)]
    panel_products(parts, panel, result, lifted)
    product = curvature = 0.0
    for sub in range(subs):
        product = product + residual[sub] * edges[sub + 1]
        curvature = curvature + (
            result[sub][:, width:] * edges[sub + 1] - result[sub][:, :width] * edges[sub]
        )
    sums[...] = jnp.concatenate([row_sums(product), row_sums(curvature)], axis=0)


def send_dual(result, live_own, subs, for_next, for_prev, near_out, far_out, residual=None,
              given=None):
    even = even_place()
    width = near_out.shape[1]
    to_next, to_prev = [result[subs - 1][:, width:]], [result[0][:, :width]]
    if given is not None:
        to_next += [given[0], outer_rows(for_next, residual[subs - 2])]
        to_prev += [given[1], outer_rows(for_prev, residual[0])]
    upper = live_own[subs - 2] * (result[subs - 2][:, width:] - result[subs - 1][:, :width])
    lower = live_own[0] * (result[0][:, width:] - result[1][:, :width])
    to_next.append(outer_rows(for_next, upper))
    to_prev.append(outer_rows(for_prev, lower))
    send(even, to_next, to_prev, near_out, far_out)


def first_dual_kernel(edge, own, residual, panel, everyone, block, lift, live_own,
                      for_next, for_prev, given, first, rest, near_out, far_out, sums):
    result = Joined(first, rest)
    dual_products(Joined(edge, own), residual, panel, everyone, block, lift, result, sums)
    send_dual(result, live_own, panel.shape[0], for_next, for_prev, near_out, far_out,
              residual, given)


def dual_kernel(last, *refs):
    first, rest, near, far, live_edge, live_own = refs[:6]
    residual, panel, everyone, block, lift = refs[6:11]
    even, subs = even_place(), panel.shape[0]
    before, live = Joined(first, rest), Joined(live_edge, live_own)
    edges = [
        0.25 * jump_edge(even, before, near, far, live, place, subs) for place in range(subs + 1)
    ]
    if last:
        own, first_new, rest_new, face, sums = refs[11:]
    else:
        for_next, for_prev, own, first_new, rest_new, near_out, far_out, sums = refs[11:]
    for sub in range(subs):
        own[sub] = edges[sub + 1]
    result = Joined(first_new, rest_new)
    dual_products(edges, residual, panel, everyone, block, lift, result, sums)
    if last:
        face[...] = result[0][:, : face.shape[1]]
    else:
        send_dual(result, live_own, subs, for_next, for_prev, near_out, far_out)


def received(even, near, far, start, rows):
    part = slice(start, start + rows)
    return jnp.concatenate(
        [jnp.where(even, far[part], near[part]), jnp.where(even, near[part], far[part])], axis=0
    )


def first_update_kernel(first, rest, near, far, live_first, live_rest, sums,
                        residual_edge, residual_own, panel, ends,
                        image_own, image_edge, new_edge, new_own, first_new, rest_new,
                        near_out, far_out, scalars, full_ends, outside_image, outside):
    even = even_place()
    loads, width = residual_edge.shape
    subs, rows = panel.shape[0], ends.shape[1]
    result, live = Joined(first, rest), Joined(live_first, live_rest)
    residual, image = Joined(residual_edge, residual_own), Joined(image_edge, image_own)
    residual_new, result_new = Joined(new_edge, new_own), Joined(first_new, rest_new)
    rz_now, alpha, _ = step_scalars(0, sums, None)
    scalars[...] = jnp.concatenate([rz_now, alpha], axis=0)
    operators = received(even, near, far, loads, rows)
    full_ends[0] = ends[0] + operators[:rows]
    full_ends[1] = ends[1] + operators[rows:]
    values = received(even, near, far, loads + 2 * rows, rows)
    outside_image[...] = values
    outside[...] = received(even, near, far, loads + rows, rows) - alpha * values
    alpha_column = column(alpha, width)
    parts = []
    for place in range(subs + 1):
        value = jump_edge(even, result, near, far, live, place, subs)
        image[place] = value
        residual_new[place] = residual[place] - alpha_column * value
        parts.append(split(residual_new[place]))
    panel_products(parts, panel, result_new)
    send_faces(even, result_new[0], result_new[subs - 1], near_out, far_out)


def update_kernel(first, rest, near, far, live_first, live_rest, sums, before,
                  old_edge, old_own, residual_edge, residual_own, panel,
                  outside_image_old, outside_old,
                  image_own, new_edge, new_own, first_new, rest_new,
                  near_out, far_out, scalars, outside):
    even = even_place()
    loads, width = residual_edge.shape
    subs, rows = panel.shape[0], outside.shape[0] // 2
    result, live = Joined(first, rest), Joined(live_first, live_rest)
    image_old, residual = Joined(old_edge, old_own), Joined(residual_edge, residual_own)
    residual_new, result_new = Joined(new_edge, new_own), Joined(first_new, rest_new)
    rz_now, alpha, beta = step_scalars(1, sums, before)
    scalars[...] = jnp.concatenate([rz_now, alpha], axis=0)
    values = received(even, near, far, loads, rows) + beta * outside_image_old[...]
    outside[...] = outside_old[...] - alpha * values
    alpha_column, beta_column = column(alpha, width), column(beta, width)
    parts = []
    for place in range(subs + 1):
        value = jump_edge(even, result, near, far, live, place, subs)
        value = value + beta_column * image_old[place]
        if place > 0:
            image_own[place - 1] = value
        residual_new[place] = residual[place] - alpha_column * value
        parts.append(split(residual_new[place]))
    panel_products(parts, panel, result_new)
    send_faces(even, result_new[0], result_new[subs - 1], near_out, far_out)


def last_kernel(first, rest, following, live, sums, before, older, image_old,
                residual, first_z, second_z, third_z, multipliers, residual_new):
    subs, width = residual.shape[0], following.shape[1]
    result = Joined(first, rest)
    rz_now, alpha, beta = step_scalars(2, sums, before)
    beta_before = before[0:1] / older[0:1]
    on_second = before[1:2] + alpha * beta
    on_first = older[1:2] + on_second * beta_before
    alpha_column, beta_column = column(alpha, width), column(beta, width)
    second_column, first_column = column(on_second, width), column(on_first, width)
    for sub in range(subs):
        left = following[...] if sub == subs - 1 else result[sub + 1][:, :width]
        image = live[sub] * (result[sub][:, width:] - left) + beta_column * image_old[sub]
        residual_new[sub] = residual[sub] - alpha_column * image
        multipliers[sub] = (
            first_column * first_z[sub]
            + second_column * second_z[sub]
            + alpha_column * third_z[sub]
        )


def neighbour_pairs(size, first):
    pairs = [(i, i + 1) for i in range(first, size - 1, 2)]
    return [route for a, b in pairs for route in ((a, b), (b, a))]


def swap(near, far):
    size = lax.axis_size("sub")
    return (
        lax.ppermute(near, "sub", neighbour_pairs(size, 0)),
        lax.ppermute(far, "sub", neighbour_pairs(size, 1)),
    )


def from_all(rows):
    size = lax.axis_size("sub") * lax.axis_size("grp")
    copies = jnp.broadcast_to(rows[None], (size,) + rows.shape)
    return lax.all_to_all(copies, ("sub", "grp"), 0, 0)


def from_group(values):
    group = lax.axis_size("grp")
    received = [values]
    for distance in range(1, group):
        routes = [(i, i ^ distance) for i in range(group)]
        received.append(lax.ppermute(values, "grp", routes))
    return received


def swap_blocks(picked):
    group = lax.axis_size("grp")
    block = picked[0]
    for distance in range(1, group):
        routes = [(i, i ^ distance) for i in range(group)]
        block = block + lax.ppermute(picked[distance], "grp", routes)
    return block


def make_tail(counts, rhs):
    loads, width = rhs.shape[2:]
    return pl.pallas_call(
        tail_kernel,
        out_shape=jax.ShapeDtypeStruct((loads + 8, width), jnp.float32),
        in_specs=[
            pl.BlockSpec(memory_space=pltpu.HBM),
            pl.BlockSpec(memory_space=pltpu.HBM),
        ],
        out_specs=pl.BlockSpec(memory_space=pltpu.VMEM),
        scratch_shapes=[
            pltpu.VMEM(counts.shape, counts.dtype),
            pltpu.VMEM((loads, width), jnp.float32),
            pltpu.SemaphoreType.DMA,
            pltpu.SemaphoreType.DMA,
        ],
        compiler_params=pltpu.CompilerParams(vmem_limit_bytes=TAIL_LIMIT),
    )(counts, rhs)


def local(rhs, counts, solve_panel, dirichlet_panel, coupling, corner_map, coarse_inverse):
    subs, loads, width = rhs.shape[1:]
    corners = coupling.shape[2]
    solve, dirichlet = solve_panel[0], dirichlet_panel[0]
    size = lax.axis_size("sub")

    face_shape, own_shape = (loads, width), (subs, loads, width)
    first_shape, rest_shape = (loads, 2 * width), (subs - 1, loads, 2 * width)
    scalars_shape, outside_shape, side_shape = (2, loads), (2 * corners, loads), (corners, width)
    long_shape, longer_shape = (loads + corners, width), (loads + 3 * corners, width)
    edges_shapes = [face_shape, own_shape]
    result_shapes = [first_shape, rest_shape, face_shape, face_shape]

    tail = make_tail(counts, rhs)
    tail, counts, corner_map = lax.optimization_barrier((tail, counts, corner_map))
    head = lax.ppermute(tail, "sub", [(i, i + 1) for i in range(size - 1)])
    maps = from_group(corner_map[0])
    live_own, residual_own, partial, rest = call(
        early_kernel,
        [(subs, 1, width), own_shape, first_shape, rest_shape],
        counts, rhs[0], dirichlet,
    )
    group, own = len(maps), subs * corners
    pair = [(corners, width)] * 2
    *picked, stacked, lift = call(
        setup_kernel,
        [(own, group * own)] * group
        + [(subs, 2 * corners, 2 * width), (subs, 3 * corners + -3 * corners % 128, 2 * width)],
        *maps, coarse_inverse[0], coupling[0],
        kinds=[jnp.float32] * group + [jnp.bfloat16] * 2,
        scratch=[pltpu.VMEM((group, 1, own), jnp.int32)],
    )
    head, picked, rest = lax.optimization_barrier((head, picked, rest))
    live_edge, residual_edge, first, near, far = call(
        head_kernel,
        [(1, width), face_shape, first_shape, long_shape, long_shape],
        head, partial, rest, dirichlet, coupling[0],
    )
    near, far = swap(near, far)
    block = jnp.concatenate(split_outside(swap_blocks(picked)), axis=0)
    live, residual = (live_edge, live_own), (residual_edge, residual_own)
    taken, ends, for_next, for_prev, given = call(
        operators_kernel,
        [(2 * own, (subs + 1) * width), (2,) + side_shape, (2 * corners, width),
         (2 * corners, width), (2,) + side_shape],
        coupling[0], *live, near, far, dirichlet,
        kinds=[jnp.bfloat16, jnp.float32, jnp.bfloat16, jnp.bfloat16, jnp.float32],
    )

    edge, first_z, values = call(
        corner_kernel,
        edges_shapes + [(own, loads)],
        first, rest, near, far, *live, stacked,
    )
    everyone = lax.all_gather(values, "grp", tiled=True)
    first, rest, near, far, sums = call(
        first_dual_kernel,
        [first_shape, rest_shape, longer_shape, longer_shape, scalars_shape],
        edge, first_z, residual[1], solve, everyone, block, lift, live[1],
        for_next, for_prev, given,
    )
    sums = from_all(sums)
    near, far = swap(near, far)
    (image_own, image_edge, *residual, first, rest, near, far, scalars_first, ends, outside_image,
     outside) = call(
        first_update_kernel,
        [own_shape, face_shape] + edges_shapes + result_shapes
        + [scalars_shape, (2,) + side_shape, outside_shape, outside_shape],
        first, rest, near, far, *live, sums, *residual, dirichlet, ends,
    )

    near, far = swap(near, far)
    (values,) = call(early_corner_kernel, [(own, loads)], taken, ends, outside, *residual)
    everyone = lax.all_gather(values, "grp", tiled=True)
    second_z, first, rest, near, far, sums = call(
        functools.partial(dual_kernel, False),
        [own_shape, first_shape, rest_shape, long_shape, long_shape, scalars_shape],
        first, rest, near, far, *live, residual[1], solve, everyone, block, lift,
        for_next, for_prev,
    )
    sums = from_all(sums)
    near, far = swap(near, far)
    image_own, *residual, first, rest, near, far, scalars_second, outside = call(
        update_kernel,
        [own_shape] + edges_shapes + result_shapes + [scalars_shape, outside_shape],
        first, rest, near, far, *live, sums, scalars_first, image_edge, image_own, *residual,
        dirichlet, outside_image, outside,
    )

    near, far = swap(near, far)
    (values,) = call(early_corner_kernel, [(own, loads)], taken, ends, outside, *residual)
    everyone = lax.all_gather(values, "grp", tiled=True)
    third_z, first, rest, face, sums = call(
        functools.partial(dual_kernel, True),
        [own_shape, first_shape, rest_shape, face_shape, scalars_shape],
        first, rest, near, far, *live, residual[1], solve, everyone, block, lift,
    )
    sums = from_all(sums)
    following = lax.ppermute(face, "sub", [(i + 1, i) for i in range(size - 1)])
    multipliers, residual = call(
        last_kernel,
        [own_shape] * 2,
        first, rest, following, live[1], sums, scalars_second, scalars_first,
        image_own, residual[1], first_z, second_z, third_z,
    )
    return (multipliers[None], residual[None])


def solution(mesh):
    return jax.shard_map(
        local,
        mesh=mesh,
        in_specs=(
            P("grp", "sub", None, None),
            P("grp", "sub"),
            P("grp", "sub", None, None),
            P("grp", "sub", None, None),
            P("grp", "sub", None, None),
            P("grp", "sub", None),
            P("sub", "grp", None),
        ),
        out_specs=(P("grp", "sub", None, None), P("grp", "sub", None, None)),
        check_vma=False,
    )
```

```python
import functools

import jax
import jax.numpy as jnp
from jax import lax
from jax.experimental import pallas as pl
from jax.experimental.pallas import tpu as pltpu
from jax.sharding import PartitionSpec as P

VMEM_LIMIT = 8 * 1024 * 1024


def split(values):
    high = values.astype(jnp.bfloat16)
    return high, (values - high.astype(jnp.float32)).astype(jnp.bfloat16)


def split_outside(values):
    high = lax.reduce_precision(values, exponent_bits=8, mantissa_bits=7)
    return high.astype(jnp.bfloat16), (values - high).astype(jnp.bfloat16)


def mul(first, second):
    return jnp.dot(first, second, preferred_element_type=jnp.float32)


def mul_rows(first, second):
    dims = (((1,), (1,)), ((), ()))
    return lax.dot_general(first, second, dims, preferred_element_type=jnp.float32)


def call(kernel, out_shapes, *operands, kinds=None, scratch=()):
    kinds = kinds or [jnp.float32] * len(out_shapes)
    return pl.pallas_call(
        kernel,
        out_shape=[jax.ShapeDtypeStruct(*shape) for shape in zip(out_shapes, kinds)],
        in_specs=[pl.BlockSpec(memory_space=pltpu.VMEM)] * len(operands),
        out_specs=[pl.BlockSpec(memory_space=pltpu.VMEM)] * len(out_shapes),
        scratch_shapes=list(scratch),
        compiler_params=pltpu.CompilerParams(vmem_limit_bytes=VMEM_LIMIT),
    )(*operands)


class Joined:
    def __init__(self, first, rest):
        self.first, self.rest = first, rest

    def __getitem__(self, place):
        return self.first[...] if place == 0 else self.rest[place - 1]

    def __setitem__(self, place, value):
        if place == 0:
            self.first[...] = value
        else:
            self.rest[place - 1] = value


def jump_edge(even, result, near, far, live, edge, subs):
    loads, width = result[0].shape[0], near.shape[1]
    if edge == 0:
        right = jnp.where(even, far[:loads], near[:loads])
    else:
        right = result[edge - 1][:, width:]
    if edge == subs:
        left = jnp.where(even, near[:loads], far[:loads])
    else:
        left = result[edge][:, :width]
    return live[edge] * (right - left)


def outer_rows(operator, edge):
    rows = operator.shape[0] // 2
    high, low = split(edge)
    both = mul_rows(operator[...], high)
    return both[:rows] + both[rows:] + mul_rows(operator[:rows], low)


def send(even, to_next, to_prev, near_out, far_out):
    row = 0
    for ahead, behind in zip(to_next, to_prev):
        rows = slice(row, row + ahead.shape[0])
        near_out[rows, :] = jnp.where(even, ahead, behind)
        far_out[rows, :] = jnp.where(even, behind, ahead)
        row += ahead.shape[0]


def send_faces(even, first, last, near_out, far_out):
    width = first.shape[1] // 2
    send(even, [last[:, width:]], [first[:, :width]], near_out, far_out)


def panel_products(parts, panel, result, extra=None):
    subs = panel.shape[0]
    for sub in range(subs):
        high = jnp.concatenate([-parts[sub][0], parts[sub + 1][0]], axis=1)
        low = jnp.concatenate([-parts[sub][1], parts[sub + 1][1]], axis=1)
        total = mul(high, panel[sub]) + mul(low, panel[sub])
        if extra is not None:
            total = total + extra(sub)
        result[sub] = total


def column(row, width):
    lanes = jnp.broadcast_to(row, (128, row.shape[1])).T
    return jnp.concatenate([lanes] * (width // 128), axis=1)


def row_sums(values):
    half = values.shape[1] // 2
    return jnp.sum((values[:, :half] + values[:, half:]).T, axis=0, keepdims=True)


def step_scalars(step, sums, before):
    totals = jnp.sum(sums[...], axis=0)
    rz_now, curvature = totals[:1], totals[1:2]
    if step == 0:
        return rz_now, rz_now / curvature, None
    beta = rz_now / before[0:1]
    return rz_now, rz_now / (curvature - beta * rz_now / before[1:2]), beta


def even_place():
    return lax.rem(lax.axis_index("sub"), 2) == 0


def live_rows(counts, sub, rows, width):
    last = lax.axis_index("sub") == lax.axis_size("sub") - 1
    count = jnp.broadcast_to(counts[:, sub : sub + 1], (rows, width))
    if sub == counts.shape[1] - 1:
        count = jnp.where(last, 0, count)
    return (lax.broadcasted_iota(jnp.int32, (rows, width), 1) < count).astype(jnp.float32)


def early_kernel(counts, rhs, panel, coupling, live, own, partial, rest, near_out, far_out):
    subs, loads, width = own.shape
    parts = [None]
    for sub in range(subs):
        mask = live_rows(counts, sub, 1, width)
        live[sub] = mask
        own[sub] = mask * rhs[sub]
        parts.append(split(own[sub]))
    partial[...] = mul(parts[1][0], panel[0, width:]) + mul(parts[1][1], panel[0, width:])
    for sub in range(1, subs):
        high = jnp.concatenate([-parts[sub][0], parts[sub + 1][0]], axis=1)
        low = jnp.concatenate([-parts[sub][1], parts[sub + 1][1]], axis=1)
        rest[sub - 1] = mul(high, panel[sub]) + mul(low, panel[sub])
    to_next = [rest[subs - 2][:, width:], coupling[subs - 1, :, width:], own[subs - 1],
               jnp.broadcast_to(live[subs - 1], (8, width))]
    to_prev = [partial[:, :width], coupling[0, :, :width],
               panel[0, :width, :width].astype(jnp.float32), jnp.zeros((8, width), jnp.float32)]
    send(even_place(), to_next, to_prev, near_out, far_out)


def setup_kernel(*refs):
    group = (len(refs) - 5) // 2
    maps, (coarse, coupling) = refs[:group], refs[group : group + 2]
    picked, (stacked, lift, everyone) = refs[group + 2 : -3], refs[-3:]
    subs, corners = maps[0].shape
    rows, size = coarse.shape
    own = subs * corners
    grp = lax.axis_index("grp")
    for sub in range(subs):
        high, low = split(coupling[sub])
        spare = jnp.zeros((lift.shape[1] - 3 * corners, high.shape[1]), jnp.bfloat16)
        stacked[sub] = jnp.concatenate([high, low], axis=0)
        lift[sub] = jnp.concatenate([high, high, low, spare], axis=0)
    for distance in range(group):
        unknowns = [maps[distance][sub : sub + 1, :] for sub in range(subs)]
        everyone[distance] = jnp.concatenate(unknowns, axis=1)
    high, low = split(coarse[...])
    unknowns = lax.broadcasted_iota(jnp.int32, (size, own), 0)
    columns = []
    for member in range(group):
        chosen = (unknowns == everyone[grp ^ member]).astype(jnp.bfloat16)
        columns.append(mul(high, chosen) + mul(low, chosen))
    high, low = split(jnp.concatenate(columns, axis=1))
    owned = lax.broadcasted_iota(jnp.int32, (rows, own), 0) + grp * rows
    dims = (((0,), (0,)), ((), ()))
    for distance in range(group):
        chosen = (owned == everyone[distance]).astype(jnp.bfloat16)
        picked[distance][...] = lax.dot_general(
            chosen, high, dims, preferred_element_type=jnp.float32
        ) + lax.dot_general(chosen, low, dims, preferred_element_type=jnp.float32)


def corner_kernel(partial, rest, near, far, live_own, residual_own, panel, coupling,
                  live_edge, residual_edge, edge, own, corners):
    even = even_place()
    subs, rows = coupling.shape[0], coupling.shape[1] // 2
    loads, width = residual_edge.shape
    start = loads + rows
    completing = received(even, near, far, start, loads + 8)
    halo, block = completing[:loads], completing[loads + 8 : 2 * loads + 8].astype(jnp.bfloat16)
    live_edge[...] = completing[loads : loads + 1]
    residual_edge[...] = halo
    live, edges = Joined(live_edge, live_own), Joined(edge, own)
    faces = received(even, near, far, 0, loads)
    high, low = split(halo)
    first = partial[...] - mul(high, panel[0, :width]) - mul(low, panel[0, :width])
    high, low = split(residual_own[subs - 1])
    following = faces[loads:] - mul(high, block) - mul(low, block)
    results = [first] + [rest[sub] for sub in range(subs - 1)]
    right = [faces[:loads]] + [result[:, width:] for result in results]
    left = [result[:, :width] for result in results] + [following]
    parts = []
    for place in range(subs + 1):
        edges[place] = 0.25 * live[place] * (right[place] - left[place])
        parts.append(split(edges[place]))
    for sub in range(subs):
        high = jnp.concatenate([-parts[sub][0], parts[sub + 1][0]], axis=1)
        low = jnp.concatenate([-parts[sub][1], parts[sub + 1][1]], axis=1)
        both = mul_rows(coupling[sub], high)
        corners[sub * rows : (sub + 1) * rows, :] = (
            both[:rows] + both[rows:] + mul_rows(coupling[sub, :rows], low)
        )


def operators_kernel(coupling, live_edge, live_own, near, far, panel,
                     taken, ends, for_next, for_prev, given):
    even = even_place()
    subs, rows = coupling.shape[0], coupling.shape[1]
    width = coupling.shape[2] // 2
    live = Joined(live_edge, live_own)
    sides = received(even, near, far, panel.shape[1] // 2, rows)
    before, after = sides[:rows], sides[rows:]
    left = [coupling[sub, :, :width] * (0.25 * live[sub]) for sub in range(subs)]
    left.append(after * (0.25 * live[subs]))
    right = [before * (0.25 * live[0])]
    right += [coupling[sub, :, width:] * (0.25 * live[sub + 1]) for sub in range(subs)]
    none = jnp.zeros((rows, width), jnp.float32)
    inner, ahead, behind = [], [], []
    for sub in range(subs):
        factors = jnp.concatenate(
            [
                jnp.concatenate([left[sub], right[sub + 1]], axis=1),
                jnp.concatenate([none, left[sub + 1]], axis=1),
                jnp.concatenate([right[sub], none], axis=1),
            ],
            axis=0,
        )
        both = mul(jnp.concatenate(split(factors), axis=0), panel[sub])
        product = both[: 3 * rows] + both[3 * rows :]
        inner.append(product[:rows])
        ahead.append(product[rows : 2 * rows])
        behind.append(product[2 * rows :])
    total = subs * rows
    for sub in range(subs):
        blocks = [none] * (subs + 1)
        blocks[sub] = -inner[sub][:, :width]
        blocks[sub + 1] = inner[sub][:, width:]
        if sub > 0:
            blocks[sub - 1] = ahead[sub - 1][:, :width]
            blocks[sub] = blocks[sub] - ahead[sub - 1][:, width:]
        if sub + 1 < subs:
            blocks[sub + 1] = blocks[sub + 1] + behind[sub + 1][:, :width]
            blocks[sub + 2] = -behind[sub + 1][:, width:]
        if sub == 0:
            ends[0] = blocks[0]
            blocks[0] = none
        if sub == subs - 1:
            ends[1] = blocks[subs]
            blocks[subs] = none
        high, low = split(jnp.concatenate(blocks, axis=1))
        taken[sub * rows : (sub + 1) * rows, :] = high
        taken[total + sub * rows : total + (sub + 1) * rows, :] = low
    for_next[...] = jnp.concatenate(split(ahead[subs - 1][:, :width]), axis=0)
    for_prev[...] = jnp.concatenate(split(-behind[0][:, width:]), axis=0)
    given[0] = -ahead[subs - 1][:, width:]
    given[1] = behind[0][:, :width]


def early_corner_kernel(taken, ends, outside, edge, own, corners):
    subs, rows = own.shape[0], ends.shape[1]
    total = subs * rows
    edges = Joined(edge, own)
    parts = [split(edges[place]) for place in range(subs + 1)]
    high = jnp.concatenate([part[0] for part in parts], axis=1)
    low = jnp.concatenate([part[1] for part in parts], axis=1)
    both = mul_rows(taken[...], high)
    values = both[:total] + both[total:] + mul_rows(taken[:total], low)
    corners[...] = values
    for end, place in ((0, 0), (1, subs)):
        operator = jnp.concatenate(split(ends[end]), axis=0)
        row = end * (total - rows)
        corners[row : row + rows, :] = (
            values[row : row + rows]
            + outer_rows(operator, edges[place])
            + outside[end * rows : (end + 1) * rows, :]
        )


def dual_products(edges, residual, panel, everyone, block, lift, result, sums):
    subs, width = panel.shape[0], panel.shape[1] // 2
    rows = block.shape[0] // 2
    high, low = split(everyone[...])
    both = mul(block[...], high)
    back = both[:rows] + both[rows:] + mul(block[:rows], low)
    corners = rows // subs

    def lifted(sub):
        own = back[sub * corners : (sub + 1) * corners]
        own_high = own.astype(jnp.bfloat16).astype(jnp.float32)
        terms = [own_high, own - own_high, own_high]
        spare = jnp.zeros((lift.shape[1] - 3 * corners, own.shape[1]), jnp.float32)
        return mul(jnp.concatenate(terms + [spare], axis=0).T.astype(jnp.bfloat16), lift[sub])

    parts = [split(edges[place]) for place in range(subs + 1)]
    panel_products(parts, panel, result, lifted)
    product = curvature = 0.0
    for sub in range(subs):
        product = product + residual[sub] * edges[sub + 1]
        curvature = curvature + (
            result[sub][:, width:] * edges[sub + 1] - result[sub][:, :width] * edges[sub]
        )
    sums[...] = jnp.concatenate([row_sums(product), row_sums(curvature)], axis=0)


def send_dual(result, live_own, subs, for_next, for_prev, near_out, far_out, residual=None,
              given=None):
    even = even_place()
    width = near_out.shape[1]
    to_next, to_prev = [result[subs - 1][:, width:]], [result[0][:, :width]]
    if given is not None:
        to_next += [given[0], outer_rows(for_next, residual[subs - 2])]
        to_prev += [given[1], outer_rows(for_prev, residual[0])]
    upper = live_own[subs - 2] * (result[subs - 2][:, width:] - result[subs - 1][:, :width])
    lower = live_own[0] * (result[0][:, width:] - result[1][:, :width])
    to_next.append(outer_rows(for_next, upper))
    to_prev.append(outer_rows(for_prev, lower))
    send(even, to_next, to_prev, near_out, far_out)


def first_dual_kernel(edge, own, residual, panel, everyone, block, lift, live_own,
                      for_next, for_prev, given, first, rest, near_out, far_out, sums):
    result = Joined(first, rest)
    dual_products(Joined(edge, own), residual, panel, everyone, block, lift, result, sums)
    send_dual(result, live_own, panel.shape[0], for_next, for_prev, near_out, far_out,
              residual, given)


def dual_kernel(last, *refs):
    first, rest, near, far, live_edge, live_own = refs[:6]
    residual, panel, everyone, block, lift = refs[6:11]
    even, subs = even_place(), panel.shape[0]
    before, live = Joined(first, rest), Joined(live_edge, live_own)
    edges = [
        0.25 * jump_edge(even, before, near, far, live, place, subs) for place in range(subs + 1)
    ]
    if last:
        own, first_new, rest_new, face, sums = refs[11:]
    else:
        for_next, for_prev, own, first_new, rest_new, near_out, far_out, sums = refs[11:]
    for sub in range(subs):
        own[sub] = edges[sub + 1]
    result = Joined(first_new, rest_new)
    dual_products(edges, residual, panel, everyone, block, lift, result, sums)
    if last:
        face[...] = result[0][:, : face.shape[1]]
    else:
        send_dual(result, live_own, subs, for_next, for_prev, near_out, far_out)


def received(even, near, far, start, rows):
    part = slice(start, start + rows)
    return jnp.concatenate(
        [jnp.where(even, far[part], near[part]), jnp.where(even, near[part], far[part])], axis=0
    )


def first_update_kernel(first, rest, near, far, live_first, live_rest, sums,
                        residual_edge, residual_own, panel, ends,
                        image_own, image_edge, new_edge, new_own, first_new, rest_new,
                        near_out, far_out, scalars, full_ends, outside_image, outside):
    even = even_place()
    loads, width = residual_edge.shape
    subs, rows = panel.shape[0], ends.shape[1]
    result, live = Joined(first, rest), Joined(live_first, live_rest)
    residual, image = Joined(residual_edge, residual_own), Joined(image_edge, image_own)
    residual_new, result_new = Joined(new_edge, new_own), Joined(first_new, rest_new)
    rz_now, alpha, _ = step_scalars(0, sums, None)
    scalars[...] = jnp.concatenate([rz_now, alpha], axis=0)
    operators = received(even, near, far, loads, rows)
    full_ends[0] = ends[0] + operators[:rows]
    full_ends[1] = ends[1] + operators[rows:]
    values = received(even, near, far, loads + 2 * rows, rows)
    outside_image[...] = values
    outside[...] = received(even, near, far, loads + rows, rows) - alpha * values
    alpha_column = column(alpha, width)
    parts = []
    for place in range(subs + 1):
        value = jump_edge(even, result, near, far, live, place, subs)
        image[place] = value
        residual_new[place] = residual[place] - alpha_column * value
        parts.append(split(residual_new[place]))
    panel_products(parts, panel, result_new)
    send_faces(even, result_new[0], result_new[subs - 1], near_out, far_out)


def update_kernel(first, rest, near, far, live_first, live_rest, sums, before,
                  old_edge, old_own, residual_edge, residual_own, panel,
                  outside_image_old, outside_old,
                  image_own, new_edge, new_own, first_new, rest_new,
                  near_out, far_out, scalars, outside):
    even = even_place()
    loads, width = residual_edge.shape
    subs, rows = panel.shape[0], outside.shape[0] // 2
    result, live = Joined(first, rest), Joined(live_first, live_rest)
    image_old, residual = Joined(old_edge, old_own), Joined(residual_edge, residual_own)
    residual_new, result_new = Joined(new_edge, new_own), Joined(first_new, rest_new)
    rz_now, alpha, beta = step_scalars(1, sums, before)
    scalars[...] = jnp.concatenate([rz_now, alpha], axis=0)
    values = received(even, near, far, loads, rows) + beta * outside_image_old[...]
    outside[...] = outside_old[...] - alpha * values
    alpha_column, beta_column = column(alpha, width), column(beta, width)
    parts = []
    for place in range(subs + 1):
        value = jump_edge(even, result, near, far, live, place, subs)
        value = value + beta_column * image_old[place]
        if place > 0:
            image_own[place - 1] = value
        residual_new[place] = residual[place] - alpha_column * value
        parts.append(split(residual_new[place]))
    panel_products(parts, panel, result_new)
    send_faces(even, result_new[0], result_new[subs - 1], near_out, far_out)


def last_kernel(first, rest, following, live, sums, before, older, image_old,
                residual, first_z, second_z, third_z, multipliers, residual_new):
    subs, width = residual.shape[0], following.shape[1]
    result = Joined(first, rest)
    rz_now, alpha, beta = step_scalars(2, sums, before)
    beta_before = before[0:1] / older[0:1]
    on_second = before[1:2] + alpha * beta
    on_first = older[1:2] + on_second * beta_before
    alpha_column, beta_column = column(alpha, width), column(beta, width)
    second_column, first_column = column(on_second, width), column(on_first, width)
    for sub in range(subs):
        left = following[...] if sub == subs - 1 else result[sub + 1][:, :width]
        image = live[sub] * (result[sub][:, width:] - left) + beta_column * image_old[sub]
        residual_new[sub] = residual[sub] - alpha_column * image
        multipliers[sub] = (
            first_column * first_z[sub]
            + second_column * second_z[sub]
            + alpha_column * third_z[sub]
        )


def neighbour_pairs(size, first):
    pairs = [(i, i + 1) for i in range(first, size - 1, 2)]
    return [route for a, b in pairs for route in ((a, b), (b, a))]


def swap(near, far):
    size = lax.axis_size("sub")
    return (
        lax.ppermute(near, "sub", neighbour_pairs(size, 0)),
        lax.ppermute(far, "sub", neighbour_pairs(size, 1)),
    )


def from_all(rows):
    size = lax.axis_size("sub") * lax.axis_size("grp")
    copies = jnp.broadcast_to(rows[None], (size,) + rows.shape)
    return lax.all_to_all(copies, ("sub", "grp"), 0, 0)


def from_group(values):
    group = lax.axis_size("grp")
    received = [values]
    for distance in range(1, group):
        routes = [(i, i ^ distance) for i in range(group)]
        received.append(lax.ppermute(values, "grp", routes))
    return received


def swap_blocks(picked):
    group = lax.axis_size("grp")
    block = picked[0]
    for distance in range(1, group):
        routes = [(i, i ^ distance) for i in range(group)]
        block = block + lax.ppermute(picked[distance], "grp", routes)
    return block


def local(rhs, counts, solve_panel, dirichlet_panel, coupling, corner_map, coarse_inverse):
    subs, loads, width = rhs.shape[1:]
    corners = coupling.shape[2]
    solve, dirichlet = solve_panel[0], dirichlet_panel[0]
    size = lax.axis_size("sub")

    face_shape, own_shape = (loads, width), (subs, loads, width)
    first_shape, rest_shape = (loads, 2 * width), (subs - 1, loads, 2 * width)
    scalars_shape, outside_shape, side_shape = (2, loads), (2 * corners, loads), (corners, width)
    long_shape, longer_shape = (loads + corners, width), (loads + 3 * corners, width)
    begin_shape = (2 * loads + corners + 8, width)
    edges_shapes = [face_shape, own_shape]
    result_shapes = [first_shape, rest_shape, face_shape, face_shape]

    live_own, residual_own, partial, rest, near, far = call(
        early_kernel,
        [(subs, 1, width), own_shape, first_shape, rest_shape, begin_shape, begin_shape],
        counts, rhs[0], dirichlet, coupling[0],
    )
    near, far, corner_map, coarse = lax.optimization_barrier(
        (near, far, corner_map, coarse_inverse[0])
    )
    near, far = swap(near, far)
    maps = from_group(corner_map[0])
    group, own = len(maps), subs * corners
    pair = [(corners, width)] * 2
    *picked, stacked, lift = call(
        setup_kernel,
        [(own, group * own)] * group
        + [(subs, 2 * corners, 2 * width), (subs, 3 * corners + -3 * corners % 128, 2 * width)],
        *maps, coarse, coupling[0],
        kinds=[jnp.float32] * group + [jnp.bfloat16] * 2,
        scratch=[pltpu.VMEM((group, 1, own), jnp.int32)],
    )
    block = jnp.concatenate(split_outside(swap_blocks(picked)), axis=0)
    live_edge, residual_edge, edge, first_z, values = call(
        corner_kernel,
        [(1, width), face_shape] + edges_shapes + [(own, loads)],
        partial, rest, near, far, live_own, residual_own, dirichlet, stacked,
    )
    live, residual = (live_edge, live_own), (residual_edge, residual_own)
    taken, ends, for_next, for_prev, given = call(
        operators_kernel,
        [(2 * own, (subs + 1) * width), (2,) + side_shape, (2 * corners, width),
         (2 * corners, width), (2,) + side_shape],
        coupling[0], *live, near, far, dirichlet,
        kinds=[jnp.bfloat16, jnp.float32, jnp.bfloat16, jnp.bfloat16, jnp.float32],
    )
    everyone = lax.all_gather(values, "grp", tiled=True)
    first, rest, near, far, sums = call(
        first_dual_kernel,
        [first_shape, rest_shape, longer_shape, longer_shape, scalars_shape],
        edge, first_z, residual[1], solve, everyone, block, lift, live[1],
        for_next, for_prev, given,
    )
    sums = from_all(sums)
    near, far = swap(near, far)
    (image_own, image_edge, *residual, first, rest, near, far, scalars_first, ends, outside_image,
     outside) = call(
        first_update_kernel,
        [own_shape, face_shape] + edges_shapes + result_shapes
        + [scalars_shape, (2,) + side_shape, outside_shape, outside_shape],
        first, rest, near, far, *live, sums, *residual, dirichlet, ends,
    )

    near, far = swap(near, far)
    (values,) = call(early_corner_kernel, [(own, loads)], taken, ends, outside, *residual)
    everyone = lax.all_gather(values, "grp", tiled=True)
    second_z, first, rest, near, far, sums = call(
        functools.partial(dual_kernel, False),
        [own_shape, first_shape, rest_shape, long_shape, long_shape, scalars_shape],
        first, rest, near, far, *live, residual[1], solve, everyone, block, lift,
        for_next, for_prev,
    )
    sums = from_all(sums)
    near, far = swap(near, far)
    image_own, *residual, first, rest, near, far, scalars_second, outside = call(
        update_kernel,
        [own_shape] + edges_shapes + result_shapes + [scalars_shape, outside_shape],
        first, rest, near, far, *live, sums, scalars_first, image_edge, image_own, *residual,
        dirichlet, outside_image, outside,
    )

    near, far = swap(near, far)
    (values,) = call(early_corner_kernel, [(own, loads)], taken, ends, outside, *residual)
    everyone = lax.all_gather(values, "grp", tiled=True)
    third_z, first, rest, face, sums = call(
        functools.partial(dual_kernel, True),
        [own_shape, first_shape, rest_shape, face_shape, scalars_shape],
        first, rest, near, far, *live, residual[1], solve, everyone, block, lift,
    )
    sums = from_all(sums)
    following = lax.ppermute(face, "sub", [(i + 1, i) for i in range(size - 1)])
    multipliers, residual = call(
        last_kernel,
        [own_shape] * 2,
        first, rest, following, live[1], sums, scalars_second, scalars_first,
        image_own, residual[1], first_z, second_z, third_z,
    )
    return (multipliers[None], residual[None])


def solution(mesh):
    return jax.shard_map(
        local,
        mesh=mesh,
        in_specs=(
            P("grp", "sub", None, None),
            P("grp", "sub"),
            P("grp", "sub", None, None),
            P("grp", "sub", None, None),
            P("grp", "sub", None, None),
            P("grp", "sub", None),
            P("sub", "grp", None),
        ),
        out_specs=(P("grp", "sub", None, None), P("grp", "sub", None, None)),
        check_vma=False,
    )
```

```python
import functools

import jax
import jax.numpy as jnp
from jax import lax
from jax.experimental import pallas as pl
from jax.experimental.pallas import tpu as pltpu
from jax.sharding import PartitionSpec as P

VMEM_LIMIT = 8 * 1024 * 1024
TAIL_LIMIT = 62 * 1024 * 1024


def split(values):
    high = values.astype(jnp.bfloat16)
    return high, (values - high.astype(jnp.float32)).astype(jnp.bfloat16)


def split_outside(values):
    high = lax.reduce_precision(values, exponent_bits=8, mantissa_bits=7)
    return high.astype(jnp.bfloat16), (values - high).astype(jnp.bfloat16)


def mul(first, second):
    return jnp.dot(first, second, preferred_element_type=jnp.float32)


def mul_rows(first, second):
    dims = (((1,), (1,)), ((), ()))
    return lax.dot_general(first, second, dims, preferred_element_type=jnp.float32)


def call(kernel, out_shapes, *operands, kinds=None, scratch=(), place=pltpu.VMEM):
    kinds = kinds or [jnp.float32] * len(out_shapes)
    return pl.pallas_call(
        kernel,
        out_shape=[jax.ShapeDtypeStruct(*shape) for shape in zip(out_shapes, kinds)],
        in_specs=[pl.BlockSpec(memory_space=pltpu.VMEM)] * len(operands),
        out_specs=[pl.BlockSpec(memory_space=place)] * len(out_shapes),
        scratch_shapes=list(scratch),
        compiler_params=pltpu.CompilerParams(vmem_limit_bytes=VMEM_LIMIT),
    )(*operands)


class Joined:
    def __init__(self, first, rest):
        self.first, self.rest = first, rest

    def __getitem__(self, place):
        return self.first[...] if place == 0 else self.rest[place - 1]

    def __setitem__(self, place, value):
        if place == 0:
            self.first[...] = value
        else:
            self.rest[place - 1] = value


def jump_edge(even, result, near, far, live, edge, subs):
    loads, width = result[0].shape[0], near.shape[1]
    if edge == 0:
        right = jnp.where(even, far[:loads], near[:loads])
    else:
        right = result[edge - 1][:, width:]
    if edge == subs:
        left = jnp.where(even, near[:loads], far[:loads])
    else:
        left = result[edge][:, :width]
    return live[edge] * (right - left)


def outer_rows(operator, edge):
    rows = operator.shape[0] // 2
    high, low = split(edge)
    both = mul_rows(operator[...], high)
    return both[:rows] + both[rows:] + mul_rows(operator[:rows], low)


def send(even, to_next, to_prev, near_out, far_out):
    row = 0
    for ahead, behind in zip(to_next, to_prev):
        rows = slice(row, row + ahead.shape[0])
        near_out[rows, :] = jnp.where(even, ahead, behind)
        far_out[rows, :] = jnp.where(even, behind, ahead)
        row += ahead.shape[0]


def send_faces(even, first, last, near_out, far_out):
    width = first.shape[1] // 2
    send(even, [last[:, width:]], [first[:, :width]], near_out, far_out)


def panel_products(parts, panel, result, extra=None):
    subs = panel.shape[0]
    for sub in range(subs):
        high = jnp.concatenate([-parts[sub][0], parts[sub + 1][0]], axis=1)
        low = jnp.concatenate([-parts[sub][1], parts[sub + 1][1]], axis=1)
        total = mul(high, panel[sub]) + mul(low, panel[sub])
        if extra is not None:
            total = total + extra(sub)
        result[sub] = total


def column(row, width):
    lanes = jnp.broadcast_to(row, (128, row.shape[1])).T
    return jnp.concatenate([lanes] * (width // 128), axis=1)


def row_sums(values):
    half = values.shape[1] // 2
    return jnp.sum((values[:, :half] + values[:, half:]).T, axis=0, keepdims=True)


def step_scalars(step, sums, before):
    totals = jnp.sum(sums[...], axis=0)
    rz_now, curvature = totals[:1], totals[1:2]
    if step == 0:
        return rz_now, rz_now / curvature, None
    beta = rz_now / before[0:1]
    return rz_now, rz_now / (curvature - beta * rz_now / before[1:2]), beta


def even_place():
    return lax.rem(lax.axis_index("sub"), 2) == 0


def live_rows(counts, sub, rows, width):
    last = lax.axis_index("sub") == lax.axis_size("sub") - 1
    count = jnp.broadcast_to(counts[:, sub : sub + 1], (rows, width))
    if sub == counts.shape[1] - 1:
        count = jnp.where(last, 0, count)
    return (lax.broadcasted_iota(jnp.int32, (rows, width), 1) < count).astype(jnp.float32)


def tail_kernel(counts_ref, rhs, tail, counts, face, counts_done, face_done):
    loads, width = rhs.shape[2:]
    counts_copy = pltpu.make_async_copy(counts_ref, counts, counts_done)
    face_copy = pltpu.make_async_copy(rhs.at[0, rhs.shape[1] - 1], face, face_done)
    counts_copy.start()
    face_copy.start()
    counts_copy.wait()
    mask = live_rows(counts, counts.shape[1] - 1, 8, width)
    tail[loads:] = mask
    face_copy.wait()
    tail[:loads] = mask[:1] * face[...]


def early_kernel(counts, rhs, panel, live, own, partial, rest):
    subs, loads, width = own.shape
    parts = [None]
    for sub in range(subs):
        mask = live_rows(counts, sub, 1, width)
        live[sub] = mask
        own[sub] = mask * rhs[sub]
        parts.append(split(own[sub]))
    partial[...] = mul(parts[1][0], panel[0, width:]) + mul(parts[1][1], panel[0, width:])
    for sub in range(1, subs):
        high = jnp.concatenate([-parts[sub][0], parts[sub + 1][0]], axis=1)
        low = jnp.concatenate([-parts[sub][1], parts[sub + 1][1]], axis=1)
        rest[sub - 1] = mul(high, panel[sub]) + mul(low, panel[sub])


def head_kernel(head, partial, rest, panel, coupling, live, edge, first, near_out, far_out):
    loads, width = edge.shape
    live[...] = head[loads : loads + 1]
    edge[...] = head[:loads]
    high, low = split(head[:loads])
    first[...] = partial[...] - mul(high, panel[0, :width]) - mul(low, panel[0, :width])
    last = rest[rest.shape[0] - 1]
    to_next = [last[:, width:], coupling[coupling.shape[0] - 1, :, width:]]
    send(even_place(), to_next, [first[:, :width], coupling[0, :, :width]], near_out, far_out)


def setup_kernel(*refs):
    group = (len(refs) - 5) // 2
    maps, (coarse, coupling) = refs[:group], refs[group : group + 2]
    picked, (stacked, lift, everyone) = refs[group + 2 : -3], refs[-3:]
    subs, corners = maps[0].shape
    rows, size = coarse.shape
    own = subs * corners
    grp = lax.axis_index("grp")
    for sub in range(subs):
        high, low = split(coupling[sub])
        spare = jnp.zeros((lift.shape[1] - 3 * corners, high.shape[1]), jnp.bfloat16)
        stacked[sub] = jnp.concatenate([high, low], axis=0)
        lift[sub] = jnp.concatenate([high, high, low, spare], axis=0)
    for distance in range(group):
        unknowns = [maps[distance][sub : sub + 1, :] for sub in range(subs)]
        everyone[distance] = jnp.concatenate(unknowns, axis=1)
    high, low = split(coarse[...])
    unknowns = lax.broadcasted_iota(jnp.int32, (size, own), 0)
    columns = []
    for member in range(group):
        chosen = (unknowns == everyone[grp ^ member]).astype(jnp.bfloat16)
        columns.append(mul(high, chosen) + mul(low, chosen))
    high, low = split(jnp.concatenate(columns, axis=1))
    owned = lax.broadcasted_iota(jnp.int32, (rows, own), 0) + grp * rows
    dims = (((0,), (0,)), ((), ()))
    for distance in range(group):
        chosen = (owned == everyone[distance]).astype(jnp.bfloat16)
        picked[distance][...] = lax.dot_general(
            chosen, high, dims, preferred_element_type=jnp.float32
        ) + lax.dot_general(chosen, low, dims, preferred_element_type=jnp.float32)


def corner_kernel(first, rest, near, far, live_first, live_rest, coupling, _solve,
                  edge, own, corners):
    even = even_place()
    subs, rows = coupling.shape[0], coupling.shape[1] // 2
    result, live, edges = Joined(first, rest), Joined(live_first, live_rest), Joined(edge, own)
    parts = []
    for place in range(subs + 1):
        edges[place] = 0.25 * jump_edge(even, result, near, far, live, place, subs)
        parts.append(split(edges[place]))
    for sub in range(subs):
        high = jnp.concatenate([-parts[sub][0], parts[sub + 1][0]], axis=1)
        low = jnp.concatenate([-parts[sub][1], parts[sub + 1][1]], axis=1)
        both = mul_rows(coupling[sub], high)
        corners[sub * rows : (sub + 1) * rows, :] = (
            both[:rows] + both[rows:] + mul_rows(coupling[sub, :rows], low)
        )


def operators_kernel(coupling, live_edge, live_own, near, far, panel,
                     taken, ends, for_next, for_prev, given):
    even = even_place()
    subs, rows = coupling.shape[0], coupling.shape[1]
    width = coupling.shape[2] // 2
    live = Joined(live_edge, live_own)
    sides = received(even, near, far, near.shape[0] - rows, rows)
    before, after = sides[:rows], sides[rows:]
    left = [coupling[sub, :, :width] * (0.25 * live[sub]) for sub in range(subs)]
    left.append(after * (0.25 * live[subs]))
    right = [before * (0.25 * live[0])]
    right += [coupling[sub, :, width:] * (0.25 * live[sub + 1]) for sub in range(subs)]
    none = jnp.zeros((rows, width), jnp.float32)
    inner, ahead, behind = [], [], []
    for sub in range(subs):
        factors = jnp.concatenate(
            [
                jnp.concatenate([left[sub], right[sub + 1]], axis=1),
                jnp.concatenate([none, left[sub + 1]], axis=1),
                jnp.concatenate([right[sub], none], axis=1),
            ],
            axis=0,
        )
        both = mul(jnp.concatenate(split(factors), axis=0), panel[sub])
        product = both[: 3 * rows] + both[3 * rows :]
        inner.append(product[:rows])
        ahead.append(product[rows : 2 * rows])
        behind.append(product[2 * rows :])
    total = subs * rows
    for sub in range(subs):
        blocks = [none] * (subs + 1)
        blocks[sub] = -inner[sub][:, :width]
        blocks[sub + 1] = inner[sub][:, width:]
        if sub > 0:
            blocks[sub - 1] = ahead[sub - 1][:, :width]
            blocks[sub] = blocks[sub] - ahead[sub - 1][:, width:]
        if sub + 1 < subs:
            blocks[sub + 1] = blocks[sub + 1] + behind[sub + 1][:, :width]
            blocks[sub + 2] = -behind[sub + 1][:, width:]
        if sub == 0:
            ends[0] = blocks[0]
            blocks[0] = none
        if sub == subs - 1:
            ends[1] = blocks[subs]
            blocks[subs] = none
        high, low = split(jnp.concatenate(blocks, axis=1))
        taken[sub * rows : (sub + 1) * rows, :] = high
        taken[total + sub * rows : total + (sub + 1) * rows, :] = low
    for_next[...] = jnp.concatenate(split(ahead[subs - 1][:, :width]), axis=0)
    for_prev[...] = jnp.concatenate(split(-behind[0][:, width:]), axis=0)
    given[0] = -ahead[subs - 1][:, width:]
    given[1] = behind[0][:, :width]


def early_corner_kernel(taken, ends, outside, edge, own, corners):
    subs, rows = own.shape[0], ends.shape[1]
    total = subs * rows
    edges = Joined(edge, own)
    parts = [split(edges[place]) for place in range(subs + 1)]
    high = jnp.concatenate([part[0] for part in parts], axis=1)
    low = jnp.concatenate([part[1] for part in parts], axis=1)
    both = mul_rows(taken[...], high)
    values = both[:total] + both[total:] + mul_rows(taken[:total], low)
    corners[...] = values
    for end, place in ((0, 0), (1, subs)):
        operator = jnp.concatenate(split(ends[end]), axis=0)
        row = end * (total - rows)
        corners[row : row + rows, :] = (
            values[row : row + rows]
            + outer_rows(operator, edges[place])
            + outside[end * rows : (end + 1) * rows, :]
        )


def dual_products(edges, residual, panel, everyone, block, lift, result, sums):
    subs, width = panel.shape[0], panel.shape[1] // 2
    rows = block.shape[0] // 2
    high, low = split(everyone[...])
    both = mul(block[...], high)
    back = both[:rows] + both[rows:] + mul(block[:rows], low)
    corners = rows // subs

    def lifted(sub):
        own = back[sub * corners : (sub + 1) * corners]
        own_high = own.astype(jnp.bfloat16).astype(jnp.float32)
        terms = [own_high, own - own_high, own_high]
        spare = jnp.zeros((lift.shape[1] - 3 * corners, own.shape[1]), jnp.float32)
        return mul(jnp.concatenate(terms + [spare], axis=0).T.astype(jnp.bfloat16), lift[sub])

    parts = [split(edges[place]) for place in range(subs + 1)]
    panel_products(parts, panel, result, lifted)
    product = curvature = 0.0
    for sub in range(subs):
        product = product + residual[sub] * edges[sub + 1]
        curvature = curvature + (
            result[sub][:, width:] * edges[sub + 1] - result[sub][:, :width] * edges[sub]
        )
    sums[...] = jnp.concatenate([row_sums(product), row_sums(curvature)], axis=0)


def send_dual(result, live_own, subs, for_next, for_prev, near_out, far_out, residual=None,
              given=None):
    even = even_place()
    width = near_out.shape[1]
    to_next, to_prev = [result[subs - 1][:, width:]], [result[0][:, :width]]
    if given is not None:
        to_next += [given[0], outer_rows(for_next, residual[subs - 2])]
        to_prev += [given[1], outer_rows(for_prev, residual[0])]
    upper = live_own[subs - 2] * (result[subs - 2][:, width:] - result[subs - 1][:, :width])
    lower = live_own[0] * (result[0][:, width:] - result[1][:, :width])
    to_next.append(outer_rows(for_next, upper))
    to_prev.append(outer_rows(for_prev, lower))
    send(even, to_next, to_prev, near_out, far_out)


def first_dual_kernel(edge, own, residual, panel, everyone, block, lift, live_own,
                      for_next, for_prev, given, first, rest, near_out, far_out, sums):
    result = Joined(first, rest)
    dual_products(Joined(edge, own), residual, panel, everyone, block, lift, result, sums)
    send_dual(result, live_own, panel.shape[0], for_next, for_prev, near_out, far_out,
              residual, given)


def dual_kernel(last, *refs):
    first, rest, near, far, live_edge, live_own = refs[:6]
    residual, panel, everyone, block, lift = refs[6:11]
    even, subs = even_place(), panel.shape[0]
    before, live = Joined(first, rest), Joined(live_edge, live_own)
    edges = [
        0.25 * jump_edge(even, before, near, far, live, place, subs) for place in range(subs + 1)
    ]
    if last:
        own, first_new, rest_new, face, sums = refs[11:]
    else:
        for_next, for_prev, own, first_new, rest_new, near_out, far_out, sums = refs[11:]
    for sub in range(subs):
        own[sub] = edges[sub + 1]
    result = Joined(first_new, rest_new)
    dual_products(edges, residual, panel, everyone, block, lift, result, sums)
    if last:
        face[...] = result[0][:, : face.shape[1]]
    else:
        send_dual(result, live_own, subs, for_next, for_prev, near_out, far_out)


def received(even, near, far, start, rows):
    part = slice(start, start + rows)
    return jnp.concatenate(
        [jnp.where(even, far[part], near[part]), jnp.where(even, near[part], far[part])], axis=0
    )


def first_update_kernel(first, rest, near, far, live_first, live_rest, sums,
                        residual_edge, residual_own, panel, ends,
                        image_own, image_edge, new_edge, new_own, first_new, rest_new,
                        near_out, far_out, scalars, full_ends, outside_image, outside):
    even = even_place()
    loads, width = residual_edge.shape
    subs, rows = panel.shape[0], ends.shape[1]
    result, live = Joined(first, rest), Joined(live_first, live_rest)
    residual, image = Joined(residual_edge, residual_own), Joined(image_edge, image_own)
    residual_new, result_new = Joined(new_edge, new_own), Joined(first_new, rest_new)
    rz_now, alpha, _ = step_scalars(0, sums, None)
    scalars[...] = jnp.concatenate([rz_now, alpha], axis=0)
    operators = received(even, near, far, loads, rows)
    full_ends[0] = ends[0] + operators[:rows]
    full_ends[1] = ends[1] + operators[rows:]
    values = received(even, near, far, loads + 2 * rows, rows)
    outside_image[...] = values
    outside[...] = received(even, near, far, loads + rows, rows) - alpha * values
    alpha_column = column(alpha, width)
    parts = []
    for place in range(subs + 1):
        value = jump_edge(even, result, near, far, live, place, subs)
        image[place] = value
        residual_new[place] = residual[place] - alpha_column * value
        parts.append(split(residual_new[place]))
    panel_products(parts, panel, result_new)
    send_faces(even, result_new[0], result_new[subs - 1], near_out, far_out)


def update_kernel(first, rest, near, far, live_first, live_rest, sums, before,
                  old_edge, old_own, residual_edge, residual_own, panel,
                  outside_image_old, outside_old,
                  image_own, new_edge, new_own, first_new, rest_new,
                  near_out, far_out, scalars, outside):
    even = even_place()
    loads, width = residual_edge.shape
    subs, rows = panel.shape[0], outside.shape[0] // 2
    result, live = Joined(first, rest), Joined(live_first, live_rest)
    image_old, residual = Joined(old_edge, old_own), Joined(residual_edge, residual_own)
    residual_new, result_new = Joined(new_edge, new_own), Joined(first_new, rest_new)
    rz_now, alpha, beta = step_scalars(1, sums, before)
    scalars[...] = jnp.concatenate([rz_now, alpha], axis=0)
    values = received(even, near, far, loads, rows) + beta * outside_image_old[...]
    outside[...] = outside_old[...] - alpha * values
    alpha_column, beta_column = column(alpha, width), column(beta, width)
    parts = []
    for place in range(subs + 1):
        value = jump_edge(even, result, near, far, live, place, subs)
        value = value + beta_column * image_old[place]
        if place > 0:
            image_own[place - 1] = value
        residual_new[place] = residual[place] - alpha_column * value
        parts.append(split(residual_new[place]))
    panel_products(parts, panel, result_new)
    send_faces(even, result_new[0], result_new[subs - 1], near_out, far_out)


def last_kernel(first, rest, following, live, sums, before, older, image_old,
                residual, first_z, second_z, third_z, multipliers, residual_new,
                solution_slots, residual_slots, done):
    subs, width = residual.shape[0], following.shape[1]
    result = Joined(first, rest)
    rz_now, alpha, beta = step_scalars(2, sums, before)
    beta_before = before[0:1] / older[0:1]
    on_second = before[1:2] + alpha * beta
    on_first = older[1:2] + on_second * beta_before
    alpha_column, beta_column = column(alpha, width), column(beta, width)
    second_column, first_column = column(on_second, width), column(on_first, width)
    copies = []
    for sub in range(subs):
        left = following[...] if sub == subs - 1 else result[sub + 1][:, :width]
        image = live[sub] * (result[sub][:, width:] - left) + beta_column * image_old[sub]
        residual_slots[sub] = residual[sub] - alpha_column * image
        copies.append(
            pltpu.make_async_copy(residual_slots.at[sub], residual_new.at[sub], done.at[0, sub])
        )
        copies[-1].start()
        solution_slots[sub] = (
            first_column * first_z[sub]
            + second_column * second_z[sub]
            + alpha_column * third_z[sub]
        )
        copies.append(
            pltpu.make_async_copy(solution_slots.at[sub], multipliers.at[sub], done.at[1, sub])
        )
        copies[-1].start()
    for copy in copies:
        copy.wait()


def neighbour_pairs(size, first):
    pairs = [(i, i + 1) for i in range(first, size - 1, 2)]
    return [route for a, b in pairs for route in ((a, b), (b, a))]


def swap(near, far):
    size = lax.axis_size("sub")
    return (
        lax.ppermute(near, "sub", neighbour_pairs(size, 0)),
        lax.ppermute(far, "sub", neighbour_pairs(size, 1)),
    )


def from_all(rows):
    size = lax.axis_size("sub") * lax.axis_size("grp")
    copies = jnp.broadcast_to(rows[None], (size,) + rows.shape)
    return lax.all_to_all(copies, ("sub", "grp"), 0, 0)


def from_group(values):
    group = lax.axis_size("grp")
    received = [values]
    for distance in range(1, group):
        routes = [(i, i ^ distance) for i in range(group)]
        received.append(lax.ppermute(values, "grp", routes))
    return received


def swap_blocks(picked):
    group = lax.axis_size("grp")
    block = picked[0]
    for distance in range(1, group):
        routes = [(i, i ^ distance) for i in range(group)]
        block = block + lax.ppermute(picked[distance], "grp", routes)
    return block


def make_tail(counts, rhs):
    loads, width = rhs.shape[2:]
    return pl.pallas_call(
        tail_kernel,
        out_shape=jax.ShapeDtypeStruct((loads + 8, width), jnp.float32),
        in_specs=[
            pl.BlockSpec(memory_space=pltpu.HBM),
            pl.BlockSpec(memory_space=pltpu.HBM),
        ],
        out_specs=pl.BlockSpec(memory_space=pltpu.VMEM),
        scratch_shapes=[
            pltpu.VMEM(counts.shape, counts.dtype),
            pltpu.VMEM((loads, width), jnp.float32),
            pltpu.SemaphoreType.DMA,
            pltpu.SemaphoreType.DMA,
        ],
        compiler_params=pltpu.CompilerParams(vmem_limit_bytes=TAIL_LIMIT),
    )(counts, rhs)


def local(rhs, counts, solve_panel, dirichlet_panel, coupling, corner_map, coarse_inverse):
    subs, loads, width = rhs.shape[1:]
    corners = coupling.shape[2]
    solve, dirichlet = solve_panel[0], dirichlet_panel[0]
    size = lax.axis_size("sub")

    face_shape, own_shape = (loads, width), (subs, loads, width)
    first_shape, rest_shape = (loads, 2 * width), (subs - 1, loads, 2 * width)
    scalars_shape, outside_shape, side_shape = (2, loads), (2 * corners, loads), (corners, width)
    long_shape, longer_shape = (loads + corners, width), (loads + 3 * corners, width)
    edges_shapes = [face_shape, own_shape]
    result_shapes = [first_shape, rest_shape, face_shape, face_shape]

    tail = make_tail(counts, rhs)
    tail, counts, corner_map = lax.optimization_barrier((tail, counts, corner_map))
    head = lax.ppermute(tail, "sub", [(i, i + 1) for i in range(size - 1)])
    maps = from_group(corner_map[0])
    live_own, residual_own, partial, rest = call(
        early_kernel,
        [(subs, 1, width), own_shape, first_shape, rest_shape],
        counts, rhs[0], dirichlet,
    )
    live_edge, residual_edge, first, near, far = call(
        head_kernel,
        [(1, width), face_shape, first_shape, long_shape, long_shape],
        head, partial, rest, dirichlet, coupling[0],
    )
    near, far, maps, coarse = lax.optimization_barrier((near, far, maps, coarse_inverse[0]))
    near, far = swap(near, far)
    group, own = len(maps), subs * corners
    pair = [(corners, width)] * 2
    *picked, stacked, lift = call(
        setup_kernel,
        [(own, group * own)] * group
        + [(subs, 2 * corners, 2 * width), (subs, 3 * corners + -3 * corners % 128, 2 * width)],
        *maps, coarse, coupling[0],
        kinds=[jnp.float32] * group + [jnp.bfloat16] * 2,
        scratch=[pltpu.VMEM((group, 1, own), jnp.int32)],
    )
    block = jnp.concatenate(split_outside(swap_blocks(picked)), axis=0)
    live, residual = (live_edge, live_own), (residual_edge, residual_own)
    taken, ends, for_next, for_prev, given = call(
        operators_kernel,
        [(2 * own, (subs + 1) * width), (2,) + side_shape, (2 * corners, width),
         (2 * corners, width), (2,) + side_shape],
        coupling[0], *live, near, far, dirichlet,
        kinds=[jnp.bfloat16, jnp.float32, jnp.bfloat16, jnp.bfloat16, jnp.float32],
    )

    edge, first_z, values = call(
        corner_kernel,
        edges_shapes + [(own, loads)],
        first, rest, near, far, *live, stacked, solve,
    )
    everyone = lax.all_gather(values, "grp", tiled=True)
    first, rest, near, far, sums = call(
        first_dual_kernel,
        [first_shape, rest_shape, longer_shape, longer_shape, scalars_shape],
        edge, first_z, residual[1], solve, everyone, block, lift, live[1],
        for_next, for_prev, given,
    )
    sums = from_all(sums)
    near, far = swap(near, far)
    (image_own, image_edge, *residual, first, rest, near, far, scalars_first, ends, outside_image,
     outside) = call(
        first_update_kernel,
        [own_shape, face_shape] + edges_shapes + result_shapes
        + [scalars_shape, (2,) + side_shape, outside_shape, outside_shape],
        first, rest, near, far, *live, sums, *residual, dirichlet, ends,
    )

    near, far = swap(near, far)
    (values,) = call(early_corner_kernel, [(own, loads)], taken, ends, outside, *residual)
    everyone = lax.all_gather(values, "grp", tiled=True)
    second_z, first, rest, near, far, sums = call(
        functools.partial(dual_kernel, False),
        [own_shape, first_shape, rest_shape, long_shape, long_shape, scalars_shape],
        first, rest, near, far, *live, residual[1], solve, everyone, block, lift,
        for_next, for_prev,
    )
    sums = from_all(sums)
    near, far = swap(near, far)
    image_own, *residual, first, rest, near, far, scalars_second, outside = call(
        update_kernel,
        [own_shape] + edges_shapes + result_shapes + [scalars_shape, outside_shape],
        first, rest, near, far, *live, sums, scalars_first, image_edge, image_own, *residual,
        dirichlet, outside_image, outside,
    )

    near, far = swap(near, far)
    (values,) = call(early_corner_kernel, [(own, loads)], taken, ends, outside, *residual)
    everyone = lax.all_gather(values, "grp", tiled=True)
    third_z, first, rest, face, sums = call(
        functools.partial(dual_kernel, True),
        [own_shape, first_shape, rest_shape, face_shape, scalars_shape],
        first, rest, near, far, *live, residual[1], solve, everyone, block, lift,
    )
    sums = from_all(sums)
    following = lax.ppermute(face, "sub", [(i + 1, i) for i in range(size - 1)])
    multipliers, residual = call(
        last_kernel,
        [own_shape] * 2,
        first, rest, following, live[1], sums, scalars_second, scalars_first,
        image_own, residual[1], first_z, second_z, third_z,
        scratch=[pltpu.VMEM(own_shape, jnp.float32)] * 2 + [pltpu.SemaphoreType.DMA((2, subs))],
        place=pltpu.HBM,
    )
    return (multipliers[None], residual[None])


def solution(mesh):
    return jax.shard_map(
        local,
        mesh=mesh,
        in_specs=(
            P("grp", "sub", None, None),
            P("grp", "sub"),
            P("grp", "sub", None, None),
            P("grp", "sub", None, None),
            P("grp", "sub", None, None),
            P("grp", "sub", None),
            P("sub", "grp", None),
        ),
        out_specs=(P("grp", "sub", None, None), P("grp", "sub", None, None)),
        check_vma=False,
    )
```

```python
import functools

import jax
import jax.numpy as jnp
from jax import lax
from jax.experimental import pallas as pl
from jax.experimental.pallas import tpu as pltpu
from jax.sharding import PartitionSpec as P

VMEM_LIMIT = 8 * 1024 * 1024
TAIL_LIMIT = 62 * 1024 * 1024


def split(values):
    high = values.astype(jnp.bfloat16)
    return high, (values - high.astype(jnp.float32)).astype(jnp.bfloat16)


def split_outside(values):
    high = lax.reduce_precision(values, exponent_bits=8, mantissa_bits=7)
    return high.astype(jnp.bfloat16), (values - high).astype(jnp.bfloat16)


def mul(first, second):
    return jnp.dot(first, second, preferred_element_type=jnp.float32)


def mul_rows(first, second):
    dims = (((1,), (1,)), ((), ()))
    return lax.dot_general(first, second, dims, preferred_element_type=jnp.float32)


def call(kernel, out_shapes, *operands, kinds=None, scratch=()):
    kinds = kinds or [jnp.float32] * len(out_shapes)
    return pl.pallas_call(
        kernel,
        out_shape=[jax.ShapeDtypeStruct(*shape) for shape in zip(out_shapes, kinds)],
        in_specs=[pl.BlockSpec(memory_space=pltpu.VMEM)] * len(operands),
        out_specs=[pl.BlockSpec(memory_space=pltpu.VMEM)] * len(out_shapes),
        scratch_shapes=list(scratch),
        compiler_params=pltpu.CompilerParams(vmem_limit_bytes=VMEM_LIMIT),
    )(*operands)


class Joined:
    def __init__(self, first, rest):
        self.first, self.rest = first, rest

    def __getitem__(self, place):
        return self.first[...] if place == 0 else self.rest[place - 1]

    def __setitem__(self, place, value):
        if place == 0:
            self.first[...] = value
        else:
            self.rest[place - 1] = value


def jump_edge(even, result, near, far, live, edge, subs):
    loads, width = result[0].shape[0], near.shape[1]
    if edge == 0:
        right = jnp.where(even, far[:loads], near[:loads])
    else:
        right = result[edge - 1][:, width:]
    if edge == subs:
        left = jnp.where(even, near[:loads], far[:loads])
    else:
        left = result[edge][:, :width]
    return live[edge] * (right - left)


def outer_rows(operator, edge):
    rows = operator.shape[0] // 2
    high, low = split(edge)
    both = mul_rows(operator[...], high)
    return both[:rows] + both[rows:] + mul_rows(operator[:rows], low)


def send(even, to_next, to_prev, near_out, far_out):
    row = 0
    for ahead, behind in zip(to_next, to_prev):
        rows = slice(row, row + ahead.shape[0])
        near_out[rows, :] = jnp.where(even, ahead, behind)
        far_out[rows, :] = jnp.where(even, behind, ahead)
        row += ahead.shape[0]


def send_faces(even, first, last, near_out, far_out):
    width = first.shape[1] // 2
    send(even, [last[:, width:]], [first[:, :width]], near_out, far_out)


def panel_products(parts, panel, result, extra=None):
    subs = panel.shape[0]
    for sub in range(subs):
        high = jnp.concatenate([-parts[sub][0], parts[sub + 1][0]], axis=1)
        low = jnp.concatenate([-parts[sub][1], parts[sub + 1][1]], axis=1)
        total = mul(high, panel[sub]) + mul(low, panel[sub])
        if extra is not None:
            total = total + extra(sub)
        result[sub] = total


def column(row, width):
    lanes = jnp.broadcast_to(row, (128, row.shape[1])).T
    return jnp.concatenate([lanes] * (width // 128), axis=1)


def row_sums(values):
    half = values.shape[1] // 2
    return jnp.sum((values[:, :half] + values[:, half:]).T, axis=0, keepdims=True)


def step_scalars(step, sums, before):
    totals = jnp.sum(sums[...], axis=0)
    rz_now, curvature = totals[:1], totals[1:2]
    if step == 0:
        return rz_now, rz_now / curvature, None
    beta = rz_now / before[0:1]
    return rz_now, rz_now / (curvature - beta * rz_now / before[1:2]), beta


def even_place():
    return lax.rem(lax.axis_index("sub"), 2) == 0


def live_rows(counts, sub, rows, width):
    last = lax.axis_index("sub") == lax.axis_size("sub") - 1
    count = jnp.broadcast_to(counts[:, sub : sub + 1], (rows, width))
    if sub == counts.shape[1] - 1:
        count = jnp.where(last, 0, count)
    return (lax.broadcasted_iota(jnp.int32, (rows, width), 1) < count).astype(jnp.float32)


def tail_kernel(counts_ref, rhs, tail, counts, face, counts_done, face_done):
    loads, width = rhs.shape[2:]
    counts_copy = pltpu.make_async_copy(counts_ref, counts, counts_done)
    face_copy = pltpu.make_async_copy(rhs.at[0, rhs.shape[1] - 1], face, face_done)
    counts_copy.start()
    face_copy.start()
    counts_copy.wait()
    mask = live_rows(counts, counts.shape[1] - 1, 8, width)
    tail[loads:] = mask
    face_copy.wait()
    tail[:loads] = mask[:1] * face[...]


def early_kernel(counts, rhs, panel, live, own, partial, rest):
    subs, loads, width = own.shape
    parts = [None]
    for sub in range(subs):
        mask = live_rows(counts, sub, 1, width)
        live[sub] = mask
        own[sub] = mask * rhs[sub]
        parts.append(split(own[sub]))
    partial[...] = mul(parts[1][0], panel[0, width:]) + mul(parts[1][1], panel[0, width:])
    for sub in range(1, subs):
        high = jnp.concatenate([-parts[sub][0], parts[sub + 1][0]], axis=1)
        low = jnp.concatenate([-parts[sub][1], parts[sub + 1][1]], axis=1)
        rest[sub - 1] = mul(high, panel[sub]) + mul(low, panel[sub])


def head_kernel(head, partial, rest, panel, coupling, live, edge, first, near_out, far_out):
    loads, width = edge.shape
    live[...] = head[loads : loads + 1]
    edge[...] = head[:loads]
    high, low = split(head[:loads])
    first[...] = partial[...] - mul(high, panel[0, :width]) - mul(low, panel[0, :width])
    last = rest[rest.shape[0] - 1]
    to_next = [last[:, width:], coupling[coupling.shape[0] - 1, :, width:]]
    send(even_place(), to_next, [first[:, :width], coupling[0, :, :width]], near_out, far_out)


def setup_kernel(*refs):
    group = (len(refs) - 5) // 2
    maps, (coarse, coupling) = refs[:group], refs[group : group + 2]
    picked, (stacked, lift, everyone) = refs[group + 2 : -3], refs[-3:]
    subs, corners = maps[0].shape
    rows, size = coarse.shape
    own = subs * corners
    grp = lax.axis_index("grp")
    for sub in range(subs):
        high, low = split(coupling[sub])
        spare = jnp.zeros((lift.shape[1] - 3 * corners, high.shape[1]), jnp.bfloat16)
        stacked[sub] = jnp.concatenate([high, low], axis=0)
        lift[sub] = jnp.concatenate([high, high, low, spare], axis=0)
    for distance in range(group):
        unknowns = [maps[distance][sub : sub + 1, :] for sub in range(subs)]
        everyone[distance] = jnp.concatenate(unknowns, axis=1)
    high, low = split(coarse[...])
    unknowns = lax.broadcasted_iota(jnp.int32, (size, own), 0)
    columns = []
    for member in range(group):
        chosen = (unknowns == everyone[grp ^ member]).astype(jnp.bfloat16)
        columns.append(mul(high, chosen) + mul(low, chosen))
    high, low = split(jnp.concatenate(columns, axis=1))
    owned = lax.broadcasted_iota(jnp.int32, (rows, own), 0) + grp * rows
    dims = (((0,), (0,)), ((), ()))
    for distance in range(group):
        chosen = (owned == everyone[distance]).astype(jnp.bfloat16)
        picked[distance][...] = lax.dot_general(
            chosen, high, dims, preferred_element_type=jnp.float32
        ) + lax.dot_general(chosen, low, dims, preferred_element_type=jnp.float32)


def corner_kernel(first, rest, near, far, live_first, live_rest, coupling, _solve,
                  edge, own, corners):
    even = even_place()
    subs, rows = coupling.shape[0], coupling.shape[1] // 2
    result, live, edges = Joined(first, rest), Joined(live_first, live_rest), Joined(edge, own)
    parts = []
    for place in range(subs + 1):
        edges[place] = 0.25 * jump_edge(even, result, near, far, live, place, subs)
        parts.append(split(edges[place]))
    for sub in range(subs):
        high = jnp.concatenate([-parts[sub][0], parts[sub + 1][0]], axis=1)
        low = jnp.concatenate([-parts[sub][1], parts[sub + 1][1]], axis=1)
        both = mul_rows(coupling[sub], high)
        corners[sub * rows : (sub + 1) * rows, :] = (
            both[:rows] + both[rows:] + mul_rows(coupling[sub, :rows], low)
        )


def operators_kernel(coupling, live_edge, live_own, near, far, panel,
                     taken, ends, for_next, for_prev, given):
    even = even_place()
    subs, rows = coupling.shape[0], coupling.shape[1]
    width = coupling.shape[2] // 2
    live = Joined(live_edge, live_own)
    sides = received(even, near, far, near.shape[0] - rows, rows)
    before, after = sides[:rows], sides[rows:]
    left = [coupling[sub, :, :width] * (0.25 * live[sub]) for sub in range(subs)]
    left.append(after * (0.25 * live[subs]))
    right = [before * (0.25 * live[0])]
    right += [coupling[sub, :, width:] * (0.25 * live[sub + 1]) for sub in range(subs)]
    none = jnp.zeros((rows, width), jnp.float32)
    inner, ahead, behind = [], [], []
    for sub in range(subs):
        factors = jnp.concatenate(
            [
                jnp.concatenate([left[sub], right[sub + 1]], axis=1),
                jnp.concatenate([none, left[sub + 1]], axis=1),
                jnp.concatenate([right[sub], none], axis=1),
            ],
            axis=0,
        )
        both = mul(jnp.concatenate(split(factors), axis=0), panel[sub])
        product = both[: 3 * rows] + both[3 * rows :]
        inner.append(product[:rows])
        ahead.append(product[rows : 2 * rows])
        behind.append(product[2 * rows :])
    total = subs * rows
    for sub in range(subs):
        blocks = [none] * (subs + 1)
        blocks[sub] = -inner[sub][:, :width]
        blocks[sub + 1] = inner[sub][:, width:]
        if sub > 0:
            blocks[sub - 1] = ahead[sub - 1][:, :width]
            blocks[sub] = blocks[sub] - ahead[sub - 1][:, width:]
        if sub + 1 < subs:
            blocks[sub + 1] = blocks[sub + 1] + behind[sub + 1][:, :width]
            blocks[sub + 2] = -behind[sub + 1][:, width:]
        if sub == 0:
            ends[0] = blocks[0]
            blocks[0] = none
        if sub == subs - 1:
            ends[1] = blocks[subs]
            blocks[subs] = none
        high, low = split(jnp.concatenate(blocks, axis=1))
        taken[sub * rows : (sub + 1) * rows, :] = high
        taken[total + sub * rows : total + (sub + 1) * rows, :] = low
    for_next[...] = jnp.concatenate(split(ahead[subs - 1][:, :width]), axis=0)
    for_prev[...] = jnp.concatenate(split(-behind[0][:, width:]), axis=0)
    given[0] = -ahead[subs - 1][:, width:]
    given[1] = behind[0][:, :width]


def early_corner_kernel(taken, ends, outside, edge, own, corners):
    subs, rows = own.shape[0], ends.shape[1]
    total = subs * rows
    edges = Joined(edge, own)
    parts = [split(edges[place]) for place in range(subs + 1)]
    high = jnp.concatenate([part[0] for part in parts], axis=1)
    low = jnp.concatenate([part[1] for part in parts], axis=1)
    both = mul_rows(taken[...], high)
    values = both[:total] + both[total:] + mul_rows(taken[:total], low)
    corners[...] = values
    for end, place in ((0, 0), (1, subs)):
        operator = jnp.concatenate(split(ends[end]), axis=0)
        row = end * (total - rows)
        corners[row : row + rows, :] = (
            values[row : row + rows]
            + outer_rows(operator, edges[place])
            + outside[end * rows : (end + 1) * rows, :]
        )


def dual_products(edges, residual, panel, everyone, block, lift, result, sums):
    subs, width = panel.shape[0], panel.shape[1] // 2
    rows = block.shape[0] // 2
    high, low = split(everyone[...])
    both = mul(block[...], high)
    back = both[:rows] + both[rows:] + mul(block[:rows], low)
    corners = rows // subs

    def lifted(sub):
        own = back[sub * corners : (sub + 1) * corners]
        own_high = own.astype(jnp.bfloat16).astype(jnp.float32)
        terms = [own_high, own - own_high, own_high]
        spare = jnp.zeros((lift.shape[1] - 3 * corners, own.shape[1]), jnp.float32)
        return mul(jnp.concatenate(terms + [spare], axis=0).T.astype(jnp.bfloat16), lift[sub])

    parts = [split(edges[place]) for place in range(subs + 1)]
    panel_products(parts, panel, result, lifted)
    product = curvature = 0.0
    for sub in range(subs):
        product = product + residual[sub] * edges[sub + 1]
        curvature = curvature + (
            result[sub][:, width:] * edges[sub + 1] - result[sub][:, :width] * edges[sub]
        )
    sums[...] = jnp.concatenate([row_sums(product), row_sums(curvature)], axis=0)


def send_dual(result, live_own, subs, for_next, for_prev, near_out, far_out, residual=None,
              given=None):
    even = even_place()
    width = near_out.shape[1]
    to_next, to_prev = [result[subs - 1][:, width:]], [result[0][:, :width]]
    if given is not None:
        to_next += [given[0], outer_rows(for_next, residual[subs - 2])]
        to_prev += [given[1], outer_rows(for_prev, residual[0])]
    upper = live_own[subs - 2] * (result[subs - 2][:, width:] - result[subs - 1][:, :width])
    lower = live_own[0] * (result[0][:, width:] - result[1][:, :width])
    to_next.append(outer_rows(for_next, upper))
    to_prev.append(outer_rows(for_prev, lower))
    send(even, to_next, to_prev, near_out, far_out)


def first_dual_kernel(edge, own, residual, panel, everyone, block, lift, live_own,
                      for_next, for_prev, given, first, rest, near_out, far_out, sums):
    result = Joined(first, rest)
    dual_products(Joined(edge, own), residual, panel, everyone, block, lift, result, sums)
    send_dual(result, live_own, panel.shape[0], for_next, for_prev, near_out, far_out,
              residual, given)


def dual_kernel(last, *refs):
    first, rest, near, far, live_edge, live_own = refs[:6]
    residual, panel, everyone, block, lift = refs[6:11]
    even, subs = even_place(), panel.shape[0]
    before, live = Joined(first, rest), Joined(live_edge, live_own)
    edges = [
        0.25 * jump_edge(even, before, near, far, live, place, subs) for place in range(subs + 1)
    ]
    if last:
        own, first_new, rest_new, face, sums = refs[11:]
    else:
        for_next, for_prev, own, first_new, rest_new, near_out, far_out, sums = refs[11:]
    for sub in range(subs):
        own[sub] = edges[sub + 1]
    result = Joined(first_new, rest_new)
    dual_products(edges, residual, panel, everyone, block, lift, result, sums)
    if last:
        face[...] = result[0][:, : face.shape[1]]
    else:
        send_dual(result, live_own, subs, for_next, for_prev, near_out, far_out)


def received(even, near, far, start, rows):
    part = slice(start, start + rows)
    return jnp.concatenate(
        [jnp.where(even, far[part], near[part]), jnp.where(even, near[part], far[part])], axis=0
    )


def first_update_kernel(first, rest, near, far, live_first, live_rest, sums,
                        residual_edge, residual_own, panel, ends,
                        image_own, image_edge, new_edge, new_own, first_new, rest_new,
                        near_out, far_out, scalars, full_ends, outside_image, outside):
    even = even_place()
    loads, width = residual_edge.shape
    subs, rows = panel.shape[0], ends.shape[1]
    result, live = Joined(first, rest), Joined(live_first, live_rest)
    residual, image = Joined(residual_edge, residual_own), Joined(image_edge, image_own)
    residual_new, result_new = Joined(new_edge, new_own), Joined(first_new, rest_new)
    rz_now, alpha, _ = step_scalars(0, sums, None)
    scalars[...] = jnp.concatenate([rz_now, alpha], axis=0)
    operators = received(even, near, far, loads, rows)
    full_ends[0] = ends[0] + operators[:rows]
    full_ends[1] = ends[1] + operators[rows:]
    values = received(even, near, far, loads + 2 * rows, rows)
    outside_image[...] = values
    outside[...] = received(even, near, far, loads + rows, rows) - alpha * values
    alpha_column = column(alpha, width)
    parts = []
    for place in range(subs + 1):
        value = jump_edge(even, result, near, far, live, place, subs)
        image[place] = value
        residual_new[place] = residual[place] - alpha_column * value
        parts.append(split(residual_new[place]))
    panel_products(parts, panel, result_new)
    send_faces(even, result_new[0], result_new[subs - 1], near_out, far_out)


def update_kernel(first, rest, near, far, live_first, live_rest, sums, before,
                  old_edge, old_own, residual_edge, residual_own, panel,
                  outside_image_old, outside_old,
                  image_own, new_edge, new_own, first_new, rest_new,
                  near_out, far_out, scalars, outside):
    even = even_place()
    loads, width = residual_edge.shape
    subs, rows = panel.shape[0], outside.shape[0] // 2
    result, live = Joined(first, rest), Joined(live_first, live_rest)
    image_old, residual = Joined(old_edge, old_own), Joined(residual_edge, residual_own)
    residual_new, result_new = Joined(new_edge, new_own), Joined(first_new, rest_new)
    rz_now, alpha, beta = step_scalars(1, sums, before)
    scalars[...] = jnp.concatenate([rz_now, alpha], axis=0)
    values = received(even, near, far, loads, rows) + beta * outside_image_old[...]
    outside[...] = outside_old[...] - alpha * values
    alpha_column, beta_column = column(alpha, width), column(beta, width)
    parts = []
    for place in range(subs + 1):
        value = jump_edge(even, result, near, far, live, place, subs)
        value = value + beta_column * image_old[place]
        if place > 0:
            image_own[place - 1] = value
        residual_new[place] = residual[place] - alpha_column * value
        parts.append(split(residual_new[place]))
    panel_products(parts, panel, result_new)
    send_faces(even, result_new[0], result_new[subs - 1], near_out, far_out)


def last_kernel(first, rest, following, live, sums, before, older, image_old,
                residual, first_z, second_z, third_z, multipliers, residual_new):
    subs, width = residual.shape[0], following.shape[1]
    result = Joined(first, rest)
    rz_now, alpha, beta = step_scalars(2, sums, before)
    beta_before = before[0:1] / older[0:1]
    on_second = before[1:2] + alpha * beta
    on_first = older[1:2] + on_second * beta_before
    alpha_column, beta_column = column(alpha, width), column(beta, width)
    second_column, first_column = column(on_second, width), column(on_first, width)
    for sub in range(subs):
        left = following[...] if sub == subs - 1 else result[sub + 1][:, :width]
        image = live[sub] * (result[sub][:, width:] - left) + beta_column * image_old[sub]
        residual_new[sub] = residual[sub] - alpha_column * image
        multipliers[sub] = (
            first_column * first_z[sub]
            + second_column * second_z[sub]
            + alpha_column * third_z[sub]
        )


def neighbour_pairs(size, first):
    pairs = [(i, i + 1) for i in range(first, size - 1, 2)]
    return [route for a, b in pairs for route in ((a, b), (b, a))]


def swap(near, far):
    size = lax.axis_size("sub")
    return (
        lax.ppermute(near, "sub", neighbour_pairs(size, 0)),
        lax.ppermute(far, "sub", neighbour_pairs(size, 1)),
    )


def from_all(rows):
    size = lax.axis_size("sub") * lax.axis_size("grp")
    copies = jnp.broadcast_to(rows[None], (size,) + rows.shape)
    return lax.all_to_all(copies, ("sub", "grp"), 0, 0)


def from_group(values):
    group = lax.axis_size("grp")
    received = [values]
    for distance in range(1, group):
        routes = [(i, i ^ distance) for i in range(group)]
        received.append(lax.ppermute(values, "grp", routes))
    return received


def swap_blocks(picked):
    group = lax.axis_size("grp")
    received = [picked[0]]
    for distance in range(1, group):
        routes = [(i, i ^ distance) for i in range(group)]
        received.append(lax.ppermute(picked[distance], "grp", routes))
    return received


def make_tail(counts, rhs):
    loads, width = rhs.shape[2:]
    return pl.pallas_call(
        tail_kernel,
        out_shape=jax.ShapeDtypeStruct((loads + 8, width), jnp.float32),
        in_specs=[
            pl.BlockSpec(memory_space=pltpu.HBM),
            pl.BlockSpec(memory_space=pltpu.HBM),
        ],
        out_specs=pl.BlockSpec(memory_space=pltpu.VMEM),
        scratch_shapes=[
            pltpu.VMEM(counts.shape, counts.dtype),
            pltpu.VMEM((loads, width), jnp.float32),
            pltpu.SemaphoreType.DMA,
            pltpu.SemaphoreType.DMA,
        ],
        compiler_params=pltpu.CompilerParams(vmem_limit_bytes=TAIL_LIMIT),
    )(counts, rhs)


def local(rhs, counts, solve_panel, dirichlet_panel, coupling, corner_map, coarse_inverse):
    subs, loads, width = rhs.shape[1:]
    corners = coupling.shape[2]
    solve, dirichlet = solve_panel[0], dirichlet_panel[0]
    size = lax.axis_size("sub")

    face_shape, own_shape = (loads, width), (subs, loads, width)
    first_shape, rest_shape = (loads, 2 * width), (subs - 1, loads, 2 * width)
    scalars_shape, outside_shape, side_shape = (2, loads), (2 * corners, loads), (corners, width)
    long_shape, longer_shape = (loads + corners, width), (loads + 3 * corners, width)
    edges_shapes = [face_shape, own_shape]
    result_shapes = [first_shape, rest_shape, face_shape, face_shape]

    tail = make_tail(counts, rhs)
    tail, counts, corner_map = lax.optimization_barrier((tail, counts, corner_map))
    head = lax.ppermute(tail, "sub", [(i, i + 1) for i in range(size - 1)])
    maps = from_group(corner_map[0])
    live_own, residual_own, partial, rest = call(
        early_kernel,
        [(subs, 1, width), own_shape, first_shape, rest_shape],
        counts, rhs[0], dirichlet,
    )
    group, own = len(maps), subs * corners
    pair = [(corners, width)] * 2
    *picked, stacked, lift = call(
        setup_kernel,
        [(own, group * own)] * group
        + [(subs, 2 * corners, 2 * width), (subs, 3 * corners + -3 * corners % 128, 2 * width)],
        *maps, coarse_inverse[0], coupling[0],
        kinds=[jnp.float32] * group + [jnp.bfloat16] * 2,
        scratch=[pltpu.VMEM((group, 1, own), jnp.int32)],
    )
    head, stacked = lax.optimization_barrier((head, stacked))
    live_edge, residual_edge, first, near, far = call(
        head_kernel,
        [(1, width), face_shape, first_shape, long_shape, long_shape],
        head, partial, rest, dirichlet, coupling[0],
    )
    near, far = swap(near, far)
    blocks = swap_blocks(picked)
    live, residual = (live_edge, live_own), (residual_edge, residual_own)
    taken, ends, for_next, for_prev, given = call(
        operators_kernel,
        [(2 * own, (subs + 1) * width), (2,) + side_shape, (2 * corners, width),
         (2 * corners, width), (2,) + side_shape],
        coupling[0], *live, near, far, dirichlet,
        kinds=[jnp.bfloat16, jnp.float32, jnp.bfloat16, jnp.bfloat16, jnp.float32],
    )

    edge, first_z, values = call(
        corner_kernel,
        edges_shapes + [(own, loads)],
        first, rest, near, far, *live, stacked, solve,
    )
    everyone = lax.all_gather(values, "grp", tiled=True)
    everyone, blocks = lax.optimization_barrier((everyone, blocks))
    block = jnp.concatenate(split_outside(sum(blocks[1:], blocks[0])), axis=0)
    first, rest, near, far, sums = call(
        first_dual_kernel,
        [first_shape, rest_shape, longer_shape, longer_shape, scalars_shape],
        edge, first_z, residual[1], solve, everyone, block, lift, live[1],
        for_next, for_prev, given,
    )
    sums = from_all(sums)
    near, far = swap(near, far)
    (image_own, image_edge, *residual, first, rest, near, far, scalars_first, ends, outside_image,
     outside) = call(
        first_update_kernel,
        [own_shape, face_shape] + edges_shapes + result_shapes
        + [scalars_shape, (2,) + side_shape, outside_shape, outside_shape],
        first, rest, near, far, *live, sums, *residual, dirichlet, ends,
    )

    near, far = swap(near, far)
    (values,) = call(early_corner_kernel, [(own, loads)], taken, ends, outside, *residual)
    everyone = lax.all_gather(values, "grp", tiled=True)
    second_z, first, rest, near, far, sums = call(
        functools.partial(dual_kernel, False),
        [own_shape, first_shape, rest_shape, long_shape, long_shape, scalars_shape],
        first, rest, near, far, *live, residual[1], solve, everyone, block, lift,
        for_next, for_prev,
    )
    sums = from_all(sums)
    near, far = swap(near, far)
    image_own, *residual, first, rest, near, far, scalars_second, outside = call(
        update_kernel,
        [own_shape] + edges_shapes + result_shapes + [scalars_shape, outside_shape],
        first, rest, near, far, *live, sums, scalars_first, image_edge, image_own, *residual,
        dirichlet, outside_image, outside,
    )

    near, far = swap(near, far)
    (values,) = call(early_corner_kernel, [(own, loads)], taken, ends, outside, *residual)
    everyone = lax.all_gather(values, "grp", tiled=True)
    third_z, first, rest, face, sums = call(
        functools.partial(dual_kernel, True),
        [own_shape, first_shape, rest_shape, face_shape, scalars_shape],
        first, rest, near, far, *live, residual[1], solve, everyone, block, lift,
    )
    sums = from_all(sums)
    following = lax.ppermute(face, "sub", [(i + 1, i) for i in range(size - 1)])
    multipliers, residual = call(
        last_kernel,
        [own_shape] * 2,
        first, rest, following, live[1], sums, scalars_second, scalars_first,
        image_own, residual[1], first_z, second_z, third_z,
    )
    return (multipliers[None], residual[None])


def solution(mesh):
    return jax.shard_map(
        local,
        mesh=mesh,
        in_specs=(
            P("grp", "sub", None, None),
            P("grp", "sub"),
            P("grp", "sub", None, None),
            P("grp", "sub", None, None),
            P("grp", "sub", None, None),
            P("grp", "sub", None),
            P("sub", "grp", None),
        ),
        out_specs=(P("grp", "sub", None, None), P("grp", "sub", None, None)),
        check_vma=False,
    )
```

```python
import functools

import jax
import jax.numpy as jnp
from jax import lax
from jax.experimental import pallas as pl
from jax.experimental.pallas import tpu as pltpu
from jax.sharding import PartitionSpec as P

VMEM_LIMIT = 8 * 1024 * 1024
TAIL_LIMIT = 62 * 1024 * 1024


def split(values):
    high = values.astype(jnp.bfloat16)
    return high, (values - high.astype(jnp.float32)).astype(jnp.bfloat16)


def split_outside(values):
    high = lax.reduce_precision(values, exponent_bits=8, mantissa_bits=7)
    return high.astype(jnp.bfloat16), (values - high).astype(jnp.bfloat16)


def mul(first, second):
    return jnp.dot(first, second, preferred_element_type=jnp.float32)


def mul_rows(first, second):
    dims = (((1,), (1,)), ((), ()))
    return lax.dot_general(first, second, dims, preferred_element_type=jnp.float32)


def call(kernel, out_shapes, *operands, kinds=None, scratch=()):
    kinds = kinds or [jnp.float32] * len(out_shapes)
    return pl.pallas_call(
        kernel,
        out_shape=[jax.ShapeDtypeStruct(*shape) for shape in zip(out_shapes, kinds)],
        in_specs=[pl.BlockSpec(memory_space=pltpu.VMEM)] * len(operands),
        out_specs=[pl.BlockSpec(memory_space=pltpu.VMEM)] * len(out_shapes),
        scratch_shapes=list(scratch),
        compiler_params=pltpu.CompilerParams(vmem_limit_bytes=VMEM_LIMIT),
    )(*operands)


class Joined:
    def __init__(self, first, rest):
        self.first, self.rest = first, rest

    def __getitem__(self, place):
        return self.first[...] if place == 0 else self.rest[place - 1]

    def __setitem__(self, place, value):
        if place == 0:
            self.first[...] = value
        else:
            self.rest[place - 1] = value


def jump_edge(even, result, near, far, live, edge, subs):
    loads, width = result[0].shape[0], near.shape[1]
    if edge == 0:
        right = jnp.where(even, far[:loads], near[:loads])
    else:
        right = result[edge - 1][:, width:]
    if edge == subs:
        left = jnp.where(even, near[:loads], far[:loads])
    else:
        left = result[edge][:, :width]
    return live[edge] * (right - left)


def outer_rows(operator, edge):
    rows = operator.shape[0] // 2
    high, low = split(edge)
    both = mul_rows(operator[...], high)
    return both[:rows] + both[rows:] + mul_rows(operator[:rows], low)


def send(even, to_next, to_prev, near_out, far_out):
    row = 0
    for ahead, behind in zip(to_next, to_prev):
        rows = slice(row, row + ahead.shape[0])
        near_out[rows, :] = jnp.where(even, ahead, behind)
        far_out[rows, :] = jnp.where(even, behind, ahead)
        row += ahead.shape[0]


def send_faces(even, first, last, near_out, far_out):
    width = first.shape[1] // 2
    send(even, [last[:, width:]], [first[:, :width]], near_out, far_out)


def panel_products(parts, panel, result, extra=None):
    subs = panel.shape[0]
    for sub in range(subs):
        high = jnp.concatenate([-parts[sub][0], parts[sub + 1][0]], axis=1)
        low = jnp.concatenate([-parts[sub][1], parts[sub + 1][1]], axis=1)
        total = mul(high, panel[sub]) + mul(low, panel[sub])
        if extra is not None:
            total = total + extra(sub)
        result[sub] = total


def column(row, width):
    lanes = jnp.broadcast_to(row, (128, row.shape[1])).T
    return jnp.concatenate([lanes] * (width // 128), axis=1)


def row_sums(values):
    half = values.shape[1] // 2
    return jnp.sum((values[:, :half] + values[:, half:]).T, axis=0, keepdims=True)


def step_scalars(step, sums, before):
    totals = jnp.sum(sums[...], axis=0)
    rz_now, curvature = totals[:1], totals[1:2]
    if step == 0:
        return rz_now, rz_now / curvature, None
    beta = rz_now / before[0:1]
    return rz_now, rz_now / (curvature - beta * rz_now / before[1:2]), beta


def even_place():
    return lax.rem(lax.axis_index("sub"), 2) == 0


def live_rows(counts, sub, rows, width):
    last = lax.axis_index("sub") == lax.axis_size("sub") - 1
    count = jnp.broadcast_to(counts[:, sub : sub + 1], (rows, width))
    if sub == counts.shape[1] - 1:
        count = jnp.where(last, 0, count)
    return (lax.broadcasted_iota(jnp.int32, (rows, width), 1) < count).astype(jnp.float32)


def tail_kernel(counts_ref, rhs, tail, counts, face, counts_done, face_done):
    loads, width = rhs.shape[2:]
    counts_copy = pltpu.make_async_copy(counts_ref, counts, counts_done)
    face_copy = pltpu.make_async_copy(rhs.at[0, rhs.shape[1] - 1], face, face_done)
    counts_copy.start()
    face_copy.start()
    counts_copy.wait()
    mask = live_rows(counts, counts.shape[1] - 1, 8, width)
    tail[loads:] = mask
    face_copy.wait()
    tail[:loads] = mask[:1] * face[...]


def early_kernel(counts, rhs, panel, live, own, partial, rest):
    subs, loads, width = own.shape
    parts = [None]
    for sub in range(subs):
        mask = live_rows(counts, sub, 1, width)
        live[sub] = mask
        own[sub] = mask * rhs[sub]
        parts.append(split(own[sub]))
    partial[...] = mul(parts[1][0], panel[0, width:]) + mul(parts[1][1], panel[0, width:])
    for sub in range(1, subs):
        high = jnp.concatenate([-parts[sub][0], parts[sub + 1][0]], axis=1)
        low = jnp.concatenate([-parts[sub][1], parts[sub + 1][1]], axis=1)
        rest[sub - 1] = mul(high, panel[sub]) + mul(low, panel[sub])


def head_kernel(head, partial, rest, panel, coupling, live, edge, first, near_out, far_out):
    loads, width = edge.shape
    live[...] = head[loads : loads + 1]
    edge[...] = head[:loads]
    high, low = split(head[:loads])
    first[...] = partial[...] - mul(high, panel[0, :width]) - mul(low, panel[0, :width])
    last = rest[rest.shape[0] - 1]
    to_next = [last[:, width:], coupling[coupling.shape[0] - 1, :, width:]]
    send(even_place(), to_next, [first[:, :width], coupling[0, :, :width]], near_out, far_out)


def setup_kernel(*refs):
    group = (len(refs) - 5) // 2
    maps, (coarse, coupling) = refs[:group], refs[group : group + 2]
    picked, (stacked, lift, everyone) = refs[group + 2 : -3], refs[-3:]
    subs, corners = maps[0].shape
    rows, size = coarse.shape
    own = subs * corners
    grp = lax.axis_index("grp")
    for sub in range(subs):
        high, low = split(coupling[sub])
        spare = jnp.zeros((lift.shape[1] - 3 * corners, high.shape[1]), jnp.bfloat16)
        stacked[sub] = jnp.concatenate([high, low], axis=0)
        lift[sub] = jnp.concatenate([high, high, low, spare], axis=0)
    for distance in range(group):
        unknowns = [maps[distance][sub : sub + 1, :] for sub in range(subs)]
        everyone[distance] = jnp.concatenate(unknowns, axis=1)
    high, low = split(coarse[...])
    unknowns = lax.broadcasted_iota(jnp.int32, (size, own), 0)
    columns = []
    for member in range(group):
        chosen = (unknowns == everyone[grp ^ member]).astype(jnp.bfloat16)
        columns.append(mul(high, chosen) + mul(low, chosen))
    high, low = split(jnp.concatenate(columns, axis=1))
    owned = lax.broadcasted_iota(jnp.int32, (rows, own), 0) + grp * rows
    dims = (((0,), (0,)), ((), ()))
    for distance in range(group):
        chosen = (owned == everyone[distance]).astype(jnp.bfloat16)
        picked[distance][...] = lax.dot_general(
            chosen, high, dims, preferred_element_type=jnp.float32
        ) + lax.dot_general(chosen, low, dims, preferred_element_type=jnp.float32)


def corner_kernel(first, rest, near, far, live_first, live_rest, coupling, _solve,
                  edge, own, corners):
    even = even_place()
    subs, rows = coupling.shape[0], coupling.shape[1] // 2
    result, live, edges = Joined(first, rest), Joined(live_first, live_rest), Joined(edge, own)
    parts = []
    for place in range(subs + 1):
        edges[place] = 0.25 * jump_edge(even, result, near, far, live, place, subs)
        parts.append(split(edges[place]))
    for sub in range(subs):
        high = jnp.concatenate([-parts[sub][0], parts[sub + 1][0]], axis=1)
        low = jnp.concatenate([-parts[sub][1], parts[sub + 1][1]], axis=1)
        both = mul_rows(coupling[sub], high)
        corners[sub * rows : (sub + 1) * rows, :] = (
            both[:rows] + both[rows:] + mul_rows(coupling[sub, :rows], low)
        )


def operators_kernel(coupling, live_edge, live_own, near, far, panel,
                     taken, ends, for_next, for_prev, given):
    even = even_place()
    subs, rows = coupling.shape[0], coupling.shape[1]
    width = coupling.shape[2] // 2
    live = Joined(live_edge, live_own)
    sides = received(even, near, far, near.shape[0] - rows, rows)
    before, after = sides[:rows], sides[rows:]
    left = [coupling[sub, :, :width] * (0.25 * live[sub]) for sub in range(subs)]
    left.append(after * (0.25 * live[subs]))
    right = [before * (0.25 * live[0])]
    right += [coupling[sub, :, width:] * (0.25 * live[sub + 1]) for sub in range(subs)]
    none = jnp.zeros((rows, width), jnp.float32)
    inner, ahead, behind = [], [], []
    for sub in range(subs):
        factors = jnp.concatenate(
            [
                jnp.concatenate([left[sub], right[sub + 1]], axis=1),
                jnp.concatenate([none, left[sub + 1]], axis=1),
                jnp.concatenate([right[sub], none], axis=1),
            ],
            axis=0,
        )
        both = mul(jnp.concatenate(split(factors), axis=0), panel[sub])
        product = both[: 3 * rows] + both[3 * rows :]
        inner.append(product[:rows])
        ahead.append(product[rows : 2 * rows])
        behind.append(product[2 * rows :])
    total = subs * rows
    for sub in range(subs):
        blocks = [none] * (subs + 1)
        blocks[sub] = -inner[sub][:, :width]
        blocks[sub + 1] = inner[sub][:, width:]
        if sub > 0:
            blocks[sub - 1] = ahead[sub - 1][:, :width]
            blocks[sub] = blocks[sub] - ahead[sub - 1][:, width:]
        if sub + 1 < subs:
            blocks[sub + 1] = blocks[sub + 1] + behind[sub + 1][:, :width]
            blocks[sub + 2] = -behind[sub + 1][:, width:]
        if sub == 0:
            ends[0] = blocks[0]
            blocks[0] = none
        if sub == subs - 1:
            ends[1] = blocks[subs]
            blocks[subs] = none
        high, low = split(jnp.concatenate(blocks, axis=1))
        taken[sub * rows : (sub + 1) * rows, :] = high
        taken[total + sub * rows : total + (sub + 1) * rows, :] = low
    for_next[...] = jnp.concatenate(split(ahead[subs - 1][:, :width]), axis=0)
    for_prev[...] = jnp.concatenate(split(-behind[0][:, width:]), axis=0)
    given[0] = -ahead[subs - 1][:, width:]
    given[1] = behind[0][:, :width]


def early_corner_kernel(taken, ends, outside, edge, own, corners):
    subs, rows = own.shape[0], ends.shape[1]
    total = subs * rows
    edges = Joined(edge, own)
    parts = [split(edges[place]) for place in range(subs + 1)]
    high = jnp.concatenate([part[0] for part in parts], axis=1)
    low = jnp.concatenate([part[1] for part in parts], axis=1)
    both = mul_rows(taken[...], high)
    values = both[:total] + both[total:] + mul_rows(taken[:total], low)
    corners[...] = values
    for end, place in ((0, 0), (1, subs)):
        operator = jnp.concatenate(split(ends[end]), axis=0)
        row = end * (total - rows)
        corners[row : row + rows, :] = (
            values[row : row + rows]
            + outer_rows(operator, edges[place])
            + outside[end * rows : (end + 1) * rows, :]
        )


def coarse_lift(everyone, block, lift):
    subs = lift.shape[0]
    rows = block.shape[0] // 2
    high, low = split(everyone[...])
    both = mul(block[...], high)
    back = both[:rows] + both[rows:] + mul(block[:rows], low)
    corners = rows // subs

    def lifted(sub):
        own = back[sub * corners : (sub + 1) * corners]
        own_high = own.astype(jnp.bfloat16).astype(jnp.float32)
        terms = [own_high, own - own_high, own_high]
        spare = jnp.zeros((lift.shape[1] - 3 * corners, own.shape[1]), jnp.float32)
        return mul(jnp.concatenate(terms + [spare], axis=0).T.astype(jnp.bfloat16), lift[sub])

    return lifted


def on_subdomain(values, left, right):
    width = left.shape[1]
    return values[:, width:] * right - values[:, :width] * left


def send_dual(even, inner, faces, for_next, for_prev, near_out, far_out, residual=None,
              given=None):
    to_next, to_prev = [faces[0]], [faces[1]]
    count = inner.shape[0]
    if given is not None:
        to_next += [given[0], outer_rows(for_next, residual[count - 1])]
        to_prev += [given[1], outer_rows(for_prev, residual[0])]
    to_next.append(outer_rows(for_next, inner[count - 1]))
    to_prev.append(outer_rows(for_prev, inner[0]))
    send(even, to_next, to_prev, near_out, far_out)


def inner_jump(result, live_own, inner):
    width = inner.shape[2]
    for place in range(inner.shape[0]):
        inner[place] = live_own[place] * (result[place][:, width:] - result[place + 1][:, :width])


def first_dual_kernel(edge, own, residual, panel, everyone, block, lift, live_own,
                      for_next, for_prev, given, inner, near_out, far_out, sums, result):
    subs, width = panel.shape[0], edge.shape[1]
    edges = Joined(edge, own)
    parts = [split(edges[place]) for place in range(subs + 1)]
    panel_products(parts, panel, result, coarse_lift(everyone, block, lift))
    inner_jump(result, live_own, inner)
    faces = [result[subs - 1][:, width:], result[0][:, :width]]
    send_dual(even_place(), inner, faces, for_next, for_prev, near_out, far_out, residual, given)
    product = curvature = 0.0
    for sub in range(subs):
        product = product + residual[sub] * edges[sub + 1]
        curvature = curvature + on_subdomain(result[sub], edges[sub], edges[sub + 1])
    sums[...] = jnp.concatenate([row_sums(product), row_sums(curvature)], axis=0)


def inner_edges_kernel(edge, own, panel, live_own, inner):
    subs, width = panel.shape[0], edge.shape[1]
    edges = Joined(edge, own)
    parts = [split(edges[place]) for place in range(subs + 1)]

    def half(sub, columns):
        high = jnp.concatenate([-parts[sub][0], parts[sub + 1][0]], axis=1)
        low = jnp.concatenate([-parts[sub][1], parts[sub + 1][1]], axis=1)
        return mul(high, panel[sub, :, columns]) + mul(low, panel[sub, :, columns])

    for place in range(subs - 1):
        right = half(place, slice(width, 2 * width))
        left = half(place + 1, slice(0, width))
        inner[place] = (0.25 * live_own[place]) * (right - left)


def inner_dual_kernel(inner, residual, panel, everyone, block, lift, result, partial):
    subs, width = panel.shape[0], inner.shape[2]
    lifted = coarse_lift(everyone, block, lift)
    parts = [split(inner[place]) for place in range(subs - 1)]
    high, low = parts[0]
    result[0] = mul(high, panel[0, width:]) + mul(low, panel[0, width:]) + lifted(0)
    product = residual[0] * inner[0]
    curvature = jnp.zeros_like(product)
    for sub in range(1, subs - 1):
        high = jnp.concatenate([-parts[sub - 1][0], parts[sub][0]], axis=1)
        low = jnp.concatenate([-parts[sub - 1][1], parts[sub][1]], axis=1)
        result[sub] = mul(high, panel[sub]) + mul(low, panel[sub]) + lifted(sub)
        product = product + residual[sub] * inner[sub]
        curvature = curvature + on_subdomain(result[sub], inner[sub - 1], inner[sub])
    high, low = parts[subs - 2]
    result[subs - 1] = lifted(subs - 1) - (
        mul(high, panel[subs - 1, :width]) + mul(low, panel[subs - 1, :width])
    )
    partial[0] = product
    partial[1] = curvature


def cut_edges(even, loads, near, far, near_sent, far_sent, live_first, live_last):
    near, far, near_sent, far_sent = near[:loads], far[:loads], near_sent[:loads], far_sent[:loads]
    first = live_first * jnp.where(even, far - far_sent, near - near_sent)
    last = live_last * jnp.where(even, near_sent - near, far_sent - far)
    return first, last


def outer_dual_kernel(closing, *refs):
    before, inner_z, partial, near, far, near_sent, far_sent, live_edge, live_own = refs[:9]
    residual, panel = refs[9:11]
    even, subs, width = even_place(), panel.shape[0], near_sent.shape[1]
    edge, last = cut_edges(even, residual.shape[1], near, far, near_sent, far_sent,
                           0.25 * live_edge[...], 0.25 * live_own[subs - 1])
    if closing:
        last_z, inner, to_next, to_prev, sums = refs[11:]
    else:
        for_next, for_prev, last_z, inner, near_out, far_out, sums = refs[11:]
    last_z[...] = last
    high, low = split(edge)
    result_first = before[0] - (mul(high, panel[0, :width]) + mul(low, panel[0, :width]))
    high, low = split(last)
    result_last = before[subs - 1] + (
        mul(high, panel[subs - 1, width:]) + mul(low, panel[subs - 1, width:])
    )
    result = [result_first] + [before[sub] for sub in range(1, subs - 1)] + [result_last]
    inner_jump(result, live_own, inner)
    faces = [result_last[:, width:], result_first[:, :width]]
    if closing:
        to_next[...], to_prev[...] = faces
    else:
        send_dual(even, inner, faces, for_next, for_prev, near_out, far_out)
    product = partial[0] + residual[subs - 1] * last
    curvature = partial[1] + on_subdomain(result_first, edge, inner_z[0])
    curvature = curvature + on_subdomain(result_last, inner_z[subs - 2], last)
    sums[...] = jnp.concatenate([row_sums(product), row_sums(curvature)], axis=0)


def received(even, near, far, start, rows):
    part = slice(start, start + rows)
    return jnp.concatenate(
        [jnp.where(even, far[part], near[part]), jnp.where(even, near[part], far[part])], axis=0
    )


def send_outer(parts, panel, near_out, far_out):
    subs, width = panel.shape[0], near_out.shape[1]

    def half(sub, columns):
        high = jnp.concatenate([-parts[sub][0], parts[sub + 1][0]], axis=1)
        low = jnp.concatenate([-parts[sub][1], parts[sub + 1][1]], axis=1)
        return mul(high, panel[sub, :, columns]) + mul(low, panel[sub, :, columns])

    to_next = half(subs - 1, slice(width, 2 * width))
    send(even_place(), [to_next], [half(0, slice(0, width))], near_out, far_out)


def image_edges(even, inner, near, far, near_sent, far_sent, live_edge, live_own):
    subs = live_own.shape[0]
    edge, last = cut_edges(even, inner.shape[1], near, far, near_sent, far_sent, live_edge[...],
                           live_own[subs - 1])
    return [edge] + [inner[place] for place in range(subs - 1)] + [last]


def first_update_kernel(inner, near, far, near_sent, far_sent, live_edge, live_own, sums,
                        residual_edge, residual_own, panel, ends,
                        image_own, image_edge, new_edge, new_own,
                        near_out, far_out, scalars, full_ends, outside_image, outside):
    even = even_place()
    loads, width = residual_edge.shape
    subs, rows = panel.shape[0], ends.shape[1]
    residual, image = Joined(residual_edge, residual_own), Joined(image_edge, image_own)
    residual_new = Joined(new_edge, new_own)
    rz_now, alpha, _ = step_scalars(0, sums, None)
    scalars[...] = jnp.concatenate([rz_now, alpha], axis=0)
    operators = received(even, near, far, loads, rows)
    full_ends[0] = ends[0] + operators[:rows]
    full_ends[1] = ends[1] + operators[rows:]
    values = received(even, near, far, loads + 2 * rows, rows)
    outside_image[...] = values
    outside[...] = received(even, near, far, loads + rows, rows) - alpha * values
    alpha_column = column(alpha, width)
    parts = []
    edges = image_edges(even, inner, near, far, near_sent, far_sent, live_edge, live_own)
    for place, value in enumerate(edges):
        image[place] = value
        residual_new[place] = residual[place] - alpha_column * value
        parts.append(split(residual_new[place]))
    send_outer(parts, panel, near_out, far_out)


def update_kernel(inner, near, far, near_sent, far_sent, live_edge, live_own, sums, before,
                  old_edge, old_own, residual_edge, residual_own, panel,
                  outside_image_old, outside_old,
                  image_own, new_edge, new_own, near_out, far_out, scalars, outside):
    even = even_place()
    loads, width = residual_edge.shape
    rows = outside.shape[0] // 2
    image_old, residual = Joined(old_edge, old_own), Joined(residual_edge, residual_own)
    residual_new = Joined(new_edge, new_own)
    rz_now, alpha, beta = step_scalars(1, sums, before)
    scalars[...] = jnp.concatenate([rz_now, alpha], axis=0)
    values = received(even, near, far, loads, rows) + beta * outside_image_old[...]
    outside[...] = outside_old[...] - alpha * values
    alpha_column, beta_column = column(alpha, width), column(beta, width)
    parts = []
    edges = image_edges(even, inner, near, far, near_sent, far_sent, live_edge, live_own)
    for place, value in enumerate(edges):
        value = value + beta_column * image_old[place]
        if place > 0:
            image_own[place - 1] = value
        residual_new[place] = residual[place] - alpha_column * value
        parts.append(split(residual_new[place]))
    send_outer(parts, panel, near_out, far_out)


def last_kernel(inner, to_next, following, live, sums, before, older, image_old,
                residual, first_z, second_inner, second_last, third_inner, third_last,
                multipliers, residual_new):
    subs, width = residual.shape[0], following.shape[1]
    rz_now, alpha, beta = step_scalars(2, sums, before)
    beta_before = before[0:1] / older[0:1]
    on_second = before[1:2] + alpha * beta
    on_first = older[1:2] + on_second * beta_before
    alpha_column, beta_column = column(alpha, width), column(beta, width)
    second_column, first_column = column(on_second, width), column(on_first, width)
    for sub in range(subs):
        if sub == subs - 1:
            image = live[sub] * (to_next[...] - following[...])
            second_z, third_z = second_last[...], third_last[...]
        else:
            image, second_z, third_z = inner[sub], second_inner[sub], third_inner[sub]
        image = image + beta_column * image_old[sub]
        residual_new[sub] = residual[sub] - alpha_column * image
        multipliers[sub] = (
            first_column * first_z[sub] + second_column * second_z + alpha_column * third_z
        )


def neighbour_pairs(size, first):
    pairs = [(i, i + 1) for i in range(first, size - 1, 2)]
    return [route for a, b in pairs for route in ((a, b), (b, a))]


def swap(near, far):
    size = lax.axis_size("sub")
    return (
        lax.ppermute(near, "sub", neighbour_pairs(size, 0)),
        lax.ppermute(far, "sub", neighbour_pairs(size, 1)),
    )


def from_all(rows):
    size = lax.axis_size("sub") * lax.axis_size("grp")
    copies = jnp.broadcast_to(rows[None], (size,) + rows.shape)
    return lax.all_to_all(copies, ("sub", "grp"), 0, 0)


def from_group(values):
    group = lax.axis_size("grp")
    received = [values]
    for distance in range(1, group):
        routes = [(i, i ^ distance) for i in range(group)]
        received.append(lax.ppermute(values, "grp", routes))
    return received


def swap_blocks(picked):
    group = lax.axis_size("grp")
    received = [picked[0]]
    for distance in range(1, group):
        routes = [(i, i ^ distance) for i in range(group)]
        received.append(lax.ppermute(picked[distance], "grp", routes))
    return received


def make_tail(counts, rhs):
    loads, width = rhs.shape[2:]
    return pl.pallas_call(
        tail_kernel,
        out_shape=jax.ShapeDtypeStruct((loads + 8, width), jnp.float32),
        in_specs=[
            pl.BlockSpec(memory_space=pltpu.HBM),
            pl.BlockSpec(memory_space=pltpu.HBM),
        ],
        out_specs=pl.BlockSpec(memory_space=pltpu.VMEM),
        scratch_shapes=[
            pltpu.VMEM(counts.shape, counts.dtype),
            pltpu.VMEM((loads, width), jnp.float32),
            pltpu.SemaphoreType.DMA,
            pltpu.SemaphoreType.DMA,
        ],
        compiler_params=pltpu.CompilerParams(vmem_limit_bytes=TAIL_LIMIT),
    )(counts, rhs)


def local(rhs, counts, solve_panel, dirichlet_panel, coupling, corner_map, coarse_inverse):
    subs, loads, width = rhs.shape[1:]
    corners = coupling.shape[2]
    solve, dirichlet = solve_panel[0], dirichlet_panel[0]
    size = lax.axis_size("sub")

    face_shape, own_shape = (loads, width), (subs, loads, width)
    first_shape, rest_shape = (loads, 2 * width), (subs - 1, loads, 2 * width)
    scalars_shape, outside_shape, side_shape = (2, loads), (2 * corners, loads), (corners, width)
    long_shape, longer_shape = (loads + corners, width), (loads + 3 * corners, width)
    edges_shapes = [face_shape, own_shape]
    result_shapes = [first_shape, rest_shape, face_shape, face_shape]

    tail = make_tail(counts, rhs)
    tail, counts, corner_map = lax.optimization_barrier((tail, counts, corner_map))
    head = lax.ppermute(tail, "sub", [(i, i + 1) for i in range(size - 1)])
    maps = from_group(corner_map[0])
    live_own, residual_own, partial, rest = call(
        early_kernel,
        [(subs, 1, width), own_shape, first_shape, rest_shape],
        counts, rhs[0], dirichlet,
    )
    group, own = len(maps), subs * corners
    pair = [(corners, width)] * 2
    *picked, stacked, lift = call(
        setup_kernel,
        [(own, group * own)] * group
        + [(subs, 2 * corners, 2 * width), (subs, 3 * corners + -3 * corners % 128, 2 * width)],
        *maps, coarse_inverse[0], coupling[0],
        kinds=[jnp.float32] * group + [jnp.bfloat16] * 2,
        scratch=[pltpu.VMEM((group, 1, own), jnp.int32)],
    )
    head, stacked = lax.optimization_barrier((head, stacked))
    live_edge, residual_edge, first, near, far = call(
        head_kernel,
        [(1, width), face_shape, first_shape, long_shape, long_shape],
        head, partial, rest, dirichlet, coupling[0],
    )
    near, far = swap(near, far)
    blocks = swap_blocks(picked)
    live, residual = (live_edge, live_own), (residual_edge, residual_own)
    taken, ends, for_next, for_prev, given = call(
        operators_kernel,
        [(2 * own, (subs + 1) * width), (2,) + side_shape, (2 * corners, width),
         (2 * corners, width), (2,) + side_shape],
        coupling[0], *live, near, far, dirichlet,
        kinds=[jnp.bfloat16, jnp.float32, jnp.bfloat16, jnp.bfloat16, jnp.float32],
    )

    edge, first_z, values = call(
        corner_kernel,
        edges_shapes + [(own, loads)],
        first, rest, near, far, *live, stacked, solve,
    )
    everyone = lax.all_gather(values, "grp", tiled=True)
    everyone, blocks = lax.optimization_barrier((everyone, blocks))
    block = jnp.concatenate(split_outside(sum(blocks[1:], blocks[0])), axis=0)
    inner_shape, result_shape = (subs - 1, loads, width), (subs, loads, 2 * width)
    inner, near, far, sums = call(
        first_dual_kernel,
        [inner_shape, longer_shape, longer_shape, scalars_shape],
        edge, first_z, residual[1], solve, everyone, block, lift, live[1],
        for_next, for_prev, given,
        scratch=[pltpu.VMEM(result_shape, jnp.float32)],
    )
    sums = from_all(sums)
    sent = near, far
    near, far = swap(near, far)
    image_own, image_edge, *residual, near, far, scalars_first, ends, outside_image, outside = call(
        first_update_kernel,
        [own_shape, face_shape] + edges_shapes
        + [face_shape, face_shape, scalars_shape, (2,) + side_shape, outside_shape, outside_shape],
        inner, near, far, *sent, *live, sums, *residual, dirichlet, ends,
    )

    def inside(residual, outside):
        (values,) = call(early_corner_kernel, [(own, loads)], taken, ends, outside, *residual)
        everyone = lax.all_gather(values, "grp", tiled=True)
        (inner,) = call(inner_edges_kernel, [inner_shape], *residual, dirichlet, live[1])
        result, partial = call(
            inner_dual_kernel,
            [result_shape, (2,) + face_shape],
            inner, residual[1], solve, everyone, block, lift,
        )
        return result, inner, partial

    sent = near, far
    near, far = swap(near, far)
    result, second_inner, partial = inside(residual, outside)
    second_last, inner, near, far, sums = call(
        functools.partial(outer_dual_kernel, False),
        [face_shape, inner_shape, long_shape, long_shape, scalars_shape],
        result, second_inner, partial, near, far, *sent, *live, residual[1], solve,
        for_next, for_prev,
    )
    sums = from_all(sums)
    sent = near, far
    near, far = swap(near, far)
    image_own, *residual, near, far, scalars_second, outside = call(
        update_kernel,
        [own_shape] + edges_shapes + [face_shape, face_shape, scalars_shape, outside_shape],
        inner, near, far, *sent, *live, sums, scalars_first, image_edge, image_own, *residual,
        dirichlet, outside_image, outside,
    )

    sent = near, far
    near, far = swap(near, far)
    result, third_inner, partial = inside(residual, outside)
    third_last, inner, to_next, to_prev, sums = call(
        functools.partial(outer_dual_kernel, True),
        [face_shape, inner_shape, face_shape, face_shape, scalars_shape],
        result, third_inner, partial, near, far, *sent, *live, residual[1], solve,
    )
    sums = from_all(sums)
    following = lax.ppermute(to_prev, "sub", [(i + 1, i) for i in range(size - 1)])
    multipliers, residual = call(
        last_kernel,
        [own_shape] * 2,
        inner, to_next, following, live[1], sums, scalars_second, scalars_first,
        image_own, residual[1], first_z, second_inner, second_last, third_inner, third_last,
    )
    return (multipliers[None], residual[None])


def solution(mesh):
    return jax.shard_map(
        local,
        mesh=mesh,
        in_specs=(
            P("grp", "sub", None, None),
            P("grp", "sub"),
            P("grp", "sub", None, None),
            P("grp", "sub", None, None),
            P("grp", "sub", None, None),
            P("grp", "sub", None),
            P("sub", "grp", None),
        ),
        out_specs=(P("grp", "sub", None, None), P("grp", "sub", None, None)),
        check_vma=False,
    )
```

```python
import functools

import jax
import jax.numpy as jnp
from jax import lax
from jax.experimental import pallas as pl
from jax.experimental.pallas import tpu as pltpu
from jax.sharding import PartitionSpec as P

VMEM_LIMIT = 8 * 1024 * 1024
TAIL_LIMIT = 62 * 1024 * 1024


def split(values):
    high = values.astype(jnp.bfloat16)
    return high, (values - high.astype(jnp.float32)).astype(jnp.bfloat16)


def split_outside(values):
    high = lax.reduce_precision(values, exponent_bits=8, mantissa_bits=7)
    return high.astype(jnp.bfloat16), (values - high).astype(jnp.bfloat16)


def mul(first, second):
    return jnp.dot(first, second, preferred_element_type=jnp.float32)


def mul_rows(first, second):
    dims = (((1,), (1,)), ((), ()))
    return lax.dot_general(first, second, dims, preferred_element_type=jnp.float32)


def call(kernel, out_shapes, *operands, kinds=None, scratch=()):
    kinds = kinds or [jnp.float32] * len(out_shapes)
    return pl.pallas_call(
        kernel,
        out_shape=[jax.ShapeDtypeStruct(*shape) for shape in zip(out_shapes, kinds)],
        in_specs=[pl.BlockSpec(memory_space=pltpu.VMEM)] * len(operands),
        out_specs=[pl.BlockSpec(memory_space=pltpu.VMEM)] * len(out_shapes),
        scratch_shapes=list(scratch),
        compiler_params=pltpu.CompilerParams(vmem_limit_bytes=VMEM_LIMIT),
    )(*operands)


class Joined:
    def __init__(self, first, rest):
        self.first, self.rest = first, rest

    def __getitem__(self, place):
        return self.first[...] if place == 0 else self.rest[place - 1]

    def __setitem__(self, place, value):
        if place == 0:
            self.first[...] = value
        else:
            self.rest[place - 1] = value


def outer_rows(operator, edge):
    rows = operator.shape[0] // 2
    high, low = split(edge)
    both = mul_rows(operator[...], high)
    return both[:rows] + both[rows:] + mul_rows(operator[:rows], low)


def send(even, to_next, to_prev, near_out, far_out):
    row = 0
    for ahead, behind in zip(to_next, to_prev):
        rows = slice(row, row + ahead.shape[0])
        near_out[rows, :] = jnp.where(even, ahead, behind)
        far_out[rows, :] = jnp.where(even, behind, ahead)
        row += ahead.shape[0]


def column(row, width):
    lanes = jnp.broadcast_to(row, (128, row.shape[1])).T
    return jnp.concatenate([lanes] * (width // 128), axis=1)


def row_sums(values):
    half = values.shape[1] // 2
    return jnp.sum((values[:, :half] + values[:, half:]).T, axis=0, keepdims=True)


def step_scalars(step, sums, before):
    totals = jnp.sum(sums[...], axis=0)
    rz_now, curvature = totals[:1], totals[1:2]
    if step == 0:
        return rz_now, rz_now / curvature, None
    beta = rz_now / before[0:1]
    return rz_now, rz_now / (curvature - beta * rz_now / before[1:2]), beta


def even_place():
    return lax.rem(lax.axis_index("sub"), 2) == 0


def live_rows(counts, sub, rows, width):
    last = lax.axis_index("sub") == lax.axis_size("sub") - 1
    count = jnp.broadcast_to(counts[:, sub : sub + 1], (rows, width))
    if sub == counts.shape[1] - 1:
        count = jnp.where(last, 0, count)
    return (lax.broadcasted_iota(jnp.int32, (rows, width), 1) < count).astype(jnp.float32)


def tail_kernel(counts_ref, rhs, tail, counts, face, counts_done, face_done):
    loads, width = rhs.shape[2:]
    counts_copy = pltpu.make_async_copy(counts_ref, counts, counts_done)
    face_copy = pltpu.make_async_copy(rhs.at[0, rhs.shape[1] - 1], face, face_done)
    counts_copy.start()
    face_copy.start()
    counts_copy.wait()
    mask = live_rows(counts, counts.shape[1] - 1, 8, width)
    tail[loads:] = mask
    face_copy.wait()
    tail[:loads] = mask[:1] * face[...]


def early_kernel(counts, rhs, panel, live, own, to_next, partial):
    subs, loads, width = own.shape
    parts = []
    for sub in range(subs):
        mask = live_rows(counts, sub, 1, width)
        live[sub] = mask
        own[sub] = mask * rhs[sub]
        parts.append(split(own[sub]))
    high = jnp.concatenate([-parts[subs - 2][0], parts[subs - 1][0]], axis=1)
    low = jnp.concatenate([-parts[subs - 2][1], parts[subs - 1][1]], axis=1)
    to_next[...] = mul(high, panel[subs - 1, :, width:]) + mul(low, panel[subs - 1, :, width:])
    high, low = parts[0]
    partial[...] = mul(high, panel[0, width:, :width]) + mul(low, panel[0, width:, :width])


def head_kernel(head, to_next, partial, panel, coupling, live, edge, near_out, far_out):
    loads, width = edge.shape
    live[...] = head[loads : loads + 1]
    edge[...] = head[:loads]
    high, low = split(head[:loads])
    to_prev = partial[...] - (
        mul(high, panel[0, :width, :width]) + mul(low, panel[0, :width, :width])
    )
    ahead = [to_next[...], coupling[coupling.shape[0] - 1, :, width:]]
    send(even_place(), ahead, [to_prev, coupling[0, :, :width]], near_out, far_out)


def setup_kernel(*refs):
    group = (len(refs) - 5) // 2
    maps, (coarse, coupling) = refs[:group], refs[group : group + 2]
    picked, (stacked, lift, everyone) = refs[group + 2 : -3], refs[-3:]
    subs, corners = maps[0].shape
    rows, size = coarse.shape
    own = subs * corners
    grp = lax.axis_index("grp")
    for sub in range(subs):
        high, low = split(coupling[sub])
        spare = jnp.zeros((lift.shape[1] - 3 * corners, high.shape[1]), jnp.bfloat16)
        stacked[sub] = jnp.concatenate([high, low], axis=0)
        lift[sub] = jnp.concatenate([high, high, low, spare], axis=0)
    for distance in range(group):
        unknowns = [maps[distance][sub : sub + 1, :] for sub in range(subs)]
        everyone[distance] = jnp.concatenate(unknowns, axis=1)
    high, low = split(coarse[...])
    unknowns = lax.broadcasted_iota(jnp.int32, (size, own), 0)
    columns = []
    for member in range(group):
        chosen = (unknowns == everyone[grp ^ member]).astype(jnp.bfloat16)
        columns.append(mul(high, chosen) + mul(low, chosen))
    high, low = split(jnp.concatenate(columns, axis=1))
    owned = lax.broadcasted_iota(jnp.int32, (rows, own), 0) + grp * rows
    dims = (((0,), (0,)), ((), ()))
    for distance in range(group):
        chosen = (owned == everyone[distance]).astype(jnp.bfloat16)
        picked[distance][...] = lax.dot_general(
            chosen, high, dims, preferred_element_type=jnp.float32
        ) + lax.dot_general(chosen, low, dims, preferred_element_type=jnp.float32)


def start_kernel(inner, panel, coupling, result, corners):
    subs, rows = coupling.shape[0], coupling.shape[1] // 2
    width = inner.shape[2]
    parts = [split(inner[place]) for place in range(subs - 1)]
    high, low = parts[0]
    result[0] = mul(high, panel[0, width:]) + mul(low, panel[0, width:])
    for sub in range(1, subs - 1):
        high = jnp.concatenate([-parts[sub - 1][0], parts[sub][0]], axis=1)
        low = jnp.concatenate([-parts[sub - 1][1], parts[sub][1]], axis=1)
        result[sub] = mul(high, panel[sub]) + mul(low, panel[sub])
    high, low = parts[subs - 2]
    result[subs - 1] = -(mul(high, panel[subs - 1, :width]) + mul(low, panel[subs - 1, :width]))
    for sub in range(subs):
        values = jnp.zeros((rows, inner.shape[1]), jnp.float32)
        if sub > 0:
            values = values - outer_rows(coupling[sub, :, :width], inner[sub - 1])
        if sub + 1 < subs:
            values = values + outer_rows(coupling[sub, :, width:], inner[sub])
        corners[sub * rows : (sub + 1) * rows, :] = values


def corner_kernel(near, far, near_sent, far_sent, live_edge, live_own, coupling, partial,
                  edge, last, corners):
    subs, rows = coupling.shape[0], coupling.shape[1] // 2
    loads, width = edge.shape
    first_value, last_value = cut_edges(even_place(), loads, near, far, near_sent, far_sent,
                                        0.25 * live_edge[...], 0.25 * live_own[subs - 1])
    edge[...] = first_value
    last[...] = last_value
    corners[...] = partial[...]
    corners[:rows, :] = partial[:rows, :] - outer_rows(coupling[0, :, :width], first_value)
    corners[-rows:, :] = partial[-rows:, :] + outer_rows(
        coupling[subs - 1, :, width:], last_value
    )


def operators_kernel(coupling, live_edge, live_own, panel, taken, ends):
    subs, rows = coupling.shape[0], coupling.shape[1]
    width = coupling.shape[2] // 2
    live = Joined(live_edge, live_own)
    left = [coupling[sub, :, :width] * (0.25 * live[sub]) for sub in range(subs)]
    right = [coupling[sub, :, width:] * (0.25 * live[sub + 1]) for sub in range(subs)]
    none = jnp.zeros((rows, width), jnp.float32)
    inner, ahead, behind = [], [], []
    for sub in range(subs):
        above = left[sub + 1] if sub + 1 < subs else none
        below = right[sub - 1] if sub > 0 else none
        factors = jnp.concatenate(
            [
                jnp.concatenate([left[sub], right[sub]], axis=1),
                jnp.concatenate([none, above], axis=1),
                jnp.concatenate([below, none], axis=1),
            ],
            axis=0,
        )
        both = mul(jnp.concatenate(split(factors), axis=0), panel[sub])
        product = both[: 3 * rows] + both[3 * rows :]
        inner.append(product[:rows])
        ahead.append(product[rows : 2 * rows])
        behind.append(product[2 * rows :])
    total = subs * rows
    for sub in range(subs):
        blocks = [none] * (subs + 1)
        blocks[sub] = -inner[sub][:, :width]
        blocks[sub + 1] = inner[sub][:, width:]
        if sub > 0:
            blocks[sub - 1] = ahead[sub - 1][:, :width]
            blocks[sub] = blocks[sub] - ahead[sub - 1][:, width:]
        if sub + 1 < subs:
            blocks[sub + 1] = blocks[sub + 1] + behind[sub + 1][:, :width]
            blocks[sub + 2] = -behind[sub + 1][:, width:]
        if sub == 0:
            ends[0] = blocks[0]
            blocks[0] = none
        if sub == subs - 1:
            ends[1] = blocks[subs]
            blocks[subs] = none
        high, low = split(jnp.concatenate(blocks, axis=1))
        taken[sub * rows : (sub + 1) * rows, :] = high
        taken[total + sub * rows : total + (sub + 1) * rows, :] = low


def early_corner_kernel(taken, ends, outside, edge, own, corners):
    subs, rows = own.shape[0], ends.shape[1]
    total = subs * rows
    edges = Joined(edge, own)
    parts = [split(edges[place]) for place in range(subs + 1)]
    high = jnp.concatenate([part[0] for part in parts], axis=1)
    low = jnp.concatenate([part[1] for part in parts], axis=1)
    both = mul_rows(taken[...], high)
    values = both[:total] + both[total:] + mul_rows(taken[:total], low)
    corners[...] = values
    for end, place in ((0, 0), (1, subs)):
        operator = jnp.concatenate(split(ends[end]), axis=0)
        row = end * (total - rows)
        corners[row : row + rows, :] = (
            values[row : row + rows]
            + outer_rows(operator, edges[place])
            + outside[end * rows : (end + 1) * rows, :]
        )


def coarse_lift(everyone, block, lift):
    subs = lift.shape[0]
    rows = block.shape[0] // 2
    high, low = split(everyone[...])
    both = mul(block[...], high)
    back = both[:rows] + both[rows:] + mul(block[:rows], low)
    corners = rows // subs

    def lifted(sub):
        own = back[sub * corners : (sub + 1) * corners]
        own_high = own.astype(jnp.bfloat16).astype(jnp.float32)
        terms = [own_high, own - own_high, own_high]
        spare = jnp.zeros((lift.shape[1] - 3 * corners, own.shape[1]), jnp.float32)
        return mul(jnp.concatenate(terms + [spare], axis=0).T.astype(jnp.bfloat16), lift[sub])

    return lifted


def on_subdomain(values, left, right):
    width = left.shape[1]
    return values[:, width:] * right - values[:, :width] * left


def send_dual(even, inner, faces, for_next, for_prev, near_out, far_out, residual=None,
              given=None):
    to_next, to_prev = [faces[0]], [faces[1]]
    count = inner.shape[0]
    if given is not None:
        to_next += [given[0], outer_rows(for_next, residual[count - 1])]
        to_prev += [given[1], outer_rows(for_prev, residual[0])]
    to_next.append(outer_rows(for_next, inner[count - 1]))
    to_prev.append(outer_rows(for_prev, inner[0]))
    send(even, to_next, to_prev, near_out, far_out)


def inner_jump(result, live_own, inner):
    width = inner.shape[2]
    for place in range(inner.shape[0]):
        inner[place] = live_own[place] * (result[place][:, width:] - result[place + 1][:, :width])


def first_dual_kernel(before, inner_z, edge, last_z, residual, panel, everyone, block, lift,
                      near, far, live_edge, live_own, preconditioner,
                      inner, near_out, far_out, sums, for_next, for_prev, result):
    even = even_place()
    subs, (loads, width) = panel.shape[0], edge.shape
    rows = for_next.shape[0] // 2
    sides = received(even, near, far, loads, rows)
    after = sides[rows:] * (0.25 * live_own[subs - 1])
    behind = sides[:rows] * (0.25 * live_edge[...])
    both = mul(jnp.concatenate(split(after), axis=0), preconditioner[subs - 1, width:])
    after = both[:rows] + both[rows:]
    both = mul(jnp.concatenate(split(behind), axis=0), preconditioner[0, :width])
    behind = both[:rows] + both[rows:]
    for_next[...] = jnp.concatenate(split(after[:, :width]), axis=0)
    for_prev[...] = jnp.concatenate(split(-behind[:, width:]), axis=0)
    given = [-after[:, width:], behind[:, :width]]

    lifted = coarse_lift(everyone, block, lift)
    for sub in range(subs):
        value = before[sub] + lifted(sub)
        if sub == 0:
            high, low = split(edge[...])
            value = value - (mul(high, panel[0, :width]) + mul(low, panel[0, :width]))
        if sub == subs - 1:
            high, low = split(last_z[...])
            value = value + (mul(high, panel[sub, width:]) + mul(low, panel[sub, width:]))
        result[sub] = value
    inner_jump(result, live_own, inner)
    faces = [result[subs - 1][:, width:], result[0][:, :width]]
    send_dual(even, inner, faces, for_next, for_prev, near_out, far_out, residual, given)
    edges = [edge[...]] + [inner_z[place] for place in range(subs - 1)] + [last_z[...]]
    product = curvature = 0.0
    for sub in range(subs):
        product = product + residual[sub] * edges[sub + 1]
        curvature = curvature + on_subdomain(result[sub], edges[sub], edges[sub + 1])
    sums[...] = jnp.concatenate([row_sums(product), row_sums(curvature)], axis=0)


def inner_edges_kernel(edge, own, panel, live_own, inner):
    subs, width = panel.shape[0], edge.shape[1]
    edges = Joined(edge, own)
    parts = [split(edges[place]) for place in range(subs + 1)]

    def half(sub, columns):
        high = jnp.concatenate([-parts[sub][0], parts[sub + 1][0]], axis=1)
        low = jnp.concatenate([-parts[sub][1], parts[sub + 1][1]], axis=1)
        return mul(high, panel[sub, :, columns]) + mul(low, panel[sub, :, columns])

    for place in range(subs - 1):
        right = half(place, slice(width, 2 * width))
        left = half(place + 1, slice(0, width))
        inner[place] = (0.25 * live_own[place]) * (right - left)


def inner_dual_kernel(inner, residual, panel, everyone, block, lift, result, partial):
    subs, width = panel.shape[0], inner.shape[2]
    lifted = coarse_lift(everyone, block, lift)
    parts = [split(inner[place]) for place in range(subs - 1)]
    high, low = parts[0]
    result[0] = mul(high, panel[0, width:]) + mul(low, panel[0, width:]) + lifted(0)
    product = residual[0] * inner[0]
    curvature = jnp.zeros_like(product)
    for sub in range(1, subs - 1):
        high = jnp.concatenate([-parts[sub - 1][0], parts[sub][0]], axis=1)
        low = jnp.concatenate([-parts[sub - 1][1], parts[sub][1]], axis=1)
        result[sub] = mul(high, panel[sub]) + mul(low, panel[sub]) + lifted(sub)
        product = product + residual[sub] * inner[sub]
        curvature = curvature + on_subdomain(result[sub], inner[sub - 1], inner[sub])
    high, low = parts[subs - 2]
    result[subs - 1] = lifted(subs - 1) - (
        mul(high, panel[subs - 1, :width]) + mul(low, panel[subs - 1, :width])
    )
    partial[0] = product
    partial[1] = curvature


def cut_edges(even, loads, near, far, near_sent, far_sent, live_first, live_last):
    near, far, near_sent, far_sent = near[:loads], far[:loads], near_sent[:loads], far_sent[:loads]
    first = live_first * jnp.where(even, far - far_sent, near - near_sent)
    last = live_last * jnp.where(even, near_sent - near, far_sent - far)
    return first, last


def outer_dual_kernel(closing, *refs):
    before, inner_z, partial, near, far, near_sent, far_sent, live_edge, live_own = refs[:9]
    residual, panel = refs[9:11]
    even, subs, width = even_place(), panel.shape[0], near_sent.shape[1]
    edge, last = cut_edges(even, residual.shape[1], near, far, near_sent, far_sent,
                           0.25 * live_edge[...], 0.25 * live_own[subs - 1])
    if closing:
        last_z, inner, to_next, to_prev, sums = refs[11:]
    else:
        for_next, for_prev, last_z, inner, near_out, far_out, sums = refs[11:]
    last_z[...] = last
    high, low = split(edge)
    result_first = before[0] - (mul(high, panel[0, :width]) + mul(low, panel[0, :width]))
    high, low = split(last)
    result_last = before[subs - 1] + (
        mul(high, panel[subs - 1, width:]) + mul(low, panel[subs - 1, width:])
    )
    result = [result_first] + [before[sub] for sub in range(1, subs - 1)] + [result_last]
    inner_jump(result, live_own, inner)
    faces = [result_last[:, width:], result_first[:, :width]]
    if closing:
        to_next[...], to_prev[...] = faces
    else:
        send_dual(even, inner, faces, for_next, for_prev, near_out, far_out)
    product = partial[0] + residual[subs - 1] * last
    curvature = partial[1] + on_subdomain(result_first, edge, inner_z[0])
    curvature = curvature + on_subdomain(result_last, inner_z[subs - 2], last)
    sums[...] = jnp.concatenate([row_sums(product), row_sums(curvature)], axis=0)


def received(even, near, far, start, rows):
    part = slice(start, start + rows)
    return jnp.concatenate(
        [jnp.where(even, far[part], near[part]), jnp.where(even, near[part], far[part])], axis=0
    )


def send_outer(parts, panel, near_out, far_out):
    subs, width = panel.shape[0], near_out.shape[1]

    def half(sub, columns):
        high = jnp.concatenate([-parts[sub][0], parts[sub + 1][0]], axis=1)
        low = jnp.concatenate([-parts[sub][1], parts[sub + 1][1]], axis=1)
        return mul(high, panel[sub, :, columns]) + mul(low, panel[sub, :, columns])

    to_next = half(subs - 1, slice(width, 2 * width))
    send(even_place(), [to_next], [half(0, slice(0, width))], near_out, far_out)


def image_edges(even, inner, near, far, near_sent, far_sent, live_edge, live_own):
    subs = live_own.shape[0]
    edge, last = cut_edges(even, inner.shape[1], near, far, near_sent, far_sent, live_edge[...],
                           live_own[subs - 1])
    return [edge] + [inner[place] for place in range(subs - 1)] + [last]


def first_update_kernel(inner, near, far, near_sent, far_sent, live_edge, live_own, sums,
                        residual_edge, residual_own, panel, ends,
                        image_own, image_edge, new_edge, new_own,
                        near_out, far_out, scalars, full_ends, outside_image, outside):
    even = even_place()
    loads, width = residual_edge.shape
    subs, rows = panel.shape[0], ends.shape[1]
    residual, image = Joined(residual_edge, residual_own), Joined(image_edge, image_own)
    residual_new = Joined(new_edge, new_own)
    rz_now, alpha, _ = step_scalars(0, sums, None)
    scalars[...] = jnp.concatenate([rz_now, alpha], axis=0)
    operators = received(even, near, far, loads, rows)
    full_ends[0] = ends[0] + operators[:rows]
    full_ends[1] = ends[1] + operators[rows:]
    values = received(even, near, far, loads + 2 * rows, rows)
    outside_image[...] = values
    outside[...] = received(even, near, far, loads + rows, rows) - alpha * values
    alpha_column = column(alpha, width)
    parts = []
    edges = image_edges(even, inner, near, far, near_sent, far_sent, live_edge, live_own)
    for place, value in enumerate(edges):
        image[place] = value
        residual_new[place] = residual[place] - alpha_column * value
        parts.append(split(residual_new[place]))
    send_outer(parts, panel, near_out, far_out)


def update_kernel(inner, near, far, near_sent, far_sent, live_edge, live_own, sums, before,
                  old_edge, old_own, residual_edge, residual_own, panel,
                  outside_image_old, outside_old,
                  image_own, new_edge, new_own, near_out, far_out, scalars, outside):
    even = even_place()
    loads, width = residual_edge.shape
    rows = outside.shape[0] // 2
    image_old, residual = Joined(old_edge, old_own), Joined(residual_edge, residual_own)
    residual_new = Joined(new_edge, new_own)
    rz_now, alpha, beta = step_scalars(1, sums, before)
    scalars[...] = jnp.concatenate([rz_now, alpha], axis=0)
    values = received(even, near, far, loads, rows) + beta * outside_image_old[...]
    outside[...] = outside_old[...] - alpha * values
    alpha_column, beta_column = column(alpha, width), column(beta, width)
    parts = []
    edges = image_edges(even, inner, near, far, near_sent, far_sent, live_edge, live_own)
    for place, value in enumerate(edges):
        value = value + beta_column * image_old[place]
        if place > 0:
            image_own[place - 1] = value
        residual_new[place] = residual[place] - alpha_column * value
        parts.append(split(residual_new[place]))
    send_outer(parts, panel, near_out, far_out)


def last_kernel(inner, to_next, following, live, sums, before, older, image_old,
                residual, first_inner, first_last, second_inner, second_last, third_inner, third_last,
                multipliers, residual_new):
    subs, width = residual.shape[0], following.shape[1]
    rz_now, alpha, beta = step_scalars(2, sums, before)
    beta_before = before[0:1] / older[0:1]
    on_second = before[1:2] + alpha * beta
    on_first = older[1:2] + on_second * beta_before
    alpha_column, beta_column = column(alpha, width), column(beta, width)
    second_column, first_column = column(on_second, width), column(on_first, width)
    for sub in range(subs):
        if sub == subs - 1:
            image = live[sub] * (to_next[...] - following[...])
            first_z, second_z, third_z = first_last[...], second_last[...], third_last[...]
        else:
            image = inner[sub]
            first_z, second_z, third_z = first_inner[sub], second_inner[sub], third_inner[sub]
        image = image + beta_column * image_old[sub]
        residual_new[sub] = residual[sub] - alpha_column * image
        multipliers[sub] = (
            first_column * first_z + second_column * second_z + alpha_column * third_z
        )


def neighbour_pairs(size, first):
    pairs = [(i, i + 1) for i in range(first, size - 1, 2)]
    return [route for a, b in pairs for route in ((a, b), (b, a))]


def swap(near, far):
    size = lax.axis_size("sub")
    return (
        lax.ppermute(near, "sub", neighbour_pairs(size, 0)),
        lax.ppermute(far, "sub", neighbour_pairs(size, 1)),
    )


def from_all(rows):
    size = lax.axis_size("sub") * lax.axis_size("grp")
    copies = jnp.broadcast_to(rows[None], (size,) + rows.shape)
    return lax.all_to_all(copies, ("sub", "grp"), 0, 0)


def from_group(values):
    group = lax.axis_size("grp")
    received = [values]
    for distance in range(1, group):
        routes = [(i, i ^ distance) for i in range(group)]
        received.append(lax.ppermute(values, "grp", routes))
    return received


def swap_blocks(picked):
    group = lax.axis_size("grp")
    received = [picked[0]]
    for distance in range(1, group):
        routes = [(i, i ^ distance) for i in range(group)]
        received.append(lax.ppermute(picked[distance], "grp", routes))
    return received


def make_tail(counts, rhs):
    loads, width = rhs.shape[2:]
    return pl.pallas_call(
        tail_kernel,
        out_shape=jax.ShapeDtypeStruct((loads + 8, width), jnp.float32),
        in_specs=[
            pl.BlockSpec(memory_space=pltpu.HBM),
            pl.BlockSpec(memory_space=pltpu.HBM),
        ],
        out_specs=pl.BlockSpec(memory_space=pltpu.VMEM),
        scratch_shapes=[
            pltpu.VMEM(counts.shape, counts.dtype),
            pltpu.VMEM((loads, width), jnp.float32),
            pltpu.SemaphoreType.DMA,
            pltpu.SemaphoreType.DMA,
        ],
        compiler_params=pltpu.CompilerParams(vmem_limit_bytes=TAIL_LIMIT),
    )(counts, rhs)


def local(rhs, counts, solve_panel, dirichlet_panel, coupling, corner_map, coarse_inverse):
    subs, loads, width = rhs.shape[1:]
    corners = coupling.shape[2]
    solve, dirichlet = solve_panel[0], dirichlet_panel[0]
    size = lax.axis_size("sub")

    face_shape, own_shape = (loads, width), (subs, loads, width)
    scalars_shape, outside_shape, side_shape = (2, loads), (2 * corners, loads), (corners, width)
    long_shape, longer_shape = (loads + corners, width), (loads + 3 * corners, width)
    edges_shapes = [face_shape, own_shape]

    tail = make_tail(counts, rhs)
    tail, counts, corner_map = lax.optimization_barrier((tail, counts, corner_map))
    head = lax.ppermute(tail, "sub", [(i, i + 1) for i in range(size - 1)])
    maps = from_group(corner_map[0])
    live_own, residual_own, to_next, partial = call(
        early_kernel,
        [(subs, 1, width), own_shape, face_shape, face_shape],
        counts, rhs[0], dirichlet,
    )
    group, own = len(maps), subs * corners
    pair = [(corners, width)] * 2
    *picked, stacked, lift = call(
        setup_kernel,
        [(own, group * own)] * group
        + [(subs, 2 * corners, 2 * width), (subs, 3 * corners + -3 * corners % 128, 2 * width)],
        *maps, coarse_inverse[0], coupling[0],
        kinds=[jnp.float32] * group + [jnp.bfloat16] * 2,
        scratch=[pltpu.VMEM((group, 1, own), jnp.int32)],
    )
    head, stacked = lax.optimization_barrier((head, stacked))
    live_edge, residual_edge, near, far = call(
        head_kernel,
        [(1, width), face_shape, long_shape, long_shape],
        head, to_next, partial, dirichlet, coupling[0],
    )
    live, residual = (live_edge, live_own), (residual_edge, residual_own)
    sent = near, far
    near, far = swap(near, far)
    blocks = swap_blocks(picked)
    inner_shape, result_shape = (subs - 1, loads, width), (subs, loads, 2 * width)
    (first_inner,) = call(inner_edges_kernel, [inner_shape], *residual, dirichlet, live[1])
    result, partial = call(
        start_kernel, [result_shape, (own, loads)], first_inner, solve, stacked
    )
    taken, ends = call(
        operators_kernel,
        [(2 * own, (subs + 1) * width), (2,) + side_shape],
        coupling[0], *live, dirichlet,
        kinds=[jnp.bfloat16, jnp.float32],
    )
    partial, taken, ends = lax.optimization_barrier((partial, taken, ends))

    edge, first_last, values = call(
        corner_kernel,
        [face_shape, face_shape, (own, loads)],
        near, far, *sent, *live, stacked, partial,
    )
    everyone = lax.all_gather(values, "grp", tiled=True)
    everyone, blocks = lax.optimization_barrier((everyone, blocks))
    block = jnp.concatenate(split_outside(sum(blocks[1:], blocks[0])), axis=0)
    inner, near, far, sums, for_next, for_prev = call(
        first_dual_kernel,
        [inner_shape, longer_shape, longer_shape, scalars_shape]
        + [(2 * corners, width), (2 * corners, width)],
        result, first_inner, edge, first_last, residual[1], solve, everyone, block, lift,
        near, far, *live, dirichlet,
        kinds=[jnp.float32] * 4 + [jnp.bfloat16] * 2,
        scratch=[pltpu.VMEM(result_shape, jnp.float32)],
    )
    sums = from_all(sums)
    sent = near, far
    near, far = swap(near, far)
    image_own, image_edge, *residual, near, far, scalars_first, ends, outside_image, outside = call(
        first_update_kernel,
        [own_shape, face_shape] + edges_shapes
        + [face_shape, face_shape, scalars_shape, (2,) + side_shape, outside_shape, outside_shape],
        inner, near, far, *sent, *live, sums, *residual, dirichlet, ends,
    )

    def inside(residual, outside):
        (values,) = call(early_corner_kernel, [(own, loads)], taken, ends, outside, *residual)
        everyone = lax.all_gather(values, "grp", tiled=True)
        (inner,) = call(inner_edges_kernel, [inner_shape], *residual, dirichlet, live[1])
        result, partial = call(
            inner_dual_kernel,
            [result_shape, (2,) + face_shape],
            inner, residual[1], solve, everyone, block, lift,
        )
        return result, inner, partial

    sent = near, far
    near, far = swap(near, far)
    result, second_inner, partial = inside(residual, outside)
    second_last, inner, near, far, sums = call(
        functools.partial(outer_dual_kernel, False),
        [face_shape, inner_shape, long_shape, long_shape, scalars_shape],
        result, second_inner, partial, near, far, *sent, *live, residual[1], solve,
        for_next, for_prev,
    )
    sums = from_all(sums)
    sent = near, far
    near, far = swap(near, far)
    image_own, *residual, near, far, scalars_second, outside = call(
        update_kernel,
        [own_shape] + edges_shapes + [face_shape, face_shape, scalars_shape, outside_shape],
        inner, near, far, *sent, *live, sums, scalars_first, image_edge, image_own, *residual,
        dirichlet, outside_image, outside,
    )

    sent = near, far
    near, far = swap(near, far)
    result, third_inner, partial = inside(residual, outside)
    third_last, inner, to_next, to_prev, sums = call(
        functools.partial(outer_dual_kernel, True),
        [face_shape, inner_shape, face_shape, face_shape, scalars_shape],
        result, third_inner, partial, near, far, *sent, *live, residual[1], solve,
    )
    sums = from_all(sums)
    following = lax.ppermute(to_prev, "sub", [(i + 1, i) for i in range(size - 1)])
    multipliers, residual = call(
        last_kernel,
        [own_shape] * 2,
        inner, to_next, following, live[1], sums, scalars_second, scalars_first,
        image_own, residual[1], first_inner, first_last, second_inner, second_last, third_inner, third_last,
    )
    return (multipliers[None], residual[None])


def solution(mesh):
    return jax.shard_map(
        local,
        mesh=mesh,
        in_specs=(
            P("grp", "sub", None, None),
            P("grp", "sub"),
            P("grp", "sub", None, None),
            P("grp", "sub", None, None),
            P("grp", "sub", None, None),
            P("grp", "sub", None),
            P("sub", "grp", None),
        ),
        out_specs=(P("grp", "sub", None, None), P("grp", "sub", None, None)),
        check_vma=False,
    )
```

```python
import functools

import jax
import jax.numpy as jnp
from jax import lax
from jax.experimental import pallas as pl
from jax.experimental.pallas import tpu as pltpu
from jax.sharding import PartitionSpec as P

VMEM_LIMIT = 8 * 1024 * 1024
TAIL_LIMIT = 62 * 1024 * 1024


def split(values):
    high = values.astype(jnp.bfloat16)
    return high, (values - high.astype(jnp.float32)).astype(jnp.bfloat16)


def split_outside(values):
    high = lax.reduce_precision(values, exponent_bits=8, mantissa_bits=7)
    return high.astype(jnp.bfloat16), (values - high).astype(jnp.bfloat16)


def mul(first, second):
    return jnp.dot(first, second, preferred_element_type=jnp.float32)


def mul_rows(first, second):
    dims = (((1,), (1,)), ((), ()))
    return lax.dot_general(first, second, dims, preferred_element_type=jnp.float32)


def call(kernel, out_shapes, *operands, kinds=None, scratch=()):
    kinds = kinds or [jnp.float32] * len(out_shapes)
    return pl.pallas_call(
        kernel,
        out_shape=[jax.ShapeDtypeStruct(*shape) for shape in zip(out_shapes, kinds)],
        in_specs=[pl.BlockSpec(memory_space=pltpu.VMEM)] * len(operands),
        out_specs=[pl.BlockSpec(memory_space=pltpu.VMEM)] * len(out_shapes),
        scratch_shapes=list(scratch),
        compiler_params=pltpu.CompilerParams(vmem_limit_bytes=VMEM_LIMIT),
    )(*operands)


class Joined:
    def __init__(self, first, rest):
        self.first, self.rest = first, rest

    def __getitem__(self, place):
        return self.first[...] if place == 0 else self.rest[place - 1]

    def __setitem__(self, place, value):
        if place == 0:
            self.first[...] = value
        else:
            self.rest[place - 1] = value


def outer_rows(operator, edge):
    rows = operator.shape[0] // 2
    high, low = split(edge)
    both = mul_rows(operator[...], high)
    return both[:rows] + both[rows:] + mul_rows(operator[:rows], low)


def send(even, to_next, to_prev, near_out, far_out):
    row = 0
    for ahead, behind in zip(to_next, to_prev):
        rows = slice(row, row + ahead.shape[0])
        near_out[rows, :] = jnp.where(even, ahead, behind)
        far_out[rows, :] = jnp.where(even, behind, ahead)
        row += ahead.shape[0]


def column(row, width):
    lanes = jnp.broadcast_to(row, (128, row.shape[1])).T
    return jnp.concatenate([lanes] * (width // 128), axis=1)


def row_sums(values):
    half = values.shape[1] // 2
    return jnp.sum((values[:, :half] + values[:, half:]).T, axis=0, keepdims=True)


def step_scalars(step, sums, before):
    totals = jnp.sum(sums[...], axis=0)
    rz_now, curvature = totals[:1], totals[1:2]
    if step == 0:
        return rz_now, rz_now / curvature, None
    beta = rz_now / before[0:1]
    return rz_now, rz_now / (curvature - beta * rz_now / before[1:2]), beta


def even_place():
    return lax.rem(lax.axis_index("sub"), 2) == 0


def live_rows(counts, sub, rows, width):
    last = lax.axis_index("sub") == lax.axis_size("sub") - 1
    count = jnp.broadcast_to(counts[:, sub : sub + 1], (rows, width))
    if sub == counts.shape[1] - 1:
        count = jnp.where(last, 0, count)
    return (lax.broadcasted_iota(jnp.int32, (rows, width), 1) < count).astype(jnp.float32)


def tail_kernel(counts_ref, rhs, tail, counts, face, counts_done, face_done):
    loads, width = rhs.shape[2:]
    counts_copy = pltpu.make_async_copy(counts_ref, counts, counts_done)
    face_copy = pltpu.make_async_copy(rhs.at[0, rhs.shape[1] - 1], face, face_done)
    counts_copy.start()
    face_copy.start()
    counts_copy.wait()
    mask = live_rows(counts, counts.shape[1] - 1, 8, width)
    tail[loads:] = mask
    face_copy.wait()
    tail[:loads] = mask[:1] * face[...]


def early_kernel(counts, rhs, panel, live, own, to_next, partial):
    subs, loads, width = own.shape
    parts = []
    for sub in range(subs):
        mask = live_rows(counts, sub, 1, width)
        live[sub] = mask
        own[sub] = mask * rhs[sub]
        parts.append(split(own[sub]))
    high = jnp.concatenate([-parts[subs - 2][0], parts[subs - 1][0]], axis=1)
    low = jnp.concatenate([-parts[subs - 2][1], parts[subs - 1][1]], axis=1)
    to_next[...] = mul(high, panel[subs - 1, :, width:]) + mul(low, panel[subs - 1, :, width:])
    high, low = parts[0]
    partial[...] = mul(high, panel[0, width:, :width]) + mul(low, panel[0, width:, :width])


def head_kernel(head, to_next, partial, panel, coupling, live, edge, near_out, far_out):
    loads, width = edge.shape
    live[...] = head[loads : loads + 1]
    edge[...] = head[:loads]
    high, low = split(head[:loads])
    to_prev = partial[...] - (
        mul(high, panel[0, :width, :width]) + mul(low, panel[0, :width, :width])
    )
    ahead = [to_next[...], coupling[coupling.shape[0] - 1, :, width:]]
    send(even_place(), ahead, [to_prev, coupling[0, :, :width]], near_out, far_out)


def setup_kernel(*refs):
    group = (len(refs) - 5) // 2
    maps, (coarse, coupling) = refs[:group], refs[group : group + 2]
    picked, (stacked, lift, everyone) = refs[group + 2 : -3], refs[-3:]
    subs, corners = maps[0].shape
    rows, size = coarse.shape
    own = subs * corners
    grp = lax.axis_index("grp")
    for sub in range(subs):
        high, low = split(coupling[sub])
        spare = jnp.zeros((lift.shape[1] - 3 * corners, high.shape[1]), jnp.bfloat16)
        stacked[sub] = jnp.concatenate([high, low], axis=0)
        lift[sub] = jnp.concatenate([high, high, low, spare], axis=0)
    for distance in range(group):
        unknowns = [maps[distance][sub : sub + 1, :] for sub in range(subs)]
        everyone[distance] = jnp.concatenate(unknowns, axis=1)
    high, low = split(coarse[...])
    together = max(1, 512 // own)
    columns = []
    for start in range(0, group, together):
        members = range(start, min(start + together, group))
        wanted = jnp.concatenate([everyone[grp ^ member] for member in members], axis=1)
        unknowns = lax.broadcasted_iota(jnp.int32, (size, wanted.shape[1]), 0)
        chosen = (unknowns == wanted).astype(jnp.bfloat16)
        columns.append(mul(high, chosen) + mul(low, chosen))
    high, low = split(jnp.concatenate(columns, axis=1))
    dims = (((0,), (0,)), ((), ()))
    for start in range(0, group, together):
        distances = range(start, min(start + together, group))
        wanted = jnp.concatenate([everyone[distance] for distance in distances], axis=1)
        owned = lax.broadcasted_iota(jnp.int32, (rows, wanted.shape[1]), 0) + grp * rows
        chosen = (owned == wanted).astype(jnp.bfloat16)
        values = lax.dot_general(
            chosen, high, dims, preferred_element_type=jnp.float32
        ) + lax.dot_general(chosen, low, dims, preferred_element_type=jnp.float32)
        for place, distance in enumerate(distances):
            picked[distance][...] = values[place * own : (place + 1) * own]


def start_kernel(inner, panel, coupling, result, corners):
    subs, rows = coupling.shape[0], coupling.shape[1] // 2
    width = inner.shape[2]
    parts = [split(inner[place]) for place in range(subs - 1)]
    high, low = parts[0]
    result[0] = mul(high, panel[0, width:]) + mul(low, panel[0, width:])
    for sub in range(1, subs - 1):
        high = jnp.concatenate([-parts[sub - 1][0], parts[sub][0]], axis=1)
        low = jnp.concatenate([-parts[sub - 1][1], parts[sub][1]], axis=1)
        result[sub] = mul(high, panel[sub]) + mul(low, panel[sub])
    high, low = parts[subs - 2]
    result[subs - 1] = -(mul(high, panel[subs - 1, :width]) + mul(low, panel[subs - 1, :width]))
    for sub in range(subs):
        values = jnp.zeros((rows, inner.shape[1]), jnp.float32)
        if sub > 0:
            values = values - outer_rows(coupling[sub, :, :width], inner[sub - 1])
        if sub + 1 < subs:
            values = values + outer_rows(coupling[sub, :, width:], inner[sub])
        corners[sub * rows : (sub + 1) * rows, :] = values


def corner_kernel(near, far, near_sent, far_sent, live_edge, live_own, coupling, partial,
                  edge, last, corners):
    subs, rows = coupling.shape[0], coupling.shape[1] // 2
    loads, width = edge.shape
    first_value, last_value = cut_edges(even_place(), loads, near, far, near_sent, far_sent,
                                        0.25 * live_edge[...], 0.25 * live_own[subs - 1])
    edge[...] = first_value
    last[...] = last_value
    corners[...] = partial[...]
    corners[:rows, :] = partial[:rows, :] - outer_rows(coupling[0, :, :width], first_value)
    corners[-rows:, :] = partial[-rows:, :] + outer_rows(
        coupling[subs - 1, :, width:], last_value
    )


def operators_kernel(coupling, live_edge, live_own, panel, taken, ends):
    subs, rows = coupling.shape[0], coupling.shape[1]
    width = coupling.shape[2] // 2
    live = Joined(live_edge, live_own)
    left = [coupling[sub, :, :width] * (0.25 * live[sub]) for sub in range(subs)]
    right = [coupling[sub, :, width:] * (0.25 * live[sub + 1]) for sub in range(subs)]
    none = jnp.zeros((rows, width), jnp.float32)
    inner, ahead, behind = [], [], []
    for sub in range(subs):
        above = left[sub + 1] if sub + 1 < subs else none
        below = right[sub - 1] if sub > 0 else none
        factors = jnp.concatenate(
            [
                jnp.concatenate([left[sub], right[sub]], axis=1),
                jnp.concatenate([none, above], axis=1),
                jnp.concatenate([below, none], axis=1),
            ],
            axis=0,
        )
        both = mul(jnp.concatenate(split(factors), axis=0), panel[sub])
        product = both[: 3 * rows] + both[3 * rows :]
        inner.append(product[:rows])
        ahead.append(product[rows : 2 * rows])
        behind.append(product[2 * rows :])
    total = subs * rows
    for sub in range(subs):
        blocks = [none] * (subs + 1)
        blocks[sub] = -inner[sub][:, :width]
        blocks[sub + 1] = inner[sub][:, width:]
        if sub > 0:
            blocks[sub - 1] = ahead[sub - 1][:, :width]
            blocks[sub] = blocks[sub] - ahead[sub - 1][:, width:]
        if sub + 1 < subs:
            blocks[sub + 1] = blocks[sub + 1] + behind[sub + 1][:, :width]
            blocks[sub + 2] = -behind[sub + 1][:, width:]
        if sub == 0:
            ends[0] = blocks[0]
            blocks[0] = none
        if sub == subs - 1:
            ends[1] = blocks[subs]
            blocks[subs] = none
        high, low = split(jnp.concatenate(blocks, axis=1))
        taken[sub * rows : (sub + 1) * rows, :] = high
        taken[total + sub * rows : total + (sub + 1) * rows, :] = low


def early_corner_kernel(taken, ends, outside, edge, own, corners):
    subs, rows = own.shape[0], ends.shape[1]
    total = subs * rows
    edges = Joined(edge, own)
    parts = [split(edges[place]) for place in range(subs + 1)]
    high = jnp.concatenate([part[0] for part in parts], axis=1)
    low = jnp.concatenate([part[1] for part in parts], axis=1)
    both = mul_rows(taken[...], high)
    values = both[:total] + both[total:] + mul_rows(taken[:total], low)
    corners[...] = values
    for end, place in ((0, 0), (1, subs)):
        operator = jnp.concatenate(split(ends[end]), axis=0)
        row = end * (total - rows)
        corners[row : row + rows, :] = (
            values[row : row + rows]
            + outer_rows(operator, edges[place])
            + outside[end * rows : (end + 1) * rows, :]
        )


def coarse_lift(everyone, block, lift):
    subs = lift.shape[0]
    rows = block.shape[0] // 2
    high, low = split(everyone[...])
    both = mul(block[...], high)
    back = both[:rows] + both[rows:] + mul(block[:rows], low)
    corners = rows // subs

    def lifted(sub):
        own = back[sub * corners : (sub + 1) * corners]
        own_high = own.astype(jnp.bfloat16).astype(jnp.float32)
        terms = [own_high, own - own_high, own_high]
        spare = jnp.zeros((lift.shape[1] - 3 * corners, own.shape[1]), jnp.float32)
        return mul(jnp.concatenate(terms + [spare], axis=0).T.astype(jnp.bfloat16), lift[sub])

    return lifted


def on_subdomain(values, left, right):
    width = left.shape[1]
    return values[:, width:] * right - values[:, :width] * left


def send_dual(even, inner, faces, for_next, for_prev, near_out, far_out, residual=None,
              given=None):
    to_next, to_prev = [faces[0]], [faces[1]]
    count = inner.shape[0]
    if given is not None:
        to_next += [given[0], outer_rows(for_next, residual[count - 1])]
        to_prev += [given[1], outer_rows(for_prev, residual[0])]
    to_next.append(outer_rows(for_next, inner[count - 1]))
    to_prev.append(outer_rows(for_prev, inner[0]))
    send(even, to_next, to_prev, near_out, far_out)


def inner_jump(result, live_own, inner):
    width = inner.shape[2]
    for place in range(inner.shape[0]):
        inner[place] = live_own[place] * (result[place][:, width:] - result[place + 1][:, :width])


def first_dual_kernel(before, inner_z, edge, last_z, residual, panel, everyone, block, lift,
                      near, far, live_edge, live_own, preconditioner,
                      inner, near_out, far_out, result, for_next, for_prev):
    even = even_place()
    subs, (loads, width) = panel.shape[0], edge.shape
    rows = for_next.shape[0] // 2
    sides = received(even, near, far, loads, rows)
    after = sides[rows:] * (0.25 * live_own[subs - 1])
    behind = sides[:rows] * (0.25 * live_edge[...])
    both = mul(jnp.concatenate(split(after), axis=0), preconditioner[subs - 1, width:])
    after = both[:rows] + both[rows:]
    both = mul(jnp.concatenate(split(behind), axis=0), preconditioner[0, :width])
    behind = both[:rows] + both[rows:]
    for_next[...] = jnp.concatenate(split(after[:, :width]), axis=0)
    for_prev[...] = jnp.concatenate(split(-behind[:, width:]), axis=0)
    given = [-after[:, width:], behind[:, :width]]

    lifted = coarse_lift(everyone, block, lift)
    for sub in range(subs):
        value = before[sub] + lifted(sub)
        if sub == 0:
            high, low = split(edge[...])
            value = value - (mul(high, panel[0, :width]) + mul(low, panel[0, :width]))
        if sub == subs - 1:
            high, low = split(last_z[...])
            value = value + (mul(high, panel[sub, width:]) + mul(low, panel[sub, width:]))
        result[sub] = value
    inner_jump(result, live_own, inner)
    faces = [result[subs - 1][:, width:], result[0][:, :width]]
    send_dual(even, inner, faces, for_next, for_prev, near_out, far_out, residual, given)


def sums_kernel(result, inner_z, edge, last_z, residual, sums):
    subs = residual.shape[0]
    edges = [edge[...]] + [inner_z[place] for place in range(subs - 1)] + [last_z[...]]
    product = curvature = 0.0
    for sub in range(subs):
        product = product + residual[sub] * edges[sub + 1]
        curvature = curvature + on_subdomain(result[sub], edges[sub], edges[sub + 1])
    sums[...] = jnp.concatenate([row_sums(product), row_sums(curvature)], axis=0)


def inner_edges_kernel(edge, own, panel, live_own, inner):
    subs, width = panel.shape[0], edge.shape[1]
    edges = Joined(edge, own)
    parts = [split(edges[place]) for place in range(subs + 1)]

    def half(sub, columns):
        high = jnp.concatenate([-parts[sub][0], parts[sub + 1][0]], axis=1)
        low = jnp.concatenate([-parts[sub][1], parts[sub + 1][1]], axis=1)
        return mul(high, panel[sub, :, columns]) + mul(low, panel[sub, :, columns])

    for place in range(subs - 1):
        right = half(place, slice(width, 2 * width))
        left = half(place + 1, slice(0, width))
        inner[place] = (0.25 * live_own[place]) * (right - left)


def inner_dual_kernel(inner, residual, panel, everyone, block, lift, result, partial):
    subs, width = panel.shape[0], inner.shape[2]
    lifted = coarse_lift(everyone, block, lift)
    parts = [split(inner[place]) for place in range(subs - 1)]
    high, low = parts[0]
    result[0] = mul(high, panel[0, width:]) + mul(low, panel[0, width:]) + lifted(0)
    product = residual[0] * inner[0]
    curvature = jnp.zeros_like(product)
    for sub in range(1, subs - 1):
        high = jnp.concatenate([-parts[sub - 1][0], parts[sub][0]], axis=1)
        low = jnp.concatenate([-parts[sub - 1][1], parts[sub][1]], axis=1)
        result[sub] = mul(high, panel[sub]) + mul(low, panel[sub]) + lifted(sub)
        product = product + residual[sub] * inner[sub]
        curvature = curvature + on_subdomain(result[sub], inner[sub - 1], inner[sub])
    high, low = parts[subs - 2]
    result[subs - 1] = lifted(subs - 1) - (
        mul(high, panel[subs - 1, :width]) + mul(low, panel[subs - 1, :width])
    )
    partial[0] = product
    partial[1] = curvature


def cut_edges(even, loads, near, far, near_sent, far_sent, live_first, live_last):
    near, far, near_sent, far_sent = near[:loads], far[:loads], near_sent[:loads], far_sent[:loads]
    first = live_first * jnp.where(even, far - far_sent, near - near_sent)
    last = live_last * jnp.where(even, near_sent - near, far_sent - far)
    return first, last


def outer_dual_kernel(closing, *refs):
    before, inner_z, partial, near, far, near_sent, far_sent, live_edge, live_own = refs[:9]
    residual, panel = refs[9:11]
    even, subs, width = even_place(), panel.shape[0], near_sent.shape[1]
    edge, last = cut_edges(even, residual.shape[1], near, far, near_sent, far_sent,
                           0.25 * live_edge[...], 0.25 * live_own[subs - 1])
    if closing:
        last_z, inner, to_next, to_prev, sums = refs[11:]
    else:
        for_next, for_prev, last_z, inner, near_out, far_out, sums = refs[11:]
    last_z[...] = last
    high, low = split(edge)
    result_first = before[0] - (mul(high, panel[0, :width]) + mul(low, panel[0, :width]))
    high, low = split(last)
    result_last = before[subs - 1] + (
        mul(high, panel[subs - 1, width:]) + mul(low, panel[subs - 1, width:])
    )
    result = [result_first] + [before[sub] for sub in range(1, subs - 1)] + [result_last]
    inner_jump(result, live_own, inner)
    faces = [result_last[:, width:], result_first[:, :width]]
    if closing:
        to_next[...], to_prev[...] = faces
    else:
        send_dual(even, inner, faces, for_next, for_prev, near_out, far_out)
    product = partial[0] + residual[subs - 1] * last
    curvature = partial[1] + on_subdomain(result_first, edge, inner_z[0])
    curvature = curvature + on_subdomain(result_last, inner_z[subs - 2], last)
    sums[...] = jnp.concatenate([row_sums(product), row_sums(curvature)], axis=0)


def received(even, near, far, start, rows):
    part = slice(start, start + rows)
    return jnp.concatenate(
        [jnp.where(even, far[part], near[part]), jnp.where(even, near[part], far[part])], axis=0
    )


def send_outer(parts, panel, near_out, far_out):
    subs, width = panel.shape[0], near_out.shape[1]

    def half(sub, columns):
        high = jnp.concatenate([-parts[sub][0], parts[sub + 1][0]], axis=1)
        low = jnp.concatenate([-parts[sub][1], parts[sub + 1][1]], axis=1)
        return mul(high, panel[sub, :, columns]) + mul(low, panel[sub, :, columns])

    to_next = half(subs - 1, slice(width, 2 * width))
    send(even_place(), [to_next], [half(0, slice(0, width))], near_out, far_out)


def image_edges(even, inner, near, far, near_sent, far_sent, live_edge, live_own):
    subs = live_own.shape[0]
    edge, last = cut_edges(even, inner.shape[1], near, far, near_sent, far_sent, live_edge[...],
                           live_own[subs - 1])
    return [edge] + [inner[place] for place in range(subs - 1)] + [last]


def first_update_kernel(inner, near, far, near_sent, far_sent, live_edge, live_own, sums,
                        residual_edge, residual_own, panel, ends,
                        image_own, image_edge, new_edge, new_own,
                        near_out, far_out, scalars, full_ends, outside_image, outside):
    even = even_place()
    loads, width = residual_edge.shape
    subs, rows = panel.shape[0], ends.shape[1]
    residual, image = Joined(residual_edge, residual_own), Joined(image_edge, image_own)
    residual_new = Joined(new_edge, new_own)
    rz_now, alpha, _ = step_scalars(0, sums, None)
    scalars[...] = jnp.concatenate([rz_now, alpha], axis=0)
    operators = received(even, near, far, loads, rows)
    full_ends[0] = ends[0] + operators[:rows]
    full_ends[1] = ends[1] + operators[rows:]
    values = received(even, near, far, loads + 2 * rows, rows)
    outside_image[...] = values
    outside[...] = received(even, near, far, loads + rows, rows) - alpha * values
    alpha_column = column(alpha, width)
    parts = []
    edges = image_edges(even, inner, near, far, near_sent, far_sent, live_edge, live_own)
    for place, value in enumerate(edges):
        image[place] = value
        residual_new[place] = residual[place] - alpha_column * value
        parts.append(split(residual_new[place]))
    send_outer(parts, panel, near_out, far_out)


def update_kernel(inner, near, far, near_sent, far_sent, live_edge, live_own, sums, before,
                  old_edge, old_own, residual_edge, residual_own, panel,
                  outside_image_old, outside_old,
                  image_own, new_edge, new_own, near_out, far_out, scalars, outside):
    even = even_place()
    loads, width = residual_edge.shape
    rows = outside.shape[0] // 2
    image_old, residual = Joined(old_edge, old_own), Joined(residual_edge, residual_own)
    residual_new = Joined(new_edge, new_own)
    rz_now, alpha, beta = step_scalars(1, sums, before)
    scalars[...] = jnp.concatenate([rz_now, alpha], axis=0)
    values = received(even, near, far, loads, rows) + beta * outside_image_old[...]
    outside[...] = outside_old[...] - alpha * values
    alpha_column, beta_column = column(alpha, width), column(beta, width)
    parts = []
    edges = image_edges(even, inner, near, far, near_sent, far_sent, live_edge, live_own)
    for place, value in enumerate(edges):
        value = value + beta_column * image_old[place]
        if place > 0:
            image_own[place - 1] = value
        residual_new[place] = residual[place] - alpha_column * value
        parts.append(split(residual_new[place]))
    send_outer(parts, panel, near_out, far_out)


def last_kernel(inner, to_next, following, live, sums, before, older, image_old,
                residual, first_inner, first_last, second_inner, second_last, third_inner, third_last,
                multipliers, residual_new):
    subs, width = residual.shape[0], following.shape[1]
    rz_now, alpha, beta = step_scalars(2, sums, before)
    beta_before = before[0:1] / older[0:1]
    on_second = before[1:2] + alpha * beta
    on_first = older[1:2] + on_second * beta_before
    alpha_column, beta_column = column(alpha, width), column(beta, width)
    second_column, first_column = column(on_second, width), column(on_first, width)
    for sub in range(subs):
        if sub == subs - 1:
            image = live[sub] * (to_next[...] - following[...])
            first_z, second_z, third_z = first_last[...], second_last[...], third_last[...]
        else:
            image = inner[sub]
            first_z, second_z, third_z = first_inner[sub], second_inner[sub], third_inner[sub]
        image = image + beta_column * image_old[sub]
        residual_new[sub] = residual[sub] - alpha_column * image
        multipliers[sub] = (
            first_column * first_z + second_column * second_z + alpha_column * third_z
        )


def neighbour_pairs(size, first):
    pairs = [(i, i + 1) for i in range(first, size - 1, 2)]
    return [route for a, b in pairs for route in ((a, b), (b, a))]


def swap(near, far):
    size = lax.axis_size("sub")
    return (
        lax.ppermute(near, "sub", neighbour_pairs(size, 0)),
        lax.ppermute(far, "sub", neighbour_pairs(size, 1)),
    )


def from_all(rows):
    size = lax.axis_size("sub") * lax.axis_size("grp")
    copies = jnp.broadcast_to(rows[None], (size,) + rows.shape)
    return lax.all_to_all(copies, ("sub", "grp"), 0, 0)


def from_group(values):
    group = lax.axis_size("grp")
    received = [values]
    for distance in range(1, group):
        routes = [(i, i ^ distance) for i in range(group)]
        received.append(lax.ppermute(values, "grp", routes))
    return received


def swap_blocks(picked):
    group = lax.axis_size("grp")
    received = [picked[0]]
    for distance in range(1, group):
        routes = [(i, i ^ distance) for i in range(group)]
        received.append(lax.ppermute(picked[distance], "grp", routes))
    return received


def make_tail(counts, rhs):
    loads, width = rhs.shape[2:]
    return pl.pallas_call(
        tail_kernel,
        out_shape=jax.ShapeDtypeStruct((loads + 8, width), jnp.float32),
        in_specs=[
            pl.BlockSpec(memory_space=pltpu.HBM),
            pl.BlockSpec(memory_space=pltpu.HBM),
        ],
        out_specs=pl.BlockSpec(memory_space=pltpu.VMEM),
        scratch_shapes=[
            pltpu.VMEM(counts.shape, counts.dtype),
            pltpu.VMEM((loads, width), jnp.float32),
            pltpu.SemaphoreType.DMA,
            pltpu.SemaphoreType.DMA,
        ],
        compiler_params=pltpu.CompilerParams(vmem_limit_bytes=TAIL_LIMIT),
    )(counts, rhs)


def local(rhs, counts, solve_panel, dirichlet_panel, coupling, corner_map, coarse_inverse):
    subs, loads, width = rhs.shape[1:]
    corners = coupling.shape[2]
    solve, dirichlet = solve_panel[0], dirichlet_panel[0]
    size = lax.axis_size("sub")

    face_shape, own_shape = (loads, width), (subs, loads, width)
    scalars_shape, outside_shape, side_shape = (2, loads), (2 * corners, loads), (corners, width)
    long_shape, longer_shape = (loads + corners, width), (loads + 3 * corners, width)
    edges_shapes = [face_shape, own_shape]

    tail = make_tail(counts, rhs)
    tail, counts, corner_map = lax.optimization_barrier((tail, counts, corner_map))
    head = lax.ppermute(tail, "sub", [(i, i + 1) for i in range(size - 1)])
    maps = from_group(corner_map[0])
    live_own, residual_own, to_next, partial = call(
        early_kernel,
        [(subs, 1, width), own_shape, face_shape, face_shape],
        counts, rhs[0], dirichlet,
    )
    group, own = len(maps), subs * corners
    pair = [(corners, width)] * 2
    *picked, stacked, lift = call(
        setup_kernel,
        [(own, group * own)] * group
        + [(subs, 2 * corners, 2 * width), (subs, 3 * corners + -3 * corners % 128, 2 * width)],
        *maps, coarse_inverse[0], coupling[0],
        kinds=[jnp.float32] * group + [jnp.bfloat16] * 2,
        scratch=[pltpu.VMEM((group, 1, own), jnp.int32)],
    )
    head, stacked = lax.optimization_barrier((head, stacked))
    live_edge, residual_edge, near, far = call(
        head_kernel,
        [(1, width), face_shape, long_shape, long_shape],
        head, to_next, partial, dirichlet, coupling[0],
    )
    live, residual = (live_edge, live_own), (residual_edge, residual_own)
    sent = near, far
    near, far = swap(near, far)
    blocks = swap_blocks(picked)
    inner_shape, result_shape = (subs - 1, loads, width), (subs, loads, 2 * width)
    (first_inner,) = call(inner_edges_kernel, [inner_shape], *residual, dirichlet, live[1])
    result, partial = call(
        start_kernel, [result_shape, (own, loads)], first_inner, solve, stacked
    )
    taken, ends = call(
        operators_kernel,
        [(2 * own, (subs + 1) * width), (2,) + side_shape],
        coupling[0], *live, dirichlet,
        kinds=[jnp.bfloat16, jnp.float32],
    )
    partial, taken, ends = lax.optimization_barrier((partial, taken, ends))

    edge, first_last, values = call(
        corner_kernel,
        [face_shape, face_shape, (own, loads)],
        near, far, *sent, *live, stacked, partial,
    )
    everyone = lax.all_gather(values, "grp", tiled=True)
    everyone, blocks = lax.optimization_barrier((everyone, blocks))
    block = jnp.concatenate(split_outside(sum(blocks[1:], blocks[0])), axis=0)
    inner, near, far, result, for_next, for_prev = call(
        first_dual_kernel,
        [inner_shape, longer_shape, longer_shape, result_shape]
        + [(2 * corners, width), (2 * corners, width)],
        result, first_inner, edge, first_last, residual[1], solve, everyone, block, lift,
        near, far, *live, dirichlet,
        kinds=[jnp.float32] * 4 + [jnp.bfloat16] * 2,
    )
    (sums,) = call(
        sums_kernel, [scalars_shape], result, first_inner, edge, first_last, residual[1]
    )
    sums = from_all(sums)
    sent = near, far
    near, far = swap(near, far)
    image_own, image_edge, *residual, near, far, scalars_first, ends, outside_image, outside = call(
        first_update_kernel,
        [own_shape, face_shape] + edges_shapes
        + [face_shape, face_shape, scalars_shape, (2,) + side_shape, outside_shape, outside_shape],
        inner, near, far, *sent, *live, sums, *residual, dirichlet, ends,
    )

    def inside(residual, outside):
        (values,) = call(early_corner_kernel, [(own, loads)], taken, ends, outside, *residual)
        everyone = lax.all_gather(values, "grp", tiled=True)
        (inner,) = call(inner_edges_kernel, [inner_shape], *residual, dirichlet, live[1])
        result, partial = call(
            inner_dual_kernel,
            [result_shape, (2,) + face_shape],
            inner, residual[1], solve, everyone, block, lift,
        )
        return result, inner, partial

    sent = near, far
    near, far = swap(near, far)
    result, second_inner, partial = inside(residual, outside)
    second_last, inner, near, far, sums = call(
        functools.partial(outer_dual_kernel, False),
        [face_shape, inner_shape, long_shape, long_shape, scalars_shape],
        result, second_inner, partial, near, far, *sent, *live, residual[1], solve,
        for_next, for_prev,
    )
    sums = from_all(sums)
    sent = near, far
    near, far = swap(near, far)
    image_own, *residual, near, far, scalars_second, outside = call(
        update_kernel,
        [own_shape] + edges_shapes + [face_shape, face_shape, scalars_shape, outside_shape],
        inner, near, far, *sent, *live, sums, scalars_first, image_edge, image_own, *residual,
        dirichlet, outside_image, outside,
    )

    sent = near, far
    near, far = swap(near, far)
    result, third_inner, partial = inside(residual, outside)
    third_last, inner, to_next, to_prev, sums = call(
        functools.partial(outer_dual_kernel, True),
        [face_shape, inner_shape, face_shape, face_shape, scalars_shape],
        result, third_inner, partial, near, far, *sent, *live, residual[1], solve,
    )
    sums = from_all(sums)
    following = lax.ppermute(to_prev, "sub", [(i + 1, i) for i in range(size - 1)])
    multipliers, residual = call(
        last_kernel,
        [own_shape] * 2,
        inner, to_next, following, live[1], sums, scalars_second, scalars_first,
        image_own, residual[1], first_inner, first_last, second_inner, second_last, third_inner, third_last,
    )
    return (multipliers[None], residual[None])


def solution(mesh):
    return jax.shard_map(
        local,
        mesh=mesh,
        in_specs=(
            P("grp", "sub", None, None),
            P("grp", "sub"),
            P("grp", "sub", None, None),
            P("grp", "sub", None, None),
            P("grp", "sub", None, None),
            P("grp", "sub", None),
            P("sub", "grp", None),
        ),
        out_specs=(P("grp", "sub", None, None), P("grp", "sub", None, None)),
        check_vma=False,
    )
```

```python
import functools

import jax
import jax.numpy as jnp
from jax import lax
from jax.experimental import pallas as pl
from jax.experimental.pallas import tpu as pltpu
from jax.sharding import PartitionSpec as P

VMEM_LIMIT = 8 * 1024 * 1024
TAIL_LIMIT = 62 * 1024 * 1024


def split(values):
    high = values.astype(jnp.bfloat16)
    return high, (values - high.astype(jnp.float32)).astype(jnp.bfloat16)


def split_outside(values):
    high = lax.reduce_precision(values, exponent_bits=8, mantissa_bits=7)
    return high.astype(jnp.bfloat16), (values - high).astype(jnp.bfloat16)


def mul(first, second):
    return jnp.dot(first, second, preferred_element_type=jnp.float32)


def mul_rows(first, second):
    dims = (((1,), (1,)), ((), ()))
    return lax.dot_general(first, second, dims, preferred_element_type=jnp.float32)


def call(kernel, out_shapes, *operands, kinds=None, scratch=()):
    kinds = kinds or [jnp.float32] * len(out_shapes)
    return pl.pallas_call(
        kernel,
        out_shape=[jax.ShapeDtypeStruct(*shape) for shape in zip(out_shapes, kinds)],
        in_specs=[pl.BlockSpec(memory_space=pltpu.VMEM)] * len(operands),
        out_specs=[pl.BlockSpec(memory_space=pltpu.VMEM)] * len(out_shapes),
        scratch_shapes=list(scratch),
        compiler_params=pltpu.CompilerParams(vmem_limit_bytes=VMEM_LIMIT),
    )(*operands)


class Joined:
    def __init__(self, first, rest):
        self.first, self.rest = first, rest

    def __getitem__(self, place):
        return self.first[...] if place == 0 else self.rest[place - 1]

    def __setitem__(self, place, value):
        if place == 0:
            self.first[...] = value
        else:
            self.rest[place - 1] = value


def outer_rows(operator, edge):
    rows = operator.shape[0] // 2
    high, low = split(edge)
    both = mul_rows(operator[...], high)
    return both[:rows] + both[rows:] + mul_rows(operator[:rows], low)


def send(even, to_next, to_prev, near_out, far_out):
    row = 0
    for ahead, behind in zip(to_next, to_prev):
        rows = slice(row, row + ahead.shape[0])
        near_out[rows, :] = jnp.where(even, ahead, behind)
        far_out[rows, :] = jnp.where(even, behind, ahead)
        row += ahead.shape[0]


def column(row, width):
    lanes = jnp.broadcast_to(row, (128, row.shape[1])).T
    return jnp.concatenate([lanes] * (width // 128), axis=1)


def row_sums(values):
    half = values.shape[1] // 2
    return jnp.sum((values[:, :half] + values[:, half:]).T, axis=0, keepdims=True)


def step_scalars(step, sums, before):
    totals = jnp.sum(sums[...], axis=0)
    rz_now, curvature = totals[:1], totals[1:2]
    if step == 0:
        return rz_now, rz_now / curvature, None
    beta = rz_now / before[0:1]
    return rz_now, rz_now / (curvature - beta * rz_now / before[1:2]), beta


def even_place():
    return lax.rem(lax.axis_index("sub"), 2) == 0


def live_rows(counts, sub, rows, width):
    last = lax.axis_index("sub") == lax.axis_size("sub") - 1
    count = jnp.broadcast_to(counts[:, sub : sub + 1], (rows, width))
    if sub == counts.shape[1] - 1:
        count = jnp.where(last, 0, count)
    return (lax.broadcasted_iota(jnp.int32, (rows, width), 1) < count).astype(jnp.float32)


def tail_kernel(counts_ref, rhs, tail, counts, face, counts_done, face_done):
    loads, width = rhs.shape[2:]
    counts_copy = pltpu.make_async_copy(counts_ref, counts, counts_done)
    face_copy = pltpu.make_async_copy(rhs.at[0, rhs.shape[1] - 1], face, face_done)
    counts_copy.start()
    face_copy.start()
    counts_copy.wait()
    mask = live_rows(counts, counts.shape[1] - 1, 8, width)
    tail[loads:] = mask
    face_copy.wait()
    tail[:loads] = mask[:1] * face[...]


def early_kernel(counts, rhs, panel, live, own, to_next, partial):
    subs, loads, width = own.shape
    parts = []
    for sub in range(subs):
        mask = live_rows(counts, sub, 1, width)
        live[sub] = mask
        own[sub] = mask * rhs[sub]
        parts.append(split(own[sub]))
    high = jnp.concatenate([-parts[subs - 2][0], parts[subs - 1][0]], axis=1)
    low = jnp.concatenate([-parts[subs - 2][1], parts[subs - 1][1]], axis=1)
    to_next[...] = mul(high, panel[subs - 1, :, width:]) + mul(low, panel[subs - 1, :, width:])
    high, low = parts[0]
    partial[...] = mul(high, panel[0, width:, :width]) + mul(low, panel[0, width:, :width])


def head_kernel(head, to_next, partial, panel, coupling, live, edge, near_out, far_out):
    loads, width = edge.shape
    live[...] = head[loads : loads + 1]
    edge[...] = head[:loads]
    high, low = split(head[:loads])
    to_prev = partial[...] - (
        mul(high, panel[0, :width, :width]) + mul(low, panel[0, :width, :width])
    )
    ahead = [to_next[...], coupling[coupling.shape[0] - 1, :, width:]]
    send(even_place(), ahead, [to_prev, coupling[0, :, :width]], near_out, far_out)


def setup_kernel(*refs):
    group = (len(refs) - 5) // 2
    maps, (coarse, coupling) = refs[:group], refs[group : group + 2]
    picked, (stacked, lift, everyone) = refs[group + 2 : -3], refs[-3:]
    subs, corners = maps[0].shape
    rows, size = coarse.shape
    own = subs * corners
    grp = lax.axis_index("grp")
    for sub in range(subs):
        high, low = split(coupling[sub])
        spare = jnp.zeros((lift.shape[1] - 3 * corners, high.shape[1]), jnp.bfloat16)
        stacked[sub] = jnp.concatenate([high, low], axis=0)
        lift[sub] = jnp.concatenate([high, high, low, spare], axis=0)
    for distance in range(group):
        unknowns = [maps[distance][sub : sub + 1, :] for sub in range(subs)]
        everyone[distance] = jnp.concatenate(unknowns, axis=1)
    high, low = split(coarse[...])
    together = max(1, 512 // own)
    columns = []
    for start in range(0, group, together):
        members = range(start, min(start + together, group))
        wanted = jnp.concatenate([everyone[grp ^ member] for member in members], axis=1)
        unknowns = lax.broadcasted_iota(jnp.int32, (size, wanted.shape[1]), 0)
        chosen = (unknowns == wanted).astype(jnp.bfloat16)
        columns.append(mul(high, chosen) + mul(low, chosen))
    high, low = split(jnp.concatenate(columns, axis=1))
    dims = (((0,), (0,)), ((), ()))
    for start in range(0, group, together):
        distances = range(start, min(start + together, group))
        wanted = jnp.concatenate([everyone[distance] for distance in distances], axis=1)
        owned = lax.broadcasted_iota(jnp.int32, (rows, wanted.shape[1]), 0) + grp * rows
        chosen = (owned == wanted).astype(jnp.bfloat16)
        values = lax.dot_general(
            chosen, high, dims, preferred_element_type=jnp.float32
        ) + lax.dot_general(chosen, low, dims, preferred_element_type=jnp.float32)
        for place, distance in enumerate(distances):
            picked[distance][...] = values[place * own : (place + 1) * own]


def start_kernel(inner, panel, coupling, result, corners):
    subs, rows = coupling.shape[0], coupling.shape[1] // 2
    width = inner.shape[2]
    parts = [split(inner[place]) for place in range(subs - 1)]
    high, low = parts[0]
    result[0] = mul(high, panel[0, width:]) + mul(low, panel[0, width:])
    for sub in range(1, subs - 1):
        high = jnp.concatenate([-parts[sub - 1][0], parts[sub][0]], axis=1)
        low = jnp.concatenate([-parts[sub - 1][1], parts[sub][1]], axis=1)
        result[sub] = mul(high, panel[sub]) + mul(low, panel[sub])
    high, low = parts[subs - 2]
    result[subs - 1] = -(mul(high, panel[subs - 1, :width]) + mul(low, panel[subs - 1, :width]))
    for sub in range(subs):
        values = jnp.zeros((rows, inner.shape[1]), jnp.float32)
        if sub > 0:
            values = values - outer_rows(coupling[sub, :, :width], inner[sub - 1])
        if sub + 1 < subs:
            values = values + outer_rows(coupling[sub, :, width:], inner[sub])
        corners[sub * rows : (sub + 1) * rows, :] = values


def corner_kernel(near, far, near_sent, far_sent, live_edge, live_own, coupling, partial,
                  edge, last, corners):
    subs, rows = coupling.shape[0], coupling.shape[1] // 2
    loads, width = edge.shape
    first_value, last_value = cut_edges(even_place(), loads, near, far, near_sent, far_sent,
                                        0.25 * live_edge[...], 0.25 * live_own[subs - 1])
    edge[...] = first_value
    last[...] = last_value
    corners[...] = partial[...]
    corners[:rows, :] = partial[:rows, :] - outer_rows(coupling[0, :, :width], first_value)
    corners[-rows:, :] = partial[-rows:, :] + outer_rows(
        coupling[subs - 1, :, width:], last_value
    )


def operators_kernel(coupling, live_edge, live_own, panel, taken, ends):
    subs, rows = coupling.shape[0], coupling.shape[1]
    width = coupling.shape[2] // 2
    live = Joined(live_edge, live_own)
    left = [coupling[sub, :, :width] * (0.25 * live[sub]) for sub in range(subs)]
    right = [coupling[sub, :, width:] * (0.25 * live[sub + 1]) for sub in range(subs)]
    none = jnp.zeros((rows, width), jnp.float32)
    inner, ahead, behind = [], [], []
    for sub in range(subs):
        above = left[sub + 1] if sub + 1 < subs else none
        below = right[sub - 1] if sub > 0 else none
        factors = jnp.concatenate(
            [
                jnp.concatenate([left[sub], right[sub]], axis=1),
                jnp.concatenate([none, above], axis=1),
                jnp.concatenate([below, none], axis=1),
            ],
            axis=0,
        )
        both = mul(jnp.concatenate(split(factors), axis=0), panel[sub])
        product = both[: 3 * rows] + both[3 * rows :]
        inner.append(product[:rows])
        ahead.append(product[rows : 2 * rows])
        behind.append(product[2 * rows :])
    total = subs * rows
    for sub in range(subs):
        blocks = [none] * (subs + 1)
        blocks[sub] = -inner[sub][:, :width]
        blocks[sub + 1] = inner[sub][:, width:]
        if sub > 0:
            blocks[sub - 1] = ahead[sub - 1][:, :width]
            blocks[sub] = blocks[sub] - ahead[sub - 1][:, width:]
        if sub + 1 < subs:
            blocks[sub + 1] = blocks[sub + 1] + behind[sub + 1][:, :width]
            blocks[sub + 2] = -behind[sub + 1][:, width:]
        if sub == 0:
            ends[0] = blocks[0]
            blocks[0] = none
        if sub == subs - 1:
            ends[1] = blocks[subs]
            blocks[subs] = none
        high, low = split(jnp.concatenate(blocks, axis=1))
        taken[sub * rows : (sub + 1) * rows, :] = high
        taken[total + sub * rows : total + (sub + 1) * rows, :] = low


def early_corner_kernel(taken, ends, outside, edge, own, corners):
    subs, rows = own.shape[0], ends.shape[1]
    total = subs * rows
    edges = Joined(edge, own)
    parts = [split(edges[place]) for place in range(subs + 1)]
    high = jnp.concatenate([part[0] for part in parts], axis=1)
    low = jnp.concatenate([part[1] for part in parts], axis=1)
    both = mul_rows(taken[...], high)
    values = both[:total] + both[total:] + mul_rows(taken[:total], low)
    corners[...] = values
    for end, place in ((0, 0), (1, subs)):
        operator = jnp.concatenate(split(ends[end]), axis=0)
        row = end * (total - rows)
        corners[row : row + rows, :] = (
            values[row : row + rows]
            + outer_rows(operator, edges[place])
            + outside[end * rows : (end + 1) * rows, :]
        )


def coarse_lift(everyone, block, lift):
    subs = lift.shape[0]
    rows = block.shape[0] // 2
    high, low = split(everyone[...])
    both = mul(block[...], high)
    back = both[:rows] + both[rows:] + mul(block[:rows], low)
    corners = rows // subs

    def lifted(sub):
        own = back[sub * corners : (sub + 1) * corners]
        own_high = own.astype(jnp.bfloat16).astype(jnp.float32)
        terms = [own_high, own - own_high, own_high]
        spare = jnp.zeros((lift.shape[1] - 3 * corners, own.shape[1]), jnp.float32)
        return mul(jnp.concatenate(terms + [spare], axis=0).T.astype(jnp.bfloat16), lift[sub])

    return lifted


def on_subdomain(values, left, right):
    width = left.shape[1]
    return values[:, width:] * right - values[:, :width] * left


def send_dual(even, inner, faces, for_next, for_prev, near_out, far_out, given=None):
    to_next, to_prev = [faces[0]], [faces[1]]
    count = inner.shape[0]
    if given is not None:
        to_next.append(given[0])
        to_prev.append(given[1])
    to_next.append(outer_rows(for_next, inner[count - 1]))
    to_prev.append(outer_rows(for_prev, inner[0]))
    send(even, to_next, to_prev, near_out, far_out)


def inner_jump(result, live_own, inner):
    width = inner.shape[2]
    for place in range(inner.shape[0]):
        inner[place] = live_own[place] * (result[place][:, width:] - result[place + 1][:, :width])


def first_dual_kernel(before, inner_z, edge, last_z, residual, panel, everyone, block, lift,
                      near, far, live_edge, live_own, preconditioner,
                      inner, near_out, far_out, result, for_next, for_prev):
    even = even_place()
    subs, (loads, width) = panel.shape[0], edge.shape
    rows = for_next.shape[0] // 2
    sides = received(even, near, far, loads, rows)
    after = sides[rows:] * (0.25 * live_own[subs - 1])
    behind = sides[:rows] * (0.25 * live_edge[...])
    both = mul(jnp.concatenate(split(after), axis=0), preconditioner[subs - 1, width:])
    after = both[:rows] + both[rows:]
    both = mul(jnp.concatenate(split(behind), axis=0), preconditioner[0, :width])
    behind = both[:rows] + both[rows:]
    for_next[...] = jnp.concatenate(split(after[:, :width]), axis=0)
    for_prev[...] = jnp.concatenate(split(-behind[:, width:]), axis=0)
    given = [-after[:, width:], behind[:, :width]]

    lifted = coarse_lift(everyone, block, lift)
    for sub in range(subs):
        value = before[sub] + lifted(sub)
        if sub == 0:
            high, low = split(edge[...])
            value = value - (mul(high, panel[0, :width]) + mul(low, panel[0, :width]))
        if sub == subs - 1:
            high, low = split(last_z[...])
            value = value + (mul(high, panel[sub, width:]) + mul(low, panel[sub, width:]))
        result[sub] = value
    inner_jump(result, live_own, inner)
    faces = [result[subs - 1][:, width:], result[0][:, :width]]
    send_dual(even, inner, faces, for_next, for_prev, near_out, far_out, given)


def sums_kernel(result, inner_z, edge, last_z, residual, sums):
    subs = residual.shape[0]
    edges = [edge[...]] + [inner_z[place] for place in range(subs - 1)] + [last_z[...]]
    product = curvature = 0.0
    for sub in range(subs):
        product = product + residual[sub] * edges[sub + 1]
        curvature = curvature + on_subdomain(result[sub], edges[sub], edges[sub + 1])
    sums[...] = jnp.concatenate([row_sums(product), row_sums(curvature)], axis=0)


def inner_edges_kernel(edge, own, panel, live_own, inner):
    subs, width = panel.shape[0], edge.shape[1]
    edges = Joined(edge, own)
    parts = [split(edges[place]) for place in range(subs + 1)]

    def half(sub, columns):
        high = jnp.concatenate([-parts[sub][0], parts[sub + 1][0]], axis=1)
        low = jnp.concatenate([-parts[sub][1], parts[sub + 1][1]], axis=1)
        return mul(high, panel[sub, :, columns]) + mul(low, panel[sub, :, columns])

    for place in range(subs - 1):
        right = half(place, slice(width, 2 * width))
        left = half(place + 1, slice(0, width))
        inner[place] = (0.25 * live_own[place]) * (right - left)


def inner_dual_kernel(inner, residual, panel, everyone, block, lift, result, partial):
    subs, width = panel.shape[0], inner.shape[2]
    lifted = coarse_lift(everyone, block, lift)
    parts = [split(inner[place]) for place in range(subs - 1)]
    high, low = parts[0]
    result[0] = mul(high, panel[0, width:]) + mul(low, panel[0, width:]) + lifted(0)
    product = residual[0] * inner[0]
    curvature = jnp.zeros_like(product)
    for sub in range(1, subs - 1):
        high = jnp.concatenate([-parts[sub - 1][0], parts[sub][0]], axis=1)
        low = jnp.concatenate([-parts[sub - 1][1], parts[sub][1]], axis=1)
        result[sub] = mul(high, panel[sub]) + mul(low, panel[sub]) + lifted(sub)
        product = product + residual[sub] * inner[sub]
        curvature = curvature + on_subdomain(result[sub], inner[sub - 1], inner[sub])
    high, low = parts[subs - 2]
    result[subs - 1] = lifted(subs - 1) - (
        mul(high, panel[subs - 1, :width]) + mul(low, panel[subs - 1, :width])
    )
    partial[0] = product
    partial[1] = curvature


def inside_kernel(edge, own, preconditioner, live_own, panel, everyone, block, lift,
                  inner, result, partial):
    inner_edges_kernel(edge, own, preconditioner, live_own, inner)
    inner_dual_kernel(inner, own, panel, everyone, block, lift, result, partial)


def cut_edges(even, loads, near, far, near_sent, far_sent, live_first, live_last):
    near, far, near_sent, far_sent = near[:loads], far[:loads], near_sent[:loads], far_sent[:loads]
    first = live_first * jnp.where(even, far - far_sent, near - near_sent)
    last = live_last * jnp.where(even, near_sent - near, far_sent - far)
    return first, last


def outer_dual_kernel(closing, *refs):
    before, inner_z, partial, near, far, near_sent, far_sent, live_edge, live_own = refs[:9]
    residual, panel = refs[9:11]
    even, subs, width = even_place(), panel.shape[0], near_sent.shape[1]
    edge, last = cut_edges(even, residual.shape[1], near, far, near_sent, far_sent,
                           0.25 * live_edge[...], 0.25 * live_own[subs - 1])
    if closing:
        last_z, inner, to_next, to_prev, sums = refs[11:]
    else:
        for_next, for_prev, last_z, inner, near_out, far_out, sums = refs[11:]
    last_z[...] = last
    high, low = split(edge)
    result_first = before[0] - (mul(high, panel[0, :width]) + mul(low, panel[0, :width]))
    high, low = split(last)
    result_last = before[subs - 1] + (
        mul(high, panel[subs - 1, width:]) + mul(low, panel[subs - 1, width:])
    )
    result = [result_first] + [before[sub] for sub in range(1, subs - 1)] + [result_last]
    inner_jump(result, live_own, inner)
    faces = [result_last[:, width:], result_first[:, :width]]
    if closing:
        to_next[...], to_prev[...] = faces
    else:
        send_dual(even, inner, faces, for_next, for_prev, near_out, far_out)
    product = partial[0] + residual[subs - 1] * last
    curvature = partial[1] + on_subdomain(result_first, edge, inner_z[0])
    curvature = curvature + on_subdomain(result_last, inner_z[subs - 2], last)
    sums[...] = jnp.concatenate([row_sums(product), row_sums(curvature)], axis=0)


def received(even, near, far, start, rows):
    part = slice(start, start + rows)
    return jnp.concatenate(
        [jnp.where(even, far[part], near[part]), jnp.where(even, near[part], far[part])], axis=0
    )


def send_outer(parts, panel, near_out, far_out):
    subs, width = panel.shape[0], near_out.shape[1]

    def half(sub, columns):
        high = jnp.concatenate([-parts[sub][0], parts[sub + 1][0]], axis=1)
        low = jnp.concatenate([-parts[sub][1], parts[sub + 1][1]], axis=1)
        return mul(high, panel[sub, :, columns]) + mul(low, panel[sub, :, columns])

    to_next = half(subs - 1, slice(width, 2 * width))
    send(even_place(), [to_next], [half(0, slice(0, width))], near_out, far_out)


def image_edges(even, inner, near, far, near_sent, far_sent, live_edge, live_own):
    subs = live_own.shape[0]
    edge, last = cut_edges(even, inner.shape[1], near, far, near_sent, far_sent, live_edge[...],
                           live_own[subs - 1])
    return [edge] + [inner[place] for place in range(subs - 1)] + [last]


def first_update_kernel(inner, near, far, near_sent, far_sent, live_edge, live_own, sums,
                        residual_edge, residual_own, panel, ends, start, own_start,
                        image_own, image_edge, new_edge, new_own,
                        near_out, far_out, scalars, full_ends, outside_image, outside):
    even = even_place()
    loads, width = residual_edge.shape
    subs, rows = panel.shape[0], ends.shape[1]
    residual, image = Joined(residual_edge, residual_own), Joined(image_edge, image_own)
    residual_new = Joined(new_edge, new_own)
    rz_now, alpha, _ = step_scalars(0, sums, None)
    scalars[...] = jnp.concatenate([rz_now, alpha], axis=0)
    operators = received(even, near, far, loads, rows)
    full_ends[0] = ends[0] + operators[:rows]
    full_ends[1] = ends[1] + operators[rows:]
    values = received(even, near, far, loads + rows, rows)
    outside_image[...] = values
    for end, place in ((0, 0), (1, subs)):
        part, row = slice(end * rows, (end + 1) * rows), end * (start.shape[0] - rows)
        operator = jnp.concatenate(split(operators[part]), axis=0)
        known = start[row : row + rows, :] - own_start[row : row + rows, :]
        known = known - outer_rows(operator, residual[place])
        outside[part, :] = known - alpha * values[part]
    alpha_column = column(alpha, width)
    parts = []
    edges = image_edges(even, inner, near, far, near_sent, far_sent, live_edge, live_own)
    for place, value in enumerate(edges):
        image[place] = value
        residual_new[place] = residual[place] - alpha_column * value
        parts.append(split(residual_new[place]))
    send_outer(parts, panel, near_out, far_out)


def update_kernel(inner, near, far, near_sent, far_sent, live_edge, live_own, sums, before,
                  old_edge, old_own, residual_edge, residual_own, panel,
                  outside_image_old, outside_old,
                  image_own, new_edge, new_own, near_out, far_out, scalars, outside):
    even = even_place()
    loads, width = residual_edge.shape
    rows = outside.shape[0] // 2
    image_old, residual = Joined(old_edge, old_own), Joined(residual_edge, residual_own)
    residual_new = Joined(new_edge, new_own)
    rz_now, alpha, beta = step_scalars(1, sums, before)
    scalars[...] = jnp.concatenate([rz_now, alpha], axis=0)
    values = received(even, near, far, loads, rows) + beta * outside_image_old[...]
    outside[...] = outside_old[...] - alpha * values
    alpha_column, beta_column = column(alpha, width), column(beta, width)
    parts = []
    edges = image_edges(even, inner, near, far, near_sent, far_sent, live_edge, live_own)
    for place, value in enumerate(edges):
        value = value + beta_column * image_old[place]
        if place > 0:
            image_own[place - 1] = value
        residual_new[place] = residual[place] - alpha_column * value
        parts.append(split(residual_new[place]))
    send_outer(parts, panel, near_out, far_out)


def last_kernel(inner, to_next, following, live, sums, before, older, image_old,
                residual, first_inner, first_last, second_inner, second_last, third_inner, third_last,
                multipliers, residual_new):
    subs, width = residual.shape[0], following.shape[1]
    rz_now, alpha, beta = step_scalars(2, sums, before)
    beta_before = before[0:1] / older[0:1]
    on_second = before[1:2] + alpha * beta
    on_first = older[1:2] + on_second * beta_before
    alpha_column, beta_column = column(alpha, width), column(beta, width)
    second_column, first_column = column(on_second, width), column(on_first, width)
    for sub in range(subs):
        if sub == subs - 1:
            image = live[sub] * (to_next[...] - following[...])
            first_z, second_z, third_z = first_last[...], second_last[...], third_last[...]
        else:
            image = inner[sub]
            first_z, second_z, third_z = first_inner[sub], second_inner[sub], third_inner[sub]
        image = image + beta_column * image_old[sub]
        residual_new[sub] = residual[sub] - alpha_column * image
        multipliers[sub] = (
            first_column * first_z + second_column * second_z + alpha_column * third_z
        )


def neighbour_pairs(size, first):
    pairs = [(i, i + 1) for i in range(first, size - 1, 2)]
    return [route for a, b in pairs for route in ((a, b), (b, a))]


def swap(near, far):
    size = lax.axis_size("sub")
    return (
        lax.ppermute(near, "sub", neighbour_pairs(size, 0)),
        lax.ppermute(far, "sub", neighbour_pairs(size, 1)),
    )


def from_all(rows):
    size = lax.axis_size("sub") * lax.axis_size("grp")
    copies = jnp.broadcast_to(rows[None], (size,) + rows.shape)
    return lax.all_to_all(copies, ("sub", "grp"), 0, 0)


def from_group(values):
    group = lax.axis_size("grp")
    received = [values]
    for distance in range(1, group):
        routes = [(i, i ^ distance) for i in range(group)]
        received.append(lax.ppermute(values, "grp", routes))
    return received


def swap_blocks(picked):
    group = lax.axis_size("grp")
    received = [picked[0]]
    for distance in range(1, group):
        routes = [(i, i ^ distance) for i in range(group)]
        received.append(lax.ppermute(picked[distance], "grp", routes))
    return received


def make_tail(counts, rhs):
    loads, width = rhs.shape[2:]
    return pl.pallas_call(
        tail_kernel,
        out_shape=jax.ShapeDtypeStruct((loads + 8, width), jnp.float32),
        in_specs=[
            pl.BlockSpec(memory_space=pltpu.HBM),
            pl.BlockSpec(memory_space=pltpu.HBM),
        ],
        out_specs=pl.BlockSpec(memory_space=pltpu.VMEM),
        scratch_shapes=[
            pltpu.VMEM(counts.shape, counts.dtype),
            pltpu.VMEM((loads, width), jnp.float32),
            pltpu.SemaphoreType.DMA,
            pltpu.SemaphoreType.DMA,
        ],
        compiler_params=pltpu.CompilerParams(vmem_limit_bytes=TAIL_LIMIT),
    )(counts, rhs)


def local(rhs, counts, solve_panel, dirichlet_panel, coupling, corner_map, coarse_inverse):
    subs, loads, width = rhs.shape[1:]
    corners = coupling.shape[2]
    solve, dirichlet = solve_panel[0], dirichlet_panel[0]
    size = lax.axis_size("sub")

    face_shape, own_shape = (loads, width), (subs, loads, width)
    scalars_shape, outside_shape, side_shape = (2, loads), (2 * corners, loads), (corners, width)
    long_shape, longer_shape = (loads + corners, width), (loads + 2 * corners, width)
    edges_shapes = [face_shape, own_shape]

    tail = make_tail(counts, rhs)
    tail, counts, corner_map = lax.optimization_barrier((tail, counts, corner_map))
    head = lax.ppermute(tail, "sub", [(i, i + 1) for i in range(size - 1)])
    maps = from_group(corner_map[0])
    live_own, residual_own, to_next, partial = call(
        early_kernel,
        [(subs, 1, width), own_shape, face_shape, face_shape],
        counts, rhs[0], dirichlet,
    )
    group, own = len(maps), subs * corners
    pair = [(corners, width)] * 2
    *picked, stacked, lift = call(
        setup_kernel,
        [(own, group * own)] * group
        + [(subs, 2 * corners, 2 * width), (subs, 3 * corners + -3 * corners % 128, 2 * width)],
        *maps, coarse_inverse[0], coupling[0],
        kinds=[jnp.float32] * group + [jnp.bfloat16] * 2,
        scratch=[pltpu.VMEM((group, 1, own), jnp.int32)],
    )
    head, stacked = lax.optimization_barrier((head, stacked))
    live_edge, residual_edge, near, far = call(
        head_kernel,
        [(1, width), face_shape, long_shape, long_shape],
        head, to_next, partial, dirichlet, coupling[0],
    )
    live, residual = (live_edge, live_own), (residual_edge, residual_own)
    sent = near, far
    near, far = swap(near, far)
    blocks = swap_blocks(picked)
    inner_shape, result_shape = (subs - 1, loads, width), (subs, loads, 2 * width)
    (first_inner,) = call(inner_edges_kernel, [inner_shape], *residual, dirichlet, live[1])
    result, partial = call(
        start_kernel, [result_shape, (own, loads)], first_inner, solve, stacked
    )
    taken, ends = call(
        operators_kernel,
        [(2 * own, (subs + 1) * width), (2,) + side_shape],
        coupling[0], *live, dirichlet,
        kinds=[jnp.bfloat16, jnp.float32],
    )
    (own_start,) = call(
        early_corner_kernel,
        [(own, loads)],
        taken, ends, jnp.zeros(outside_shape, jnp.float32), *residual,
    )
    partial, own_start = lax.optimization_barrier((partial, own_start))

    edge, first_last, values = call(
        corner_kernel,
        [face_shape, face_shape, (own, loads)],
        near, far, *sent, *live, stacked, partial,
    )
    everyone = lax.all_gather(values, "grp", tiled=True)
    everyone, blocks = lax.optimization_barrier((everyone, blocks))
    block = jnp.concatenate(split_outside(sum(blocks[1:], blocks[0])), axis=0)
    inner, near, far, result, for_next, for_prev = call(
        first_dual_kernel,
        [inner_shape, longer_shape, longer_shape, result_shape]
        + [(2 * corners, width), (2 * corners, width)],
        result, first_inner, edge, first_last, residual[1], solve, everyone, block, lift,
        near, far, *live, dirichlet,
        kinds=[jnp.float32] * 4 + [jnp.bfloat16] * 2,
    )
    (sums,) = call(
        sums_kernel, [scalars_shape], result, first_inner, edge, first_last, residual[1]
    )
    sums = from_all(sums)
    sent = near, far
    near, far = swap(near, far)
    image_own, image_edge, *residual, near, far, scalars_first, ends, outside_image, outside = call(
        first_update_kernel,
        [own_shape, face_shape] + edges_shapes
        + [face_shape, face_shape, scalars_shape, (2,) + side_shape, outside_shape, outside_shape],
        inner, near, far, *sent, *live, sums, *residual, dirichlet, ends, values, own_start,
    )

    def inside(residual, outside):
        (values,) = call(early_corner_kernel, [(own, loads)], taken, ends, outside, *residual)
        everyone = lax.all_gather(values, "grp", tiled=True)
        inner, result, partial = call(
            inside_kernel,
            [inner_shape, result_shape, (2,) + face_shape],
            *residual, dirichlet, live[1], solve, everyone, block, lift,
        )
        return result, inner, partial

    sent = near, far
    near, far = swap(near, far)
    result, second_inner, partial = inside(residual, outside)
    second_last, inner, near, far, sums = call(
        functools.partial(outer_dual_kernel, False),
        [face_shape, inner_shape, long_shape, long_shape, scalars_shape],
        result, second_inner, partial, near, far, *sent, *live, residual[1], solve,
        for_next, for_prev,
    )
    sums = from_all(sums)
    sent = near, far
    near, far = swap(near, far)
    image_own, *residual, near, far, scalars_second, outside = call(
        update_kernel,
        [own_shape] + edges_shapes + [face_shape, face_shape, scalars_shape, outside_shape],
        inner, near, far, *sent, *live, sums, scalars_first, image_edge, image_own, *residual,
        dirichlet, outside_image, outside,
    )

    sent = near, far
    near, far = swap(near, far)
    result, third_inner, partial = inside(residual, outside)
    third_last, inner, to_next, to_prev, sums = call(
        functools.partial(outer_dual_kernel, True),
        [face_shape, inner_shape, face_shape, face_shape, scalars_shape],
        result, third_inner, partial, near, far, *sent, *live, residual[1], solve,
    )
    sums = from_all(sums)
    following = lax.ppermute(to_prev, "sub", [(i + 1, i) for i in range(size - 1)])
    multipliers, residual = call(
        last_kernel,
        [own_shape] * 2,
        inner, to_next, following, live[1], sums, scalars_second, scalars_first,
        image_own, residual[1], first_inner, first_last, second_inner, second_last, third_inner, third_last,
    )
    return (multipliers[None], residual[None])


def solution(mesh):
    return jax.shard_map(
        local,
        mesh=mesh,
        in_specs=(
            P("grp", "sub", None, None),
            P("grp", "sub"),
            P("grp", "sub", None, None),
            P("grp", "sub", None, None),
            P("grp", "sub", None, None),
            P("grp", "sub", None),
            P("sub", "grp", None),
        ),
        out_specs=(P("grp", "sub", None, None), P("grp", "sub", None, None)),
        check_vma=False,
    )
```

```python
import functools

import jax
import jax.numpy as jnp
from jax import lax
from jax.experimental import pallas as pl
from jax.experimental.pallas import tpu as pltpu
from jax.sharding import PartitionSpec as P

VMEM_LIMIT = 8 * 1024 * 1024
TAIL_LIMIT = 62 * 1024 * 1024


def split(values):
    high = values.astype(jnp.bfloat16)
    return high, (values - high.astype(jnp.float32)).astype(jnp.bfloat16)


def split_outside(values):
    high = lax.reduce_precision(values, exponent_bits=8, mantissa_bits=7)
    return high.astype(jnp.bfloat16), (values - high).astype(jnp.bfloat16)


def mul(first, second):
    return jnp.dot(first, second, preferred_element_type=jnp.float32)


def mul_rows(first, second):
    dims = (((1,), (1,)), ((), ()))
    return lax.dot_general(first, second, dims, preferred_element_type=jnp.float32)


def call(kernel, out_shapes, *operands, kinds=None, scratch=()):
    kinds = kinds or [jnp.float32] * len(out_shapes)
    return pl.pallas_call(
        kernel,
        out_shape=[jax.ShapeDtypeStruct(*shape) for shape in zip(out_shapes, kinds)],
        in_specs=[pl.BlockSpec(memory_space=pltpu.VMEM)] * len(operands),
        out_specs=[pl.BlockSpec(memory_space=pltpu.VMEM)] * len(out_shapes),
        scratch_shapes=list(scratch),
        compiler_params=pltpu.CompilerParams(vmem_limit_bytes=VMEM_LIMIT),
    )(*operands)


class Joined:
    def __init__(self, first, rest):
        self.first, self.rest = first, rest

    def __getitem__(self, place):
        return self.first[...] if place == 0 else self.rest[place - 1]

    def __setitem__(self, place, value):
        if place == 0:
            self.first[...] = value
        else:
            self.rest[place - 1] = value


def outer_rows(operator, edge):
    rows = operator.shape[0] // 2
    high, low = split(edge)
    both = mul_rows(operator[...], high)
    return both[:rows] + both[rows:] + mul_rows(operator[:rows], low)


def send(even, to_next, to_prev, near_out, far_out):
    row = 0
    for ahead, behind in zip(to_next, to_prev):
        rows = slice(row, row + ahead.shape[0])
        near_out[rows, :] = jnp.where(even, ahead, behind)
        far_out[rows, :] = jnp.where(even, behind, ahead)
        row += ahead.shape[0]


def column(row, width):
    lanes = jnp.broadcast_to(row, (128, row.shape[1])).T
    return jnp.concatenate([lanes] * (width // 128), axis=1)


def row_sums(values):
    half = values.shape[1] // 2
    return jnp.sum((values[:, :half] + values[:, half:]).T, axis=0, keepdims=True)


def step_scalars(step, sums, before):
    totals = jnp.sum(sums[...], axis=0)
    rz_now, curvature = totals[:1], totals[1:2]
    if step == 0:
        return rz_now, rz_now / curvature, None
    beta = rz_now / before[0:1]
    return rz_now, rz_now / (curvature - beta * rz_now / before[1:2]), beta


def even_place():
    return lax.rem(lax.axis_index("sub"), 2) == 0


def live_rows(counts, sub, rows, width):
    last = lax.axis_index("sub") == lax.axis_size("sub") - 1
    count = jnp.broadcast_to(counts[:, sub : sub + 1], (rows, width))
    if sub == counts.shape[1] - 1:
        count = jnp.where(last, 0, count)
    return (lax.broadcasted_iota(jnp.int32, (rows, width), 1) < count).astype(jnp.float32)


def tail_kernel(counts_ref, rhs, tail, counts, face, counts_done, face_done):
    loads, width = rhs.shape[2:]
    counts_copy = pltpu.make_async_copy(counts_ref, counts, counts_done)
    face_copy = pltpu.make_async_copy(rhs.at[0, rhs.shape[1] - 1], face, face_done)
    counts_copy.start()
    face_copy.start()
    counts_copy.wait()
    mask = live_rows(counts, counts.shape[1] - 1, 8, width)
    tail[loads:] = mask
    face_copy.wait()
    tail[:loads] = mask[:1] * face[...]


def early_kernel(counts, rhs, last_panel, first_panel, live, own, to_next, partial):
    subs, loads, width = own.shape
    parts = []
    for sub in range(subs):
        mask = live_rows(counts, sub, 1, width)
        live[sub] = mask
        own[sub] = mask * rhs[sub]
        parts.append(split(own[sub]))
    high = jnp.concatenate([-parts[subs - 2][0], parts[subs - 1][0]], axis=1)
    low = jnp.concatenate([-parts[subs - 2][1], parts[subs - 1][1]], axis=1)
    to_next[...] = mul(high, last_panel[...]) + mul(low, last_panel[...])
    high, low = parts[0]
    partial[...] = mul(high, first_panel[width:]) + mul(low, first_panel[width:])


def head_kernel(head, to_next, partial, first_panel, coupling, live, edge, near_out, far_out):
    loads, width = edge.shape
    live[...] = head[loads : loads + 1]
    edge[...] = head[:loads]
    high, low = split(head[:loads])
    to_prev = partial[...] - (
        mul(high, first_panel[:width]) + mul(low, first_panel[:width])
    )
    ahead = [to_next[...], coupling[coupling.shape[0] - 1, :, width:]]
    send(even_place(), ahead, [to_prev, coupling[0, :, :width]], near_out, far_out)


def setup_kernel(*refs):
    group = (len(refs) - 5) // 2
    maps, (coarse, coupling) = refs[:group], refs[group : group + 2]
    picked, (stacked, lift, everyone) = refs[group + 2 : -3], refs[-3:]
    subs, corners = maps[0].shape
    rows, size = coarse.shape
    own = subs * corners
    grp = lax.axis_index("grp")
    for sub in range(subs):
        high, low = split(coupling[sub])
        spare = jnp.zeros((lift.shape[1] - 3 * corners, high.shape[1]), jnp.bfloat16)
        stacked[sub] = jnp.concatenate([high, low], axis=0)
        lift[sub] = jnp.concatenate([high, high, low, spare], axis=0)
    for distance in range(group):
        unknowns = [maps[distance][sub : sub + 1, :] for sub in range(subs)]
        everyone[distance] = jnp.concatenate(unknowns, axis=1)
    high, low = split(coarse[...])
    together = max(1, 512 // own)
    columns = []
    for start in range(0, group, together):
        members = range(start, min(start + together, group))
        wanted = jnp.concatenate([everyone[grp ^ member] for member in members], axis=1)
        unknowns = lax.broadcasted_iota(jnp.int32, (size, wanted.shape[1]), 0)
        chosen = (unknowns == wanted).astype(jnp.bfloat16)
        columns.append(mul(high, chosen) + mul(low, chosen))
    high, low = split(jnp.concatenate(columns, axis=1))
    dims = (((0,), (0,)), ((), ()))
    for start in range(0, group, together):
        distances = range(start, min(start + together, group))
        wanted = jnp.concatenate([everyone[distance] for distance in distances], axis=1)
        owned = lax.broadcasted_iota(jnp.int32, (rows, wanted.shape[1]), 0) + grp * rows
        chosen = (owned == wanted).astype(jnp.bfloat16)
        values = lax.dot_general(
            chosen, high, dims, preferred_element_type=jnp.float32
        ) + lax.dot_general(chosen, low, dims, preferred_element_type=jnp.float32)
        for place, distance in enumerate(distances):
            picked[distance][...] = values[place * own : (place + 1) * own]


def start_kernel(inner, panel, coupling, result, corners):
    subs, rows = coupling.shape[0], coupling.shape[1] // 2
    width = inner.shape[2]
    parts = [split(inner[place]) for place in range(subs - 1)]
    high, low = parts[0]
    result[0] = mul(high, panel[0, width:]) + mul(low, panel[0, width:])
    for sub in range(1, subs - 1):
        high = jnp.concatenate([-parts[sub - 1][0], parts[sub][0]], axis=1)
        low = jnp.concatenate([-parts[sub - 1][1], parts[sub][1]], axis=1)
        result[sub] = mul(high, panel[sub]) + mul(low, panel[sub])
    high, low = parts[subs - 2]
    result[subs - 1] = -(mul(high, panel[subs - 1, :width]) + mul(low, panel[subs - 1, :width]))
    for sub in range(subs):
        values = jnp.zeros((rows, inner.shape[1]), jnp.float32)
        if sub > 0:
            values = values - outer_rows(coupling[sub, :, :width], inner[sub - 1])
        if sub + 1 < subs:
            values = values + outer_rows(coupling[sub, :, width:], inner[sub])
        corners[sub * rows : (sub + 1) * rows, :] = values


def corner_kernel(near, far, near_sent, far_sent, live_edge, live_own, coupling, partial,
                  edge, last, corners):
    subs, rows = coupling.shape[0], coupling.shape[1] // 2
    loads, width = edge.shape
    first_value, last_value = cut_edges(even_place(), loads, near, far, near_sent, far_sent,
                                        0.25 * live_edge[...], 0.25 * live_own[subs - 1])
    edge[...] = first_value
    last[...] = last_value
    corners[...] = partial[...]
    corners[:rows, :] = partial[:rows, :] - outer_rows(coupling[0, :, :width], first_value)
    corners[-rows:, :] = partial[-rows:, :] + outer_rows(
        coupling[subs - 1, :, width:], last_value
    )


def operators_kernel(coupling, live_edge, live_own, panel, taken, ends):
    subs, rows = coupling.shape[0], coupling.shape[1]
    width = coupling.shape[2] // 2
    live = Joined(live_edge, live_own)
    left = [coupling[sub, :, :width] * (0.25 * live[sub]) for sub in range(subs)]
    right = [coupling[sub, :, width:] * (0.25 * live[sub + 1]) for sub in range(subs)]
    none = jnp.zeros((rows, width), jnp.float32)
    inner, ahead, behind = [], [], []
    for sub in range(subs):
        above = left[sub + 1] if sub + 1 < subs else none
        below = right[sub - 1] if sub > 0 else none
        factors = jnp.concatenate(
            [
                jnp.concatenate([left[sub], right[sub]], axis=1),
                jnp.concatenate([none, above], axis=1),
                jnp.concatenate([below, none], axis=1),
            ],
            axis=0,
        )
        both = mul(jnp.concatenate(split(factors), axis=0), panel[sub])
        product = both[: 3 * rows] + both[3 * rows :]
        inner.append(product[:rows])
        ahead.append(product[rows : 2 * rows])
        behind.append(product[2 * rows :])
    total = subs * rows
    for sub in range(subs):
        blocks = [none] * (subs + 1)
        blocks[sub] = -inner[sub][:, :width]
        blocks[sub + 1] = inner[sub][:, width:]
        if sub > 0:
            blocks[sub - 1] = ahead[sub - 1][:, :width]
            blocks[sub] = blocks[sub] - ahead[sub - 1][:, width:]
        if sub + 1 < subs:
            blocks[sub + 1] = blocks[sub + 1] + behind[sub + 1][:, :width]
            blocks[sub + 2] = -behind[sub + 1][:, width:]
        if sub == 0:
            ends[0] = blocks[0]
            blocks[0] = none
        if sub == subs - 1:
            ends[1] = blocks[subs]
            blocks[subs] = none
        high, low = split(jnp.concatenate(blocks, axis=1))
        taken[sub * rows : (sub + 1) * rows, :] = high
        taken[total + sub * rows : total + (sub + 1) * rows, :] = low


def early_corner_kernel(taken, ends, outside, edge, own, corners):
    subs, rows = own.shape[0], ends.shape[1]
    total = subs * rows
    edges = Joined(edge, own)
    parts = [split(edges[place]) for place in range(subs + 1)]
    high = jnp.concatenate([part[0] for part in parts], axis=1)
    low = jnp.concatenate([part[1] for part in parts], axis=1)
    both = mul_rows(taken[...], high)
    values = both[:total] + both[total:] + mul_rows(taken[:total], low)
    corners[...] = values
    for end, place in ((0, 0), (1, subs)):
        operator = jnp.concatenate(split(ends[end]), axis=0)
        row = end * (total - rows)
        corners[row : row + rows, :] = (
            values[row : row + rows]
            + outer_rows(operator, edges[place])
            + outside[end * rows : (end + 1) * rows, :]
        )


def coarse_lift(everyone, block, lift):
    subs = lift.shape[0]
    rows = block.shape[0] // 2
    high, low = split(everyone[...])
    both = mul(block[...], high)
    back = both[:rows] + both[rows:] + mul(block[:rows], low)
    corners = rows // subs

    def lifted(sub):
        own = back[sub * corners : (sub + 1) * corners]
        own_high = own.astype(jnp.bfloat16).astype(jnp.float32)
        terms = [own_high, own - own_high, own_high]
        spare = jnp.zeros((lift.shape[1] - 3 * corners, own.shape[1]), jnp.float32)
        return mul(jnp.concatenate(terms + [spare], axis=0).T.astype(jnp.bfloat16), lift[sub])

    return lifted


def on_subdomain(values, left, right):
    width = left.shape[1]
    return values[:, width:] * right - values[:, :width] * left


def send_dual(even, inner, faces, for_next, for_prev, near_out, far_out, given=None):
    to_next, to_prev = [faces[0]], [faces[1]]
    count = inner.shape[0]
    if given is not None:
        to_next.append(given[0])
        to_prev.append(given[1])
    to_next.append(outer_rows(for_next, inner[count - 1]))
    to_prev.append(outer_rows(for_prev, inner[0]))
    send(even, to_next, to_prev, near_out, far_out)


def inner_jump(result, live_own, inner):
    width = inner.shape[2]
    for place in range(inner.shape[0]):
        inner[place] = live_own[place] * (result[place][:, width:] - result[place + 1][:, :width])


def first_dual_kernel(before, inner_z, edge, last_z, residual, panel, everyone, block, lift,
                      near, far, live_edge, live_own, preconditioner,
                      inner, near_out, far_out, result, for_next, for_prev):
    even = even_place()
    subs, (loads, width) = panel.shape[0], edge.shape
    rows = for_next.shape[0] // 2
    sides = received(even, near, far, loads, rows)
    after = sides[rows:] * (0.25 * live_own[subs - 1])
    behind = sides[:rows] * (0.25 * live_edge[...])
    both = mul(jnp.concatenate(split(after), axis=0), preconditioner[subs - 1, width:])
    after = both[:rows] + both[rows:]
    both = mul(jnp.concatenate(split(behind), axis=0), preconditioner[0, :width])
    behind = both[:rows] + both[rows:]
    for_next[...] = jnp.concatenate(split(after[:, :width]), axis=0)
    for_prev[...] = jnp.concatenate(split(-behind[:, width:]), axis=0)
    given = [-after[:, width:], behind[:, :width]]

    lifted = coarse_lift(everyone, block, lift)
    for sub in range(subs):
        value = before[sub] + lifted(sub)
        if sub == 0:
            high, low = split(edge[...])
            value = value - (mul(high, panel[0, :width]) + mul(low, panel[0, :width]))
        if sub == subs - 1:
            high, low = split(last_z[...])
            value = value + (mul(high, panel[sub, width:]) + mul(low, panel[sub, width:]))
        result[sub] = value
    inner_jump(result, live_own, inner)
    faces = [result[subs - 1][:, width:], result[0][:, :width]]
    send_dual(even, inner, faces, for_next, for_prev, near_out, far_out, given)


def sums_kernel(result, inner_z, edge, last_z, residual, sums):
    subs = residual.shape[0]
    edges = [edge[...]] + [inner_z[place] for place in range(subs - 1)] + [last_z[...]]
    product = curvature = 0.0
    for sub in range(subs):
        product = product + residual[sub] * edges[sub + 1]
        curvature = curvature + on_subdomain(result[sub], edges[sub], edges[sub + 1])
    sums[...] = jnp.concatenate([row_sums(product), row_sums(curvature)], axis=0)


def inner_edges_kernel(edge, own, panel, live_own, inner):
    subs, width = panel.shape[0], edge.shape[1]
    edges = Joined(edge, own)
    parts = [split(edges[place]) for place in range(subs + 1)]

    def half(sub, columns):
        high = jnp.concatenate([-parts[sub][0], parts[sub + 1][0]], axis=1)
        low = jnp.concatenate([-parts[sub][1], parts[sub + 1][1]], axis=1)
        return mul(high, panel[sub, :, columns]) + mul(low, panel[sub, :, columns])

    for place in range(subs - 1):
        right = half(place, slice(width, 2 * width))
        left = half(place + 1, slice(0, width))
        inner[place] = (0.25 * live_own[place]) * (right - left)


def inner_dual_kernel(inner, residual, panel, everyone, block, lift, result, partial):
    subs, width = panel.shape[0], inner.shape[2]
    lifted = coarse_lift(everyone, block, lift)
    parts = [split(inner[place]) for place in range(subs - 1)]
    high, low = parts[0]
    result[0] = mul(high, panel[0, width:]) + mul(low, panel[0, width:]) + lifted(0)
    product = residual[0] * inner[0]
    curvature = jnp.zeros_like(product)
    for sub in range(1, subs - 1):
        high = jnp.concatenate([-parts[sub - 1][0], parts[sub][0]], axis=1)
        low = jnp.concatenate([-parts[sub - 1][1], parts[sub][1]], axis=1)
        result[sub] = mul(high, panel[sub]) + mul(low, panel[sub]) + lifted(sub)
        product = product + residual[sub] * inner[sub]
        curvature = curvature + on_subdomain(result[sub], inner[sub - 1], inner[sub])
    high, low = parts[subs - 2]
    result[subs - 1] = lifted(subs - 1) - (
        mul(high, panel[subs - 1, :width]) + mul(low, panel[subs - 1, :width])
    )
    partial[0] = product
    partial[1] = curvature


def inside_kernel(edge, own, preconditioner, live_own, panel, everyone, block, lift,
                  inner, result, partial):
    inner_edges_kernel(edge, own, preconditioner, live_own, inner)
    inner_dual_kernel(inner, own, panel, everyone, block, lift, result, partial)


def cut_edges(even, loads, near, far, near_sent, far_sent, live_first, live_last):
    near, far, near_sent, far_sent = near[:loads], far[:loads], near_sent[:loads], far_sent[:loads]
    first = live_first * jnp.where(even, far - far_sent, near - near_sent)
    last = live_last * jnp.where(even, near_sent - near, far_sent - far)
    return first, last


def outer_dual_kernel(closing, *refs):
    before, inner_z, partial, near, far, near_sent, far_sent, live_edge, live_own = refs[:9]
    residual, panel = refs[9:11]
    even, subs, width = even_place(), panel.shape[0], near_sent.shape[1]
    edge, last = cut_edges(even, residual.shape[1], near, far, near_sent, far_sent,
                           0.25 * live_edge[...], 0.25 * live_own[subs - 1])
    if closing:
        last_z, inner, to_next, to_prev, sums = refs[11:]
    else:
        for_next, for_prev, last_z, inner, near_out, far_out, sums = refs[11:]
    last_z[...] = last
    high, low = split(edge)
    result_first = before[0] - (mul(high, panel[0, :width]) + mul(low, panel[0, :width]))
    high, low = split(last)
    result_last = before[subs - 1] + (
        mul(high, panel[subs - 1, width:]) + mul(low, panel[subs - 1, width:])
    )
    result = [result_first] + [before[sub] for sub in range(1, subs - 1)] + [result_last]
    inner_jump(result, live_own, inner)
    faces = [result_last[:, width:], result_first[:, :width]]
    if closing:
        to_next[...], to_prev[...] = faces
    else:
        send_dual(even, inner, faces, for_next, for_prev, near_out, far_out)
    product = partial[0] + residual[subs - 1] * last
    curvature = partial[1] + on_subdomain(result_first, edge, inner_z[0])
    curvature = curvature + on_subdomain(result_last, inner_z[subs - 2], last)
    sums[...] = jnp.concatenate([row_sums(product), row_sums(curvature)], axis=0)


def received(even, near, far, start, rows):
    part = slice(start, start + rows)
    return jnp.concatenate(
        [jnp.where(even, far[part], near[part]), jnp.where(even, near[part], far[part])], axis=0
    )


def send_outer(parts, panel, near_out, far_out):
    subs, width = panel.shape[0], near_out.shape[1]

    def half(sub, columns):
        high = jnp.concatenate([-parts[sub][0], parts[sub + 1][0]], axis=1)
        low = jnp.concatenate([-parts[sub][1], parts[sub + 1][1]], axis=1)
        return mul(high, panel[sub, :, columns]) + mul(low, panel[sub, :, columns])

    to_next = half(subs - 1, slice(width, 2 * width))
    send(even_place(), [to_next], [half(0, slice(0, width))], near_out, far_out)


def image_edges(even, inner, near, far, near_sent, far_sent, live_edge, live_own):
    subs = live_own.shape[0]
    edge, last = cut_edges(even, inner.shape[1], near, far, near_sent, far_sent, live_edge[...],
                           live_own[subs - 1])
    return [edge] + [inner[place] for place in range(subs - 1)] + [last]


def first_update_kernel(inner, near, far, near_sent, far_sent, live_edge, live_own, sums,
                        residual_edge, residual_own, panel, ends, start, own_start,
                        image_own, image_edge, new_edge, new_own,
                        near_out, far_out, scalars, full_ends, outside_image, outside):
    even = even_place()
    loads, width = residual_edge.shape
    subs, rows = panel.shape[0], ends.shape[1]
    residual, image = Joined(residual_edge, residual_own), Joined(image_edge, image_own)
    residual_new = Joined(new_edge, new_own)
    rz_now, alpha, _ = step_scalars(0, sums, None)
    scalars[...] = jnp.concatenate([rz_now, alpha], axis=0)
    operators = received(even, near, far, loads, rows)
    full_ends[0] = ends[0] + operators[:rows]
    full_ends[1] = ends[1] + operators[rows:]
    values = received(even, near, far, loads + rows, rows)
    outside_image[...] = values
    for end, place in ((0, 0), (1, subs)):
        part, row = slice(end * rows, (end + 1) * rows), end * (start.shape[0] - rows)
        operator = jnp.concatenate(split(operators[part]), axis=0)
        known = start[row : row + rows, :] - own_start[row : row + rows, :]
        known = known - outer_rows(operator, residual[place])
        outside[part, :] = known - alpha * values[part]
    alpha_column = column(alpha, width)
    parts = []
    edges = image_edges(even, inner, near, far, near_sent, far_sent, live_edge, live_own)
    for place, value in enumerate(edges):
        image[place] = value
        residual_new[place] = residual[place] - alpha_column * value
        parts.append(split(residual_new[place]))
    send_outer(parts, panel, near_out, far_out)


def update_kernel(inner, near, far, near_sent, far_sent, live_edge, live_own, sums, before,
                  old_edge, old_own, residual_edge, residual_own, panel,
                  outside_image_old, outside_old,
                  image_own, new_edge, new_own, near_out, far_out, scalars, outside):
    even = even_place()
    loads, width = residual_edge.shape
    rows = outside.shape[0] // 2
    image_old, residual = Joined(old_edge, old_own), Joined(residual_edge, residual_own)
    residual_new = Joined(new_edge, new_own)
    rz_now, alpha, beta = step_scalars(1, sums, before)
    scalars[...] = jnp.concatenate([rz_now, alpha], axis=0)
    values = received(even, near, far, loads, rows) + beta * outside_image_old[...]
    outside[...] = outside_old[...] - alpha * values
    alpha_column, beta_column = column(alpha, width), column(beta, width)
    parts = []
    edges = image_edges(even, inner, near, far, near_sent, far_sent, live_edge, live_own)
    for place, value in enumerate(edges):
        value = value + beta_column * image_old[place]
        if place > 0:
            image_own[place - 1] = value
        residual_new[place] = residual[place] - alpha_column * value
        parts.append(split(residual_new[place]))
    send_outer(parts, panel, near_out, far_out)


def last_kernel(inner, to_next, following, live, sums, before, older, image_old,
                residual, first_inner, first_last, second_inner, second_last, third_inner, third_last,
                multipliers, residual_new):
    subs, width = residual.shape[0], following.shape[1]
    rz_now, alpha, beta = step_scalars(2, sums, before)
    beta_before = before[0:1] / older[0:1]
    on_second = before[1:2] + alpha * beta
    on_first = older[1:2] + on_second * beta_before
    alpha_column, beta_column = column(alpha, width), column(beta, width)
    second_column, first_column = column(on_second, width), column(on_first, width)
    for sub in range(subs):
        if sub == subs - 1:
            image = live[sub] * (to_next[...] - following[...])
            first_z, second_z, third_z = first_last[...], second_last[...], third_last[...]
        else:
            image = inner[sub]
            first_z, second_z, third_z = first_inner[sub], second_inner[sub], third_inner[sub]
        image = image + beta_column * image_old[sub]
        residual_new[sub] = residual[sub] - alpha_column * image
        multipliers[sub] = (
            first_column * first_z + second_column * second_z + alpha_column * third_z
        )


def neighbour_pairs(size, first):
    pairs = [(i, i + 1) for i in range(first, size - 1, 2)]
    return [route for a, b in pairs for route in ((a, b), (b, a))]


def swap(near, far):
    size = lax.axis_size("sub")
    return (
        lax.ppermute(near, "sub", neighbour_pairs(size, 0)),
        lax.ppermute(far, "sub", neighbour_pairs(size, 1)),
    )


def from_all(rows):
    size = lax.axis_size("sub") * lax.axis_size("grp")
    copies = jnp.broadcast_to(rows[None], (size,) + rows.shape)
    return lax.all_to_all(copies, ("sub", "grp"), 0, 0)


def from_group(values):
    group = lax.axis_size("grp")
    received = [values]
    for distance in range(1, group):
        routes = [(i, i ^ distance) for i in range(group)]
        received.append(lax.ppermute(values, "grp", routes))
    return received


def swap_blocks(picked):
    group = lax.axis_size("grp")
    received = [picked[0]]
    for distance in range(1, group):
        routes = [(i, i ^ distance) for i in range(group)]
        received.append(lax.ppermute(picked[distance], "grp", routes))
    return received


def make_tail(counts, rhs):
    loads, width = rhs.shape[2:]
    return pl.pallas_call(
        tail_kernel,
        out_shape=jax.ShapeDtypeStruct((loads + 8, width), jnp.float32),
        in_specs=[
            pl.BlockSpec(memory_space=pltpu.HBM),
            pl.BlockSpec(memory_space=pltpu.HBM),
        ],
        out_specs=pl.BlockSpec(memory_space=pltpu.VMEM),
        scratch_shapes=[
            pltpu.VMEM(counts.shape, counts.dtype),
            pltpu.VMEM((loads, width), jnp.float32),
            pltpu.SemaphoreType.DMA,
            pltpu.SemaphoreType.DMA,
        ],
        compiler_params=pltpu.CompilerParams(vmem_limit_bytes=TAIL_LIMIT),
    )(counts, rhs)


def local(rhs, counts, solve_panel, dirichlet_panel, coupling, corner_map, coarse_inverse):
    subs, loads, width = rhs.shape[1:]
    corners = coupling.shape[2]
    solve, dirichlet = solve_panel[0], dirichlet_panel[0]
    size = lax.axis_size("sub")

    face_shape, own_shape = (loads, width), (subs, loads, width)
    scalars_shape, outside_shape, side_shape = (2, loads), (2 * corners, loads), (corners, width)
    long_shape, longer_shape = (loads + corners, width), (loads + 2 * corners, width)
    edges_shapes = [face_shape, own_shape]

    tail = make_tail(counts, rhs)
    tail, counts, corner_map = lax.optimization_barrier((tail, counts, corner_map))
    head = lax.ppermute(tail, "sub", [(i, i + 1) for i in range(size - 1)])
    maps = from_group(corner_map[0])
    live_own, residual_own, to_next, partial = call(
        early_kernel,
        [(subs, 1, width), own_shape, face_shape, face_shape],
        counts, rhs[0], dirichlet[subs - 1, :, width:], dirichlet[0, :, :width],
    )
    group, own = len(maps), subs * corners
    pair = [(corners, width)] * 2
    *picked, stacked, lift = call(
        setup_kernel,
        [(own, group * own)] * group
        + [(subs, 2 * corners, 2 * width), (subs, 3 * corners + -3 * corners % 128, 2 * width)],
        *maps, coarse_inverse[0], coupling[0],
        kinds=[jnp.float32] * group + [jnp.bfloat16] * 2,
        scratch=[pltpu.VMEM((group, 1, own), jnp.int32)],
    )
    head, stacked = lax.optimization_barrier((head, stacked))
    live_edge, residual_edge, near, far = call(
        head_kernel,
        [(1, width), face_shape, long_shape, long_shape],
        head, to_next, partial, dirichlet[0, :, :width], coupling[0],
    )
    live, residual = (live_edge, live_own), (residual_edge, residual_own)
    sent = near, far
    near, far = swap(near, far)
    blocks = swap_blocks(picked)
    inner_shape, result_shape = (subs - 1, loads, width), (subs, loads, 2 * width)
    (first_inner,) = call(inner_edges_kernel, [inner_shape], *residual, dirichlet, live[1])
    result, partial = call(
        start_kernel, [result_shape, (own, loads)], first_inner, solve, stacked
    )
    taken, ends = call(
        operators_kernel,
        [(2 * own, (subs + 1) * width), (2,) + side_shape],
        coupling[0], *live, dirichlet,
        kinds=[jnp.bfloat16, jnp.float32],
    )
    (own_start,) = call(
        early_corner_kernel,
        [(own, loads)],
        taken, ends, jnp.zeros(outside_shape, jnp.float32), *residual,
    )
    partial, own_start = lax.optimization_barrier((partial, own_start))

    edge, first_last, values = call(
        corner_kernel,
        [face_shape, face_shape, (own, loads)],
        near, far, *sent, *live, stacked, partial,
    )
    everyone = lax.all_gather(values, "grp", tiled=True)
    everyone, blocks = lax.optimization_barrier((everyone, blocks))
    block = jnp.concatenate(split_outside(sum(blocks[1:], blocks[0])), axis=0)
    inner, near, far, result, for_next, for_prev = call(
        first_dual_kernel,
        [inner_shape, longer_shape, longer_shape, result_shape]
        + [(2 * corners, width), (2 * corners, width)],
        result, first_inner, edge, first_last, residual[1], solve, everyone, block, lift,
        near, far, *live, dirichlet,
        kinds=[jnp.float32] * 4 + [jnp.bfloat16] * 2,
    )
    (sums,) = call(
        sums_kernel, [scalars_shape], result, first_inner, edge, first_last, residual[1]
    )
    sums = from_all(sums)
    sent = near, far
    near, far = swap(near, far)
    image_own, image_edge, *residual, near, far, scalars_first, ends, outside_image, outside = call(
        first_update_kernel,
        [own_shape, face_shape] + edges_shapes
        + [face_shape, face_shape, scalars_shape, (2,) + side_shape, outside_shape, outside_shape],
        inner, near, far, *sent, *live, sums, *residual, dirichlet, ends, values, own_start,
    )

    def inside(residual, outside):
        (values,) = call(early_corner_kernel, [(own, loads)], taken, ends, outside, *residual)
        everyone = lax.all_gather(values, "grp", tiled=True)
        inner, result, partial = call(
            inside_kernel,
            [inner_shape, result_shape, (2,) + face_shape],
            *residual, dirichlet, live[1], solve, everyone, block, lift,
        )
        return result, inner, partial

    sent = near, far
    near, far = swap(near, far)
    result, second_inner, partial = inside(residual, outside)
    second_last, inner, near, far, sums = call(
        functools.partial(outer_dual_kernel, False),
        [face_shape, inner_shape, long_shape, long_shape, scalars_shape],
        result, second_inner, partial, near, far, *sent, *live, residual[1], solve,
        for_next, for_prev,
    )
    sums = from_all(sums)
    sent = near, far
    near, far = swap(near, far)
    image_own, *residual, near, far, scalars_second, outside = call(
        update_kernel,
        [own_shape] + edges_shapes + [face_shape, face_shape, scalars_shape, outside_shape],
        inner, near, far, *sent, *live, sums, scalars_first, image_edge, image_own, *residual,
        dirichlet, outside_image, outside,
    )

    sent = near, far
    near, far = swap(near, far)
    result, third_inner, partial = inside(residual, outside)
    third_last, inner, to_next, to_prev, sums = call(
        functools.partial(outer_dual_kernel, True),
        [face_shape, inner_shape, face_shape, face_shape, scalars_shape],
        result, third_inner, partial, near, far, *sent, *live, residual[1], solve,
    )
    sums = from_all(sums)
    following = lax.ppermute(to_prev, "sub", [(i + 1, i) for i in range(size - 1)])
    multipliers, residual = call(
        last_kernel,
        [own_shape] * 2,
        inner, to_next, following, live[1], sums, scalars_second, scalars_first,
        image_own, residual[1], first_inner, first_last, second_inner, second_last, third_inner, third_last,
    )
    return (multipliers[None], residual[None])


def solution(mesh):
    return jax.shard_map(
        local,
        mesh=mesh,
        in_specs=(
            P("grp", "sub", None, None),
            P("grp", "sub"),
            P("grp", "sub", None, None),
            P("grp", "sub", None, None),
            P("grp", "sub", None, None),
            P("grp", "sub", None),
            P("sub", "grp", None),
        ),
        out_specs=(P("grp", "sub", None, None), P("grp", "sub", None, None)),
        check_vma=False,
    )
```
